512 devices in a mesh: grp: 4 (over x), seq: 16 (over z, y_lo), dp: 8 (over y_hi, core).
Axes of the slice: x: 4, y: 8 (y_hi: 4, y_lo: 2; y = y_hi * 2 + y_lo), z: 8, core: 2. Of those that a mesh axis runs over, the one named last changes fastest.
Arguments:
- video: bfloat16 [8, 128, 256, 512], P('dp', 'seq', 'grp'), may hold values from -7 to 7
- conv_weight: bfloat16 [3, 128, 128], replicated, may hold values from -0.3125 to 0.3125
- latent_weight: bfloat16 [512, 64], replicated, may hold values from -0.25 to 0.25
- assign: int32 [8, 128, 256], P('dp', 'seq', 'grp'), may hold values from 0 to 1023, as said below
- embed_weight: bfloat16 [64, 3072], replicated, may hold values from -0.75 to 0.75
- norm_gain: float32 [3072], replicated, may hold values from 0.1 to 1.9
- qkv_weight: bfloat16 [3, 3072, 2048], P(None, None, 'seq'), may hold values from -6 to 6
- q_gain: float32 [128], replicated, may hold values from 0.5 to 5
- k_gain: float32 [128], replicated, may hold values from 0.5 to 5
- out_weight: bfloat16 [2048, 3072], P('seq'), may hold values from -2.390625 to 2.390625
- cotangent: bfloat16 [8, 1024, 3072], P('dp', ('grp', 'seq')), may hold values from -6 to 6
Outputs:
- attended: bfloat16 [8, 1024, 3072], P('dp', ('grp', 'seq'))
- out_grad: bfloat16 [2048, 3072], P('seq')
The draws below stay inside these ranges and needn't reach their ends.
Inputs may be any that keep to these rules, and one draw needn't show every extreme that they name: `assign`: every one of the 1024 merged groups of a clip receives at least one token.
All inputs are finite; a program needn't handle non-finite values.
Results may differ from the reference program's by a relative error of at most 0.04.
The reference program's roundings to bfloat16 on the way count: a program that leaves them out, or rounds other values in their place, can miss the bound.
Values may be sent and summed in bfloat16 or wider, within the bound.
No kernel may reach another device: no remote copies, remote signals or barrier semaphores. Data moves between devices by JAX's collectives and lax.ppermute only.
A program may use at most 64 MiB of HBM per device.

```python
import math
import jax
import jax.numpy as jnp
from jax import lax

D = 3072
HEADS = 16
HEAD = 128
CH = 128
LAT = 64
FR_DEV = 8
TPF = 64
M_DEV = 16
FRAMES = 128
PIX = 256
GROUPS = 1024
CLIPS = 8


def draw_video(key, part):
    key = jax.random.fold_in(key, 41)
    region_key, noise_key = jax.random.split(key)
    slab_count = FRAMES // FR_DEV
    column_count = PIX // TPF
    offsets = jnp.clip(jax.random.normal(region_key, (CLIPS, slab_count, 1, column_count, 1, 4 * CH), jnp.float32), -2.0, 2.0) * 1.5
    noise = jnp.clip(jax.random.normal(noise_key, (CLIPS, slab_count, FR_DEV, column_count, TPF, 4 * CH), jnp.float32), -4.0, 4.0)
    return (noise + offsets).reshape(CLIPS, FRAMES, PIX, 4 * CH).astype(jnp.bfloat16)


def draw_assign(key, part):
    key = jax.random.fold_in(key, 11)
    token_total = FRAMES * PIX
    slab_count = FRAMES // FR_DEV
    column_count = PIX // TPF
    owner_total = slab_count * column_count
    frame_index = jnp.arange(token_total, dtype=jnp.int32) // PIX
    pixel_index = jnp.arange(token_total, dtype=jnp.int32) % PIX
    source = pixel_index // TPF * slab_count + frame_index // FR_DEV
    owner = (source + owner_total // 2) % owner_total

    def one_clip(clip_key):
        first_key, second_key, third_key, fourth_key = jax.random.split(clip_key, 4)
        spread_labels = jax.random.randint(first_key, (token_total,), 0, GROUPS, dtype=jnp.int32)
        local_labels = owner * M_DEV + jax.random.randint(third_key, (token_total,), 0, M_DEV, dtype=jnp.int32)
        pick_spread = jax.random.randint(fourth_key, (token_total,), 0, 8, dtype=jnp.int32) == 0
        labels = jnp.where(pick_spread, spread_labels, local_labels)
        shuffled = jax.random.permutation(second_key, token_total)
        labels = labels.at[shuffled[:GROUPS]].set(jnp.arange(GROUPS, dtype=jnp.int32))
        return labels.reshape(FRAMES, PIX)
    return jax.vmap(one_clip)(jax.random.split(key, CLIPS))


def draw_qkv_weight(key, part):
    key = jax.random.fold_in(key, 31)
    base_key = jax.random.fold_in(key, 0)
    base = jnp.clip(jax.random.normal(base_key, (3, D, HEADS * HEAD), jnp.float32), -6.0, 6.0) / D ** 0.5
    return base.astype(jnp.bfloat16)


def gain_values(key, lower, upper):
    return jax.random.uniform(key, (HEAD,), jnp.float32, lower, upper)


def draw_q_gain(key, part):
    key = jax.random.fold_in(key, 21)
    return gain_values(key, 0.5, 1.2)


def draw_k_gain(key, part):
    key = jax.random.fold_in(key, 22)
    return gain_values(key, 0.5, 1.2)


def block_levels(key, dims, cuts, least, largest):
    loudness, own = 1.0, jax.random.fold_in(key, 6)
    for axis_at, parts in cuts:
        draws = jnp.exp(jax.random.uniform(jax.random.fold_in(own, axis_at), (parts,), jnp.float32, least / len(cuts), largest / len(cuts)))
        loudness = loudness * jnp.repeat(draws, dims[axis_at] // parts).reshape([-1 if axis == axis_at else 1 for axis in range(len(dims))])
    return loudness


def scatter_about(key, dims, deviation, limit, cuts=(), kind=jnp.bfloat16):
    entries = jax.random.normal(key, dims, jnp.float32) * deviation
    if len(cuts) > 0:
        entries = block_levels(key, dims, cuts, -0.22, 0.18) * entries
    return jnp.clip(entries, min=-limit, max=limit).astype(kind)


def setup_inputs(seed: int = 0) -> dict:
    seeds = jax.random.split(jax.random.key(seed), 12)
    video = draw_video(jax.random.fold_in(seeds[11], 71), 0)
    conv_weight = scatter_about(seeds[1], (3, CH, CH), (3 * CH) ** -0.5, 0.3125)
    latent_weight = scatter_about(seeds[2], (4 * CH, LAT), (4 * CH) ** -0.5, 0.25)
    assign = draw_assign(jax.random.fold_in(seeds[11], 71), 0)
    embed_weight = scatter_about(seeds[4], (LAT, D), LAT ** -0.5, 0.75)
    norm_gain = jnp.clip(1.0 + 0.18 * jax.random.normal(seeds[5], (D,), jnp.float32), 0.1, 1.9)
    qkv_weight = draw_qkv_weight(jax.random.fold_in(seeds[11], 71), 0)
    q_gain = draw_q_gain(jax.random.fold_in(seeds[11], 71), 0)
    k_gain = draw_k_gain(jax.random.fold_in(seeds[11], 71), 0)
    out_weight = scatter_about(seeds[9], (HEADS * HEAD, D), 0.4, 2.390625, ((0, 16),))
    cotangent = scatter_about(seeds[10], (CLIPS, GROUPS, D), 1.0, 6.0, ((0, 8), (1, 64)))
    return dict(video=video, conv_weight=conv_weight, latent_weight=latent_weight, assign=assign, embed_weight=embed_weight, norm_gain=norm_gain, qkv_weight=qkv_weight, q_gain=q_gain, k_gain=k_gain, out_weight=out_weight, cotangent=cotangent)


def embed_norm(merged_rows, embed_weight, norm_gain):
    embedded = jnp.dot(merged_rows, embed_weight, preferred_element_type=jnp.float32)
    center = embedded - lax.optimization_barrier(jnp.mean(embedded, axis=-1, keepdims=True))
    spread = lax.optimization_barrier(jnp.mean(center * center, axis=-1, keepdims=True))
    return (center * lax.rsqrt(spread + 1e-06) * norm_gain).astype(jnp.bfloat16)

def head_norm(projected_part, gain_vector):
    square_mean = lax.optimization_barrier(jnp.mean(projected_part * projected_part, axis=-1, keepdims=True))
    return (projected_part * lax.rsqrt(square_mean + 1e-06) * gain_vector).astype(jnp.bfloat16)

def reference(video, conv_weight, latent_weight, assign, embed_weight, norm_gain, qkv_weight, q_gain, k_gain, out_weight, cotangent):
    score_scale = 1.0 / math.sqrt(HEAD)

    def one_clip(operands):
        frames, labels, grad_rows = operands
        pixels = frames.reshape(FRAMES, -1, CH)
        padded = jnp.concatenate([jnp.zeros((2,) + pixels.shape[1:], jnp.bfloat16), pixels], axis=0)
        preact = jnp.zeros((FRAMES * pixels.shape[1], CH), jnp.float32)
        for offset in range(3):
            window = padded[2 - offset:2 - offset + FRAMES].reshape(-1, CH)
            preact = preact + jnp.dot(window, conv_weight[offset], preferred_element_type=jnp.float32)
        own_pixels = pixels.reshape(-1, CH).astype(jnp.float32)
        hidden = (own_pixels + jax.nn.silu(preact)).astype(jnp.bfloat16).reshape(FRAMES * PIX, 4 * CH)
        latent = jnp.dot(hidden, latent_weight, preferred_element_type=jnp.float32).astype(jnp.bfloat16)
        flat_labels = labels.reshape(-1)
        group_sum = jax.ops.segment_sum(latent.astype(jnp.float32), flat_labels, num_segments=GROUPS)
        counts = jax.ops.segment_sum(jnp.ones(flat_labels.shape, jnp.float32), flat_labels, num_segments=GROUPS)
        merged = (group_sum / counts[:, None]).astype(jnp.bfloat16)
        normed = embed_norm(merged, embed_weight, norm_gain)
        projected = jnp.einsum('rd,kdc->rkc', normed.astype(jnp.float32), qkv_weight.astype(jnp.float32))
        projected = projected.reshape(GROUPS, 3, HEADS, HEAD)
        queries = head_norm(projected[:, 0], q_gain)
        key_rows = head_norm(projected[:, 1], k_gain)
        value_rows = projected[:, 2].astype(jnp.bfloat16)
        key_bias = jnp.log(counts)

        def one_head(head_parts):
            q_rows, k_rows, v_rows = head_parts
            scores = jnp.dot(q_rows, k_rows.T, preferred_element_type=jnp.float32) * score_scale + key_bias[None, :]
            row_top = lax.optimization_barrier(jnp.max(scores, axis=-1, keepdims=True))
            weights = jnp.exp(scores - row_top)
            denominator = lax.optimization_barrier(jnp.sum(weights, axis=-1, keepdims=True))
            mixed = jnp.dot(weights.astype(jnp.bfloat16), v_rows, preferred_element_type=jnp.float32)
            return (mixed / denominator).astype(jnp.bfloat16)
        head_out = lax.map(one_head, (queries.transpose(1, 0, 2), key_rows.transpose(1, 0, 2), value_rows.transpose(1, 0, 2)))
        flat_out = head_out.transpose(1, 0, 2).reshape(GROUPS, HEADS * HEAD)
        attended = jnp.dot(flat_out, out_weight, preferred_element_type=jnp.float32)
        weight_grad = jnp.dot(flat_out.T, grad_rows, preferred_element_type=jnp.float32)
        return (attended.astype(jnp.bfloat16), weight_grad)
    attended, weight_grads = lax.map(one_clip, (video, assign, cotangent))
    return (attended, lax.optimization_barrier(jnp.sum(weight_grads, axis=0)).astype(jnp.bfloat16))
```

```python
import functools
import math

import jax
import jax.numpy as jnp
from jax import lax
from jax.experimental import pallas as pl
from jax.experimental.pallas import tpu as pltpu
from jax.sharding import PartitionSpec as P

F32 = jnp.float32
BF16 = jnp.bfloat16
LANES = 128
HALF = 64
NT = (((1,), (1,)), ((), ()))
TN = (((0,), (0,)), ((), ()))


def shifted_frames(block, axis, distance):
    devices = range(lax.axis_size(axis))
    route = [(i - distance, i) for i in devices if i - distance in devices]
    return lax.ppermute(block, axis, route)


def xor_swap(block, axis, mask):
    route = [(i, i ^ mask) for i in range(lax.axis_size(axis))]
    return lax.ppermute(block, axis, route)


def lane_index(rows):
    return lax.broadcasted_iota(jnp.int32, (rows, LANES), 1)


def split_pairs(sums):
    lane = lane_index(sums.shape[0])
    high = sums.astype(BF16).astype(F32)
    keep = jnp.logical_or(lane < HALF, lane == LANES - 2)
    return jnp.where(keep, high, sums - high).astype(BF16)


def join_pairs(pairs):
    lane = lane_index(pairs.shape[0])
    total = pairs + jnp.where(lane < HALF - 2, pltpu.roll(pairs, HALF, 1), 0.0)
    counts = pairs[:, LANES - 2 : LANES - 1] + pairs[:, LANES - 1 :]
    return total, counts


def latent_rows(windows, conv_ref, latent_ref):
    channels = conv_ref.shape[1]
    taps = conv_ref[...].reshape(3 * channels, channels)
    weights = jnp.concatenate([latent_ref[...], latent_ref[...]], axis=0)
    latent = None
    for part, views in enumerate(windows):
        cols = slice(part * channels, (part + 1) * channels)
        preact = jnp.dot(jnp.concatenate(views, axis=1), taps, preferred_element_type=F32)
        hidden = (views[0].astype(F32) + preact / (1.0 + jnp.exp(-preact))).astype(BF16)
        term = lax.dot_general(hidden, weights[:, cols], NT, preferred_element_type=F32)
        latent = term if latent is None else latent + term
    return jnp.where(lane_index(latent.shape[0]) < LANES - 2, latent, 1.0).astype(BF16)


def late_kernel(video_ref, conv_ref, latent_ref, out_ref):
    frame_count, tokens, width = video_ref.shape
    channels = conv_ref.shape[1]
    windows = []
    for start in range(0, width, channels):
        cols = slice(start, start + channels)
        windows.append([
            video_ref[2 - k : frame_count - k, :, cols].reshape(-1, channels) for k in range(3)
        ])
    out_ref[...] = latent_rows(windows, conv_ref, latent_ref)


def sums_kernel(
    video_ref, earlier_ref, conv_ref, latent_ref, late_ref, labels_ref, out_ref, *, grp, seq,
):
    channels = conv_ref.shape[1]
    width = video_ref.shape[2]
    windows = []
    for start in range(0, width, channels):
        cols = slice(start, start + channels)
        padded = jnp.concatenate([earlier_ref[:, :, cols], video_ref[:2, :, cols]], axis=0)
        windows.append([padded[2 - k : 4 - k].reshape(-1, channels) for k in range(3)])
    first = latent_rows(windows, conv_ref, latent_ref)
    rows = jnp.concatenate([first, late_ref[...]], axis=0)
    labels = labels_ref[...]
    total = out_ref.shape[0]
    block = total // (grp * seq)
    step = 256
    for start in range(0, total, step):
        place = lax.broadcasted_iota(jnp.int32, (step, labels.shape[1]), 0) + start
        inner = place & (block - 1)
        column = (place >> (block.bit_length() - 1)) & (grp - 1)
        slab = place >> ((block * grp).bit_length() - 1)
        member = (labels == (column * seq + slab) * block + inner).astype(F32).astype(BF16)
        out_ref[start : start + step, :] = split_pairs(
            jnp.dot(member, rows, preferred_element_type=F32)
        )


def add_up(parts_ref):
    total = parts_ref[0].astype(F32)
    for i in range(1, parts_ref.shape[0]):
        total = total + parts_ref[i].astype(F32)
    return total


def resplit_kernel(parts_ref, out_ref):
    total, counts = join_pairs(add_up(parts_ref))
    lane = lane_index(total.shape[0])
    doubled = jnp.where(lane < HALF, total, pltpu.roll(total, HALF, 1))
    pairs = split_pairs(jnp.where(lane < LANES - 2, doubled, counts))
    for i in range(out_ref.shape[0]):
        out_ref[i] = pairs


def merge_kernel(parts_ref, out_ref):
    total, counts = join_pairs(add_up(parts_ref))
    lane = lane_index(total.shape[0])
    merged = jnp.where(lane < HALF, total / counts, 0.0)
    high = counts.astype(BF16).astype(F32)
    marks = jnp.where(lane == LANES - 2, high, counts - high)
    rows = jnp.where(lane < LANES - 2, merged, marks).astype(BF16)
    for i in range(out_ref.shape[0]):
        out_ref[i] = rows


def spread_kernel(parts_ref, out_ref):
    total = add_up(parts_ref).astype(BF16)
    for i in range(out_ref.shape[0]):
        out_ref[i] = total


def head_norm(projected, gain):
    square_mean = jnp.mean(projected * projected, axis=-1, keepdims=True)
    return (projected * lax.rsqrt(square_mean + 1e-06) * gain).astype(BF16)


def attend_kernel(
    merged_ref, embed_ref, norm_ref, qkv_ref, qgain_ref, kgain_ref, out_ref,
    kv_ref, q_ref, k_ref, v_ref,
):
    latents, width = embed_ref.shape
    head = q_ref.shape[1]
    total = out_ref.shape[0]
    step = 256
    kv_ref[:, :head] = qkv_ref[1]
    kv_ref[:, head:] = qkv_ref[2]
    pick = (lane_index(16) >= LANES - 2).astype(F32).astype(BF16)
    count_row = lax.dot_general(pick, merged_ref[...], NT, preferred_element_type=F32)[0:1, :]
    bias = jnp.log(count_row)
    ones = jnp.ones((16, width), BF16)
    embed_mean = lax.dot_general(ones, embed_ref[...], NT, preferred_element_type=F32)
    embed_mean = embed_mean[0:1, :] * (1.0 / width)
    embed = jnp.concatenate([embed_ref[...], jnp.ones((LANES - latents, width), BF16)], axis=0)
    lane = lane_index(step)
    for start in range(0, total, step):
        here = slice(start, start + step)
        rows = merged_ref[here, :].astype(F32)
        mean = -jnp.sum(rows[:, :latents] * embed_mean, axis=-1, keepdims=True)
        high = mean.astype(BF16).astype(F32)
        middle = (mean - high).astype(BF16).astype(F32)
        low = mean - high - middle
        tail = jnp.where(lane == latents, high, 0.0)
        tail = jnp.where(lane == latents + 1, middle, tail)
        tail = jnp.where(lane == latents + 2, low, tail)
        factors = jnp.where(lane < latents, rows, tail).astype(BF16)
        center = jnp.dot(factors, embed, preferred_element_type=F32)
        spread = jnp.mean(center * center, axis=-1, keepdims=True)
        normed = (center * lax.rsqrt(spread + 1e-06) * norm_ref[...]).astype(BF16)
        q_part = jnp.dot(normed, qkv_ref[0], preferred_element_type=F32)
        kv_part = jnp.dot(normed, kv_ref[...], preferred_element_type=F32)
        q_ref[here, :] = head_norm(q_part, qgain_ref[...])
        k_ref[here, :] = head_norm(kv_part[:, :head], kgain_ref[...])
        v_ref[here, :] = kv_part[:, head:].astype(BF16)
    scale = 1.0 / math.sqrt(head)
    for start in range(0, total, step):
        here = slice(start, start + step)
        scores = lax.dot_general(
            q_ref[here, :], k_ref[...], NT, preferred_element_type=F32
        ) * scale + bias
        top = jnp.max(scores, axis=-1, keepdims=True)
        weights = jnp.exp(scores - top)
        denominator = jnp.sum(weights, axis=-1, keepdims=True)
        mixed = jnp.dot(weights.astype(BF16), v_ref[...], preferred_element_type=F32)
        out_ref[here, :] = (mixed / denominator).astype(BF16)


def call(body, shape, dtype, *args, name, scratch=(), flops=10**8, moved=10**6):
    return pl.pallas_call(
        body,
        out_shape=jax.ShapeDtypeStruct(shape, dtype),
        in_specs=[pl.BlockSpec(memory_space=pltpu.VMEM)] * len(args),
        out_specs=pl.BlockSpec(memory_space=pltpu.VMEM),
        scratch_shapes=list(scratch),
        cost_estimate=pl.CostEstimate(flops=flops, bytes_accessed=moved, transcendentals=0),
        compiler_params=pltpu.CompilerParams(vmem_limit_bytes=48 * 2**20),
        name=name,
    )(*args)


def shards(
    video, conv_weight, latent_weight, assign, embed_weight, norm_gain, qkv_weight, q_gain, k_gain,
    out_weight, cotangent,
):
    grp_size, seq_size, dp_size = (lax.axis_size(a) for a in ("grp", "seq", "dp"))
    slabs = seq_size // 2
    owners = grp_size * seq_size
    block, width = cotangent.shape[1:]
    head = q_gain.shape[0]
    groups = block * owners
    columns = width // grp_size
    grp = lax.axis_index("grp")
    seq = lax.axis_index("seq")
    same_side = [list(range(k, seq_size, 2)) for k in range(2)]

    frames = video[0]
    frame_count, tokens = frames.shape[:2]
    earlier = shifted_frames(frames[frame_count - 2 :], "seq", 1)
    latent_t = latent_weight.T
    labels = assign[0].reshape(1, -1)
    late = call(
        late_kernel, ((frame_count - 2) * tokens, LANES), BF16, frames, conv_weight, latent_t,
        name="late_frames", flops=10**9,
    )
    sums = call(
        functools.partial(sums_kernel, grp=grp_size, seq=seq_size), (groups, LANES), BF16,
        frames, earlier, conv_weight, latent_t, late, labels, name="group_sums", flops=10**9,
    )

    shared = block * grp_size
    parts = lax.all_to_all(sums.reshape(seq_size, shared, LANES), "seq", 0, 0, tiled=True)
    slab_sums = call(resplit_kernel, (grp_size, shared, LANES), BF16, parts, name="slab_sums")
    slab_parts = lax.all_to_all(slab_sums, "grp", 0, 0, tiled=True)
    merged = call(merge_kernel, (seq_size, shared, LANES), BF16, slab_parts, name="merged")
    merged = lax.all_to_all(merged, "seq", 0, 0, tiled=True).reshape(groups, LANES)

    cot, _ = lax.optimization_barrier((cotangent, sums))
    by_column = cot[0].reshape(block, grp_size, columns).transpose(1, 0, 2)
    by_column = jnp.broadcast_to(by_column[None], (2,) + by_column.shape)
    corners = [
        [g * seq_size + 2 * z + y for y in range(2) for g in range(grp_size)] for z in range(slabs)
    ]
    near = lax.all_to_all(
        by_column.reshape(2 * grp_size, block, columns), ("grp", "seq"), 0, 0,
        axis_index_groups=corners, tiled=True,
    ).reshape(2 * shared, columns)
    far = lax.all_to_all(
        jnp.broadcast_to(near[None], (slabs,) + near.shape), "seq", 0, 0,
        axis_index_groups=same_side, tiled=True,
    )
    grad_rows = far.reshape(groups, columns)

    late_weight, _ = lax.optimization_barrier((out_weight, slab_parts))
    weight_pair = xor_swap(late_weight, "seq", 1)

    head_out = call(
        attend_kernel, (groups, head), BF16, merged, embed_weight, norm_gain[None], qkv_weight,
        q_gain[None], k_gain[None], name="attend", flops=8 * 10**9,
        scratch=[pltpu.VMEM((width, 2 * head), BF16)] + [pltpu.VMEM((groups, head), BF16)] * 3,
    )

    side = seq % 2
    by_owner = lax.dynamic_index_in_dim(
        head_out.reshape(slabs, 2, grp_size, block, head), grp, 2, keepdims=False
    )
    mine = lax.dynamic_index_in_dim(by_owner, side, 1, keepdims=False)
    theirs = xor_swap(lax.dynamic_index_in_dim(by_owner, 1 - side, 1, keepdims=False), "seq", 1)

    local_grad = lax.dot_general(
        head_out, grad_rows, TN, preferred_element_type=F32
    ).astype(BF16)
    grad_parts = lax.all_to_all(
        local_grad.reshape(dp_size, head // dp_size, columns), "dp", 0, 0, tiled=True
    )

    both = jnp.concatenate([mine, theirs], axis=2).reshape(-1, 2 * head)
    both_weights = jnp.concatenate([out_weight, weight_pair], axis=0)
    partial = jnp.dot(both, both_weights, preferred_element_type=F32).astype(BF16)
    out_parts = lax.all_to_all(
        partial.reshape(slabs, block, width), "seq", 0, 0, axis_index_groups=same_side, tiled=True
    )

    grad_block = call(
        spread_kernel, (dp_size, head // dp_size, columns), BF16, grad_parts, name="grad_block"
    )
    grad_cols = lax.all_to_all(grad_block, "dp", 0, 0, tiled=True).reshape(head, columns)
    out_grad = lax.all_to_all(
        jnp.broadcast_to(grad_cols[None], (grp_size, head, columns)), "grp", 0, 0, tiled=True
    )
    out_grad = out_grad.transpose(1, 0, 2).reshape(head, width)
    attended = jnp.sum(out_parts.astype(F32), axis=0).astype(BF16)
    return (attended[None], out_grad)


def solution(mesh):
    placed = (
        P("dp", "seq", "grp", None), P(), P(), P("dp", "seq", "grp"), P(), P(),
        P(None, None, "seq"), P(), P(), P("seq", None), P("dp", ("grp", "seq"), None),
    )
    return jax.shard_map(
        shards,
        mesh=mesh,
        in_specs=placed,
        out_specs=(P("dp", ("grp", "seq"), None), P("seq", None)),
        check_vma=False,
    )
```

```python
import functools
import math

import jax
import jax.numpy as jnp
from jax import lax
from jax.experimental import pallas as pl
from jax.experimental.pallas import tpu as pltpu
from jax.sharding import PartitionSpec as P

F32 = jnp.float32
BF16 = jnp.bfloat16
LANES = 128
HALF = 64
NT = (((1,), (1,)), ((), ()))
TN = (((0,), (0,)), ((), ()))


def shifted_frames(block, axis, distance):
    devices = range(lax.axis_size(axis))
    route = [(i - distance, i) for i in devices if i - distance in devices]
    return lax.ppermute(block, axis, route)


def xor_swap(block, axis, mask):
    route = [(i, i ^ mask) for i in range(lax.axis_size(axis))]
    return lax.ppermute(block, axis, route)


def lane_index(rows):
    return lax.broadcasted_iota(jnp.int32, (rows, LANES), 1)


def split_pairs(sums):
    lane = lane_index(sums.shape[0])
    high = sums.astype(BF16).astype(F32)
    keep = jnp.logical_or(lane < HALF, lane == LANES - 2)
    return jnp.where(keep, high, sums - high).astype(BF16)


def join_pairs(pairs):
    lane = lane_index(pairs.shape[0])
    total = pairs + jnp.where(lane < HALF - 2, pltpu.roll(pairs, HALF, 1), 0.0)
    counts = pairs[:, LANES - 2 : LANES - 1] + pairs[:, LANES - 1 :]
    return total, counts


def latent_rows(windows, conv_ref, latent_ref):
    channels = conv_ref.shape[1]
    taps = conv_ref[...].reshape(3 * channels, channels)
    weights = jnp.concatenate([latent_ref[...], latent_ref[...]], axis=0)
    latent = None
    for part, views in enumerate(windows):
        cols = slice(part * channels, (part + 1) * channels)
        preact = jnp.dot(jnp.concatenate(views, axis=1), taps, preferred_element_type=F32)
        hidden = (views[0].astype(F32) + preact / (1.0 + jnp.exp(-preact))).astype(BF16)
        term = lax.dot_general(hidden, weights[:, cols], NT, preferred_element_type=F32)
        latent = term if latent is None else latent + term
    return jnp.where(lane_index(latent.shape[0]) < LANES - 2, latent, 1.0).astype(BF16)


def late_kernel(video_hbm, conv_hbm, latent_hbm, out_ref, video_ref, conv_ref, latent_ref, sems):
    copies = [
        pltpu.make_async_copy(src, dst, sems.at[i])
        for i, (src, dst) in enumerate(
            [(video_hbm, video_ref), (conv_hbm, conv_ref), (latent_hbm, latent_ref)]
        )
    ]
    for copy in copies:
        copy.start()
    for copy in copies:
        copy.wait()
    frame_count, tokens, width = video_ref.shape
    channels = conv_ref.shape[1]
    windows = []
    for start in range(0, width, channels):
        cols = slice(start, start + channels)
        windows.append([
            video_ref[2 - k : frame_count - k, :, cols].reshape(-1, channels) for k in range(3)
        ])
    out_ref[...] = latent_rows(windows, conv_ref, latent_ref)


def sums_kernel(
    video_ref, earlier_ref, conv_ref, latent_ref, late_ref, labels_ref, out_ref, *, grp, seq,
):
    channels = conv_ref.shape[1]
    width = video_ref.shape[2]
    windows = []
    for start in range(0, width, channels):
        cols = slice(start, start + channels)
        padded = jnp.concatenate([earlier_ref[:, :, cols], video_ref[:2, :, cols]], axis=0)
        windows.append([padded[2 - k : 4 - k].reshape(-1, channels) for k in range(3)])
    first = latent_rows(windows, conv_ref, latent_ref)
    rows = jnp.concatenate([first, late_ref[...]], axis=0)
    labels = labels_ref[...]
    total = out_ref.shape[0]
    block = total // (grp * seq)
    step = 256
    for start in range(0, total, step):
        place = lax.broadcasted_iota(jnp.int32, (step, labels.shape[1]), 0) + start
        inner = place & (block - 1)
        column = (place >> (block.bit_length() - 1)) & (grp - 1)
        slab = place >> ((block * grp).bit_length() - 1)
        member = (labels == (column * seq + slab) * block + inner).astype(F32).astype(BF16)
        out_ref[start : start + step, :] = split_pairs(
            jnp.dot(member, rows, preferred_element_type=F32)
        )


def add_up(parts_ref):
    total = parts_ref[0].astype(F32)
    for i in range(1, parts_ref.shape[0]):
        total = total + parts_ref[i].astype(F32)
    return total


def resplit_kernel(parts_ref, out_ref):
    total, counts = join_pairs(add_up(parts_ref))
    lane = lane_index(total.shape[0])
    doubled = jnp.where(lane < HALF, total, pltpu.roll(total, HALF, 1))
    pairs = split_pairs(jnp.where(lane < LANES - 2, doubled, counts))
    for i in range(out_ref.shape[0]):
        out_ref[i] = pairs


def merge_kernel(parts_ref, out_ref):
    total, counts = join_pairs(add_up(parts_ref))
    lane = lane_index(total.shape[0])
    merged = jnp.where(lane < HALF, total / counts, 0.0)
    high = counts.astype(BF16).astype(F32)
    marks = jnp.where(lane == LANES - 2, high, counts - high)
    rows = jnp.where(lane < LANES - 2, merged, marks).astype(BF16)
    for i in range(out_ref.shape[0]):
        out_ref[i] = rows


def spread_kernel(parts_ref, out_ref):
    total = add_up(parts_ref).astype(BF16)
    for i in range(out_ref.shape[0]):
        out_ref[i] = total


def grad_kernel(place_ref, head_ref, first_ref, second_ref, out_ref, rows_ref, *, masks):
    seq = place_ref[1]
    half = first_ref.shape[0]
    part = rows_ref.shape[0] >> len(masks)
    for slot in range(1 << len(masks)):
        mask = sum(m for bit, m in enumerate(masks) if slot >> bit & 1)
        start = pl.multiple_of((seq ^ mask) * part, part)
        rows_ref[slot * part : (slot + 1) * part, :] = head_ref[pl.ds(start, part), :]
    out_ref[...] = (
        lax.dot_general(rows_ref[:half, :], first_ref[...], TN, preferred_element_type=F32)
        + lax.dot_general(rows_ref[half:, :], second_ref[...], TN, preferred_element_type=F32)
    ).astype(BF16)


def project_kernel(place_ref, heads_ref, weight_ref, out_ref):
    member = place_ref[1] & 3
    heads = jnp.concatenate([heads_ref[member ^ k] for k in range(4)], axis=1)
    out_ref[...] = jnp.dot(heads, weight_ref[...], preferred_element_type=F32).astype(BF16)


def attended_kernel(parts_ref, out_ref):
    columns = parts_ref.shape[2]
    for t in range(4):
        total = parts_ref[t].astype(F32)
        for i in range(t + 4, parts_ref.shape[0], 4):
            total = total + parts_ref[i].astype(F32)
        start = (2 * (t & 1) + (t >> 1)) * columns
        out_ref[:, start : start + columns] = total.astype(BF16)


def columns_kernel(place_ref, *refs):
    out_ref = refs[-1]
    columns = refs[0].shape[1]
    for k, ref in enumerate(refs[:-1]):
        start = pl.multiple_of((place_ref[0] ^ k) * columns, columns)
        out_ref[:, pl.ds(start, columns)] = ref[...]


def head_norm(projected, gain):
    square_mean = jnp.mean(projected * projected, axis=-1, keepdims=True)
    return (projected * lax.rsqrt(square_mean + 1e-06) * gain).astype(BF16)


def attend_kernel(
    place_ref, merged_ref, embed_ref, norm_ref, qkv_ref, qgain_ref, kgain_ref, out_ref, own_ref,
    kv_ref, q_ref, k_ref, v_ref, *, grp_size, block,
):
    latents, width = embed_ref.shape
    head = q_ref.shape[1]
    total = out_ref.shape[0]
    step = 256
    kv_ref[:, :head] = qkv_ref[1]
    kv_ref[:, head:] = qkv_ref[2]
    pick = (lane_index(16) >= LANES - 2).astype(F32).astype(BF16)
    count_row = lax.dot_general(pick, merged_ref[...], NT, preferred_element_type=F32)[0:1, :]
    bias = jnp.log(count_row)
    ones = jnp.ones((16, width), BF16)
    embed_mean = lax.dot_general(ones, embed_ref[...], NT, preferred_element_type=F32)
    embed_mean = embed_mean[0:1, :] * (1.0 / width)
    embed = jnp.concatenate([embed_ref[...], jnp.ones((LANES - latents, width), BF16)], axis=0)
    lane = lane_index(step)
    for start in range(0, total, step):
        here = slice(start, start + step)
        rows = merged_ref[here, :].astype(F32)
        mean = -jnp.sum(rows[:, :latents] * embed_mean, axis=-1, keepdims=True)
        high = mean.astype(BF16).astype(F32)
        middle = (mean - high).astype(BF16).astype(F32)
        low = mean - high - middle
        tail = jnp.where(lane == latents, high, 0.0)
        tail = jnp.where(lane == latents + 1, middle, tail)
        tail = jnp.where(lane == latents + 2, low, tail)
        factors = jnp.where(lane < latents, rows, tail).astype(BF16)
        center = jnp.dot(factors, embed, preferred_element_type=F32)
        spread = jnp.mean(center * center, axis=-1, keepdims=True)
        normed = (center * lax.rsqrt(spread + 1e-06) * norm_ref[...]).astype(BF16)
        q_part = jnp.dot(normed, qkv_ref[0], preferred_element_type=F32)
        kv_part = jnp.dot(normed, kv_ref[...], preferred_element_type=F32)
        q_ref[here, :] = head_norm(q_part, qgain_ref[...])
        k_ref[here, :] = head_norm(kv_part[:, :head], kgain_ref[...])
        v_ref[here, :] = kv_part[:, head:].astype(BF16)
    scale = 1.0 / math.sqrt(head)
    for start in range(0, total, step):
        here = slice(start, start + step)
        scores = lax.dot_general(
            q_ref[here, :], k_ref[...], NT, preferred_element_type=F32
        ) * scale + bias
        top = jnp.max(scores, axis=-1, keepdims=True)
        weights = jnp.exp(scores - top)
        denominator = jnp.sum(weights, axis=-1, keepdims=True)
        mixed = jnp.dot(weights.astype(BF16), v_ref[...], preferred_element_type=F32)
        out_ref[here, :] = (mixed / denominator).astype(BF16)
    grp = place_ref[0]
    for i in range(total // (block * grp_size)):
        start = pl.multiple_of((i * grp_size + grp) * block, block)
        mine = out_ref[pl.ds(start, block), :]
        for j in range(own_ref.shape[0]):
            own_ref[j, i * block : (i + 1) * block, :] = mine


def call(body, shapes, *args, name, scratch=(), places=(), flops=10**8, moved=10**6):
    spaces = {"smem": pltpu.SMEM, "any": pl.ANY}
    outs = tuple(jax.ShapeDtypeStruct(shape, BF16) for shape in shapes)
    whole = pl.BlockSpec(memory_space=pltpu.VMEM)
    in_specs = [whole] * len(args)
    for i, place in enumerate(places):
        in_specs[i] = pl.BlockSpec(memory_space=spaces[place])
    result = pl.pallas_call(
        body,
        out_shape=outs,
        in_specs=in_specs,
        out_specs=(whole,) * len(outs),
        scratch_shapes=list(scratch),
        cost_estimate=pl.CostEstimate(flops=flops, bytes_accessed=moved, transcendentals=0),
        compiler_params=pltpu.CompilerParams(vmem_limit_bytes=48 * 2**20),
        name=name,
    )(*args)
    return result[0] if len(outs) == 1 else result


def shards(
    video, conv_weight, latent_weight, assign, embed_weight, norm_gain, qkv_weight, q_gain, k_gain,
    out_weight, cotangent,
):
    grp_size, seq_size, dp_size = (lax.axis_size(a) for a in ("grp", "seq", "dp"))
    owners = grp_size * seq_size
    block, width = cotangent.shape[1:]
    head = q_gain.shape[0]
    groups = block * owners
    columns = width // grp_size
    shared = block * grp_size
    rows = block * seq_size
    grp = lax.axis_index("grp")
    seq = lax.axis_index("seq")
    place = jnp.stack([grp, seq]).astype(jnp.int32)

    frames = video[0]
    frame_count, tokens = frames.shape[:2]
    earlier = shifted_frames(frames[frame_count - 2 :], "seq", 1)
    latent_t = latent_weight.T
    labels = assign[0].reshape(1, -1)
    late = call(
        late_kernel, [((frame_count - 2) * tokens, LANES)], frames, conv_weight, latent_t,
        name="late_frames", flops=10**9, places=["any"] * 3,
        scratch=[
            pltpu.VMEM(x.shape, BF16) for x in (frames, conv_weight, latent_t)
        ] + [pltpu.SemaphoreType.DMA((3,))],
    )
    sums = call(
        functools.partial(sums_kernel, grp=grp_size, seq=seq_size), [(groups, LANES)],
        frames, earlier, conv_weight, latent_t, late, labels, name="group_sums", flops=10**9,
    )

    by_column = jnp.concatenate(
        [cotangent[0, :, g * columns : (g + 1) * columns] for g in range(grp_size)], axis=0
    ).reshape(grp_size, block, columns)
    near = lax.all_to_all(by_column, "grp", 0, 0, tiled=True).reshape(shared, columns)

    parts = lax.all_to_all(sums.reshape(seq_size, shared, LANES), "seq", 0, 0, tiled=True)
    slab_sums = call(resplit_kernel, [(grp_size, shared, LANES)], parts, name="slab_sums")
    slab_parts = lax.all_to_all(slab_sums, "grp", 0, 0, tiled=True)
    merged = call(merge_kernel, [(seq_size, shared, LANES)], slab_parts, name="merged")
    merged = lax.all_to_all(merged, "seq", 0, 0, tiled=True).reshape(groups, LANES)

    masks = (8, 4, 1, 2)
    for mask in masks[:-1]:
        near = jnp.concatenate([near, xor_swap(near, "seq", mask)], axis=0)
    far = xor_swap(near, "seq", masks[-1])

    side = seq & 1
    depth = (seq >> 1) & 1

    def halved(block, choice, mask):
        size = block.shape[1] // 2
        kept = lax.dynamic_slice_in_dim(block, choice * size, size, 1)
        given = lax.dynamic_slice_in_dim(block, (1 - choice) * size, size, 1)
        return jnp.concatenate([kept, xor_swap(given, "seq", mask)], axis=0)

    weight, _ = lax.optimization_barrier((out_weight, slab_sums))
    weight_quad = halved(halved(weight, side, 1), depth, 2)

    head_out, own_rows = call(
        functools.partial(attend_kernel, grp_size=grp_size, block=block),
        [(groups, head), (4, rows, head)], place, merged, embed_weight, norm_gain[None],
        qkv_weight, q_gain[None], k_gain[None], name="attend", flops=8 * 10**9, places=["smem"],
        scratch=[pltpu.VMEM((width, 2 * head), BF16)] + [pltpu.VMEM((groups, head), BF16)] * 3,
    )

    quads = [list(range(k, k + 4)) for k in range(0, seq_size, 4)]
    quad_heads = lax.all_to_all(own_rows, "seq", 0, 0, axis_index_groups=quads, tiled=True)
    local_grad = call(
        functools.partial(grad_kernel, masks=masks), [(head, columns)], place, head_out, near, far,
        name="local_grad", places=["smem"], scratch=[pltpu.VMEM((groups, head), BF16)],
        flops=10**9,
    )
    grad_parts = lax.all_to_all(
        local_grad.reshape(dp_size, head // dp_size, columns), "dp", 0, 0, tiled=True
    )
    grad_block = call(
        spread_kernel, [(dp_size, head // dp_size, columns)], grad_parts, name="grad_block"
    )
    grad_cols = lax.all_to_all(grad_block, "dp", 0, 0, tiled=True).reshape(head, columns)

    partial = call(
        project_kernel, [(rows, columns)], place, quad_heads, weight_quad, name="project",
        places=["smem"], flops=10**9,
    )
    partial, _ = lax.optimization_barrier((partial, grad_cols))
    out_parts = lax.all_to_all(
        partial.reshape(seq_size, block, columns), "seq", 0, 0, tiled=True
    )
    gathered = [grad_cols] + [xor_swap(grad_cols, "grp", k) for k in range(1, grp_size)]
    out_grad = call(
        columns_kernel, [(head, width)], place, *gathered, name="grad_columns", places=["smem"]
    )
    attended = call(attended_kernel, [(block, width)], out_parts, name="attended")
    return (attended[None], out_grad)


def solution(mesh):
    placed = (
        P("dp", "seq", "grp", None), P(), P(), P("dp", "seq", "grp"), P(), P(),
        P(None, None, "seq"), P(), P(), P("seq", None), P("dp", ("grp", "seq"), None),
    )
    return jax.shard_map(
        shards,
        mesh=mesh,
        in_specs=placed,
        out_specs=(P("dp", ("grp", "seq"), None), P("seq", None)),
        check_vma=False,
    )
```

```python
import functools
import math

import jax
import jax.numpy as jnp
from jax import lax
from jax.experimental import pallas as pl
from jax.experimental.pallas import tpu as pltpu
from jax.sharding import PartitionSpec as P

F32 = jnp.float32
BF16 = jnp.bfloat16
LANES = 128
HALF = 64
NT = (((1,), (1,)), ((), ()))
TN = (((0,), (0,)), ((), ()))


def shifted_frames(block, axis, distance):
    devices = range(lax.axis_size(axis))
    route = [(i - distance, i) for i in devices if i - distance in devices]
    return lax.ppermute(block, axis, route)


def xor_swap(block, axis, mask):
    route = [(i, i ^ mask) for i in range(lax.axis_size(axis))]
    return lax.ppermute(block, axis, route)


def lane_index(rows):
    return lax.broadcasted_iota(jnp.int32, (rows, LANES), 1)


def split_pairs(sums):
    lane = lane_index(sums.shape[0])
    high = sums.astype(BF16).astype(F32)
    keep = jnp.logical_or(lane < HALF, lane == LANES - 2)
    return jnp.where(keep, high, sums - high).astype(BF16)


def join_pairs(pairs):
    lane = lane_index(pairs.shape[0])
    total = pairs + jnp.where(lane < HALF - 2, pltpu.roll(pairs, HALF, 1), 0.0)
    counts = pairs[:, LANES - 2 : LANES - 1] + pairs[:, LANES - 1 :]
    return total, counts


def latent_rows(windows, conv_ref, latent_ref):
    channels = conv_ref.shape[1]
    taps = conv_ref[...].reshape(3 * channels, channels)
    weights = jnp.concatenate([latent_ref[...], latent_ref[...]], axis=0)
    latent = None
    for part, views in enumerate(windows):
        cols = slice(part * channels, (part + 1) * channels)
        preact = jnp.dot(jnp.concatenate(views, axis=1), taps, preferred_element_type=F32)
        hidden = (views[0].astype(F32) + preact / (1.0 + jnp.exp(-preact))).astype(BF16)
        term = lax.dot_general(hidden, weights[:, cols], NT, preferred_element_type=F32)
        latent = term if latent is None else latent + term
    return jnp.where(lane_index(latent.shape[0]) < LANES - 2, latent, 1.0).astype(BF16)


def late_kernel(
    video_hbm, conv_hbm, latent_hbm, out_ref, first_ref, conv_ref, latent_ref, video_ref, sems,
):
    copies = [
        pltpu.make_async_copy(src, dst, sems.at[i])
        for i, (src, dst) in enumerate([
            (video_hbm, video_ref), (conv_hbm, conv_ref), (latent_hbm, latent_ref),
            (video_hbm.at[: first_ref.shape[0]], first_ref),
        ])
    ]
    for copy in copies:
        copy.start()
    for copy in copies:
        copy.wait()
    frame_count, tokens, width = video_ref.shape
    channels = conv_ref.shape[1]
    windows = []
    for start in range(0, width, channels):
        cols = slice(start, start + channels)
        windows.append([
            video_ref[2 - k : frame_count - k, :, cols].reshape(-1, channels) for k in range(3)
        ])
    out_ref[...] = latent_rows(windows, conv_ref, latent_ref)


def sums_kernel(
    video_ref, earlier_ref, conv_ref, latent_ref, late_ref, labels_ref, out_ref, *, grp, seq,
):
    channels = conv_ref.shape[1]
    width = video_ref.shape[2]
    windows = []
    for start in range(0, width, channels):
        cols = slice(start, start + channels)
        padded = jnp.concatenate([earlier_ref[:, :, cols], video_ref[:, :, cols]], axis=0)
        windows.append([padded[2 - k : 4 - k].reshape(-1, channels) for k in range(3)])
    first = latent_rows(windows, conv_ref, latent_ref)
    rows = jnp.concatenate([first, late_ref[...]], axis=0)
    labels = labels_ref[...]
    total = out_ref.shape[0]
    block = total // (grp * seq)
    step = 256
    for start in range(0, total, step):
        place = lax.broadcasted_iota(jnp.int32, (step, labels.shape[1]), 0) + start
        inner = place & (block - 1)
        column = (place >> (block.bit_length() - 1)) & (grp - 1)
        slab = place >> ((block * grp).bit_length() - 1)
        member = (labels == (column * seq + slab) * block + inner).astype(F32).astype(BF16)
        out_ref[start : start + step, :] = split_pairs(
            jnp.dot(member, rows, preferred_element_type=F32)
        )


def add_up(parts_ref):
    total = parts_ref[0].astype(F32)
    for i in range(1, parts_ref.shape[0]):
        total = total + parts_ref[i].astype(F32)
    return total


def resplit_kernel(parts_ref, out_ref):
    total, counts = join_pairs(add_up(parts_ref))
    lane = lane_index(total.shape[0])
    doubled = jnp.where(lane < HALF, total, pltpu.roll(total, HALF, 1))
    pairs = split_pairs(jnp.where(lane < LANES - 2, doubled, counts))
    for i in range(out_ref.shape[0]):
        out_ref[i] = pairs


def merge_kernel(parts_ref, out_ref):
    total, counts = join_pairs(add_up(parts_ref))
    lane = lane_index(total.shape[0])
    merged = jnp.where(lane < HALF, total / counts, 0.0)
    high = counts.astype(BF16).astype(F32)
    marks = jnp.where(lane == LANES - 2, high, counts - high)
    rows = jnp.where(lane < LANES - 2, merged, marks).astype(BF16)
    for i in range(out_ref.shape[0]):
        out_ref[i] = rows


def spread_kernel(parts_ref, out_ref):
    total = add_up(parts_ref).astype(BF16)
    for i in range(out_ref.shape[0]):
        out_ref[i] = total


def grad_kernel(place_ref, head_ref, first_ref, second_ref, out_ref, rows_ref, *, masks):
    seq = place_ref[1]
    half = first_ref.shape[0]
    part = rows_ref.shape[0] >> len(masks)
    for slot in range(1 << len(masks)):
        mask = sum(m for bit, m in enumerate(masks) if slot >> bit & 1)
        start = pl.multiple_of((seq ^ mask) * part, part)
        rows_ref[slot * part : (slot + 1) * part, :] = head_ref[pl.ds(start, part), :]
    out_ref[...] = (
        lax.dot_general(rows_ref[:half, :], first_ref[...], TN, preferred_element_type=F32)
        + lax.dot_general(rows_ref[half:, :], second_ref[...], TN, preferred_element_type=F32)
    ).astype(BF16)


def project_kernel(near_ref, far_ref, weight_ref, out_ref):
    heads = jnp.concatenate([near_ref[0], near_ref[1], far_ref[0], far_ref[1]], axis=1)
    out_ref[...] = jnp.dot(heads, weight_ref[...], preferred_element_type=F32).astype(BF16)


def attended_kernel(parts_ref, out_ref):
    columns = parts_ref.shape[2]
    for t in range(4):
        total = parts_ref[t].astype(F32)
        for i in range(t + 4, parts_ref.shape[0], 4):
            total = total + parts_ref[i].astype(F32)
        start = (2 * (t & 1) + (t >> 1)) * columns
        out_ref[:, start : start + columns] = total.astype(BF16)


def columns_kernel(place_ref, *refs):
    out_ref = refs[-1]
    columns = refs[0].shape[1]
    for k, ref in enumerate(refs[:-1]):
        start = pl.multiple_of((place_ref[0] ^ k) * columns, columns)
        out_ref[:, pl.ds(start, columns)] = ref[...]


def head_norm(projected, gain):
    square_mean = jnp.mean(projected * projected, axis=-1, keepdims=True)
    return (projected * lax.rsqrt(square_mean + 1e-06) * gain).astype(BF16)


def attend_kernel(
    place_ref, merged_ref, embed_ref, norm_ref, qkv_ref, qgain_ref, kgain_ref, out_ref, own_ref,
    kv_ref, q_ref, k_ref, v_ref, *, grp_size, block,
):
    latents, width = embed_ref.shape
    head = q_ref.shape[1]
    total = out_ref.shape[0]
    step = 256
    kv_ref[:, :head] = qkv_ref[1]
    kv_ref[:, head:] = qkv_ref[2]
    pick = (lane_index(16) >= LANES - 2).astype(F32).astype(BF16)
    count_row = lax.dot_general(pick, merged_ref[...], NT, preferred_element_type=F32)[0:1, :]
    bias = jnp.log(count_row)
    ones = jnp.ones((16, width), BF16)
    embed_mean = lax.dot_general(ones, embed_ref[...], NT, preferred_element_type=F32)
    embed_mean = embed_mean[0:1, :] * (1.0 / width)
    embed = jnp.concatenate([embed_ref[...], jnp.ones((LANES - latents, width), BF16)], axis=0)
    lane = lane_index(step)
    for start in range(0, total, step):
        here = slice(start, start + step)
        rows = merged_ref[here, :].astype(F32)
        mean = -jnp.sum(rows[:, :latents] * embed_mean, axis=-1, keepdims=True)
        high = mean.astype(BF16).astype(F32)
        middle = (mean - high).astype(BF16).astype(F32)
        low = mean - high - middle
        tail = jnp.where(lane == latents, high, 0.0)
        tail = jnp.where(lane == latents + 1, middle, tail)
        tail = jnp.where(lane == latents + 2, low, tail)
        factors = jnp.where(lane < latents, rows, tail).astype(BF16)
        center = jnp.dot(factors, embed, preferred_element_type=F32)
        spread = jnp.mean(center * center, axis=-1, keepdims=True)
        normed = (center * lax.rsqrt(spread + 1e-06) * norm_ref[...]).astype(BF16)
        q_part = jnp.dot(normed, qkv_ref[0], preferred_element_type=F32)
        kv_part = jnp.dot(normed, kv_ref[...], preferred_element_type=F32)
        q_ref[here, :] = head_norm(q_part, qgain_ref[...])
        k_ref[here, :] = head_norm(kv_part[:, :head], kgain_ref[...])
        v_ref[here, :] = kv_part[:, head:].astype(BF16)
    scale = 1.0 / math.sqrt(head)
    for start in range(0, total, step):
        here = slice(start, start + step)
        scores = lax.dot_general(
            q_ref[here, :], k_ref[...], NT, preferred_element_type=F32
        ) * scale + bias
        top = jnp.max(scores, axis=-1, keepdims=True)
        weights = jnp.exp(scores - top)
        denominator = jnp.sum(weights, axis=-1, keepdims=True)
        mixed = jnp.dot(weights.astype(BF16), v_ref[...], preferred_element_type=F32)
        out_ref[here, :] = (mixed / denominator).astype(BF16)
    grp = place_ref[0]
    for i in range(total // (block * grp_size)):
        start = pl.multiple_of((i * grp_size + grp) * block, block)
        own_ref[i * block : (i + 1) * block, :] = out_ref[pl.ds(start, block), :]


def call(body, shapes, *args, name, scratch=(), places=(), flops=10**8, moved=10**6):
    spaces = {"smem": pltpu.SMEM, "hbm": pltpu.HBM}
    outs = tuple(jax.ShapeDtypeStruct(shape, BF16) for shape in shapes)
    whole = pl.BlockSpec(memory_space=pltpu.VMEM)
    in_specs = [whole] * len(args)
    for i, place in enumerate(places):
        in_specs[i] = pl.BlockSpec(memory_space=spaces[place])
    result = pl.pallas_call(
        body,
        out_shape=outs,
        in_specs=in_specs,
        out_specs=(whole,) * len(outs),
        scratch_shapes=list(scratch),
        cost_estimate=pl.CostEstimate(flops=flops, bytes_accessed=moved, transcendentals=0),
        compiler_params=pltpu.CompilerParams(vmem_limit_bytes=48 * 2**20),
        name=name,
    )(*args)
    return result[0] if len(outs) == 1 else result


def shards(
    video, conv_weight, latent_weight, assign, embed_weight, norm_gain, qkv_weight, q_gain, k_gain,
    out_weight, cotangent,
):
    grp_size, seq_size, dp_size = (lax.axis_size(a) for a in ("grp", "seq", "dp"))
    owners = grp_size * seq_size
    block, width = cotangent.shape[1:]
    head = q_gain.shape[0]
    groups = block * owners
    columns = width // grp_size
    shared = block * grp_size
    rows = block * seq_size
    grp = lax.axis_index("grp")
    seq = lax.axis_index("seq")
    place = jnp.stack([grp, seq]).astype(jnp.int32)

    frames = video[0]
    frame_count, tokens = frames.shape[:2]
    earlier = shifted_frames(frames[frame_count - 2 :], "seq", 1)
    latent_t = latent_weight.T
    labels = assign[0].reshape(1, -1)
    late, first, taps, latent_rhs = call(
        late_kernel,
        [((frame_count - 2) * tokens, LANES), (2,) + frames.shape[1:], conv_weight.shape,
         latent_t.shape],
        frames, conv_weight, latent_t, name="late_frames", flops=10**9, places=["hbm"] * 3,
        scratch=[pltpu.VMEM(frames.shape, BF16), pltpu.SemaphoreType.DMA((4,))],
    )
    sums = call(
        functools.partial(sums_kernel, grp=grp_size, seq=seq_size), [(groups, LANES)],
        first, earlier, taps, latent_rhs, late, labels, name="group_sums", flops=10**9,
    )

    by_column = jnp.concatenate(
        [cotangent[0, :, g * columns : (g + 1) * columns] for g in range(grp_size)], axis=0
    ).reshape(grp_size, block, columns)
    by_column, _ = lax.optimization_barrier((by_column, earlier))
    near = lax.all_to_all(by_column, "grp", 0, 0, tiled=True).reshape(shared, columns)

    parts = lax.all_to_all(sums.reshape(seq_size, shared, LANES), "seq", 0, 0, tiled=True)
    slab_sums = call(resplit_kernel, [(grp_size, shared, LANES)], parts, name="slab_sums")
    slab_parts = lax.all_to_all(slab_sums, "grp", 0, 0, tiled=True)
    merged = call(merge_kernel, [(seq_size, shared, LANES)], slab_parts, name="merged")
    merged = lax.all_to_all(merged, "seq", 0, 0, tiled=True).reshape(groups, LANES)

    masks = (8, 4, 1, 2)
    for mask in masks[:-1]:
        near = jnp.concatenate([near, xor_swap(near, "seq", mask)], axis=0)
    far = xor_swap(near, "seq", masks[-1])

    side = seq & 1
    depth = (seq >> 1) & 1

    def halved(block, choice, mask):
        size = block.shape[1] // 2
        kept = lax.dynamic_slice_in_dim(block, choice * size, size, 1)
        given = lax.dynamic_slice_in_dim(block, (1 - choice) * size, size, 1)
        return jnp.concatenate([kept, xor_swap(given, "seq", mask)], axis=0)

    weight, _ = lax.optimization_barrier((out_weight, slab_sums))
    weight_pair = halved(weight, side, 1)

    head_out, own_rows = call(
        functools.partial(attend_kernel, grp_size=grp_size, block=block),
        [(groups, head), (rows, head)], place, merged, embed_weight, norm_gain[None],
        qkv_weight, q_gain[None], k_gain[None], name="attend", flops=8 * 10**9, places=["smem"],
        scratch=[pltpu.VMEM((width, 2 * head), BF16)] + [pltpu.VMEM((groups, head), BF16)] * 3,
    )

    other_rows = xor_swap(own_rows, "seq", 1)
    local_grad = call(
        functools.partial(grad_kernel, masks=masks), [(head, columns)], place, head_out, near, far,
        name="local_grad", places=["smem"], scratch=[pltpu.VMEM((groups, head), BF16)],
        flops=10**9,
    )
    pair_heads, weight_pair, _ = lax.optimization_barrier(
        (jnp.stack([own_rows, other_rows]), weight_pair, local_grad)
    )
    quad_heads = (pair_heads, xor_swap(pair_heads, "seq", 2))
    weight_quad = halved(weight_pair, depth, 2)
    grad_parts = lax.all_to_all(
        local_grad.reshape(dp_size, head // dp_size, columns), "dp", 0, 0, tiled=True
    )
    grad_block = call(
        spread_kernel, [(dp_size, head // dp_size, columns)], grad_parts, name="grad_block"
    )
    grad_cols = lax.all_to_all(grad_block, "dp", 0, 0, tiled=True).reshape(head, columns)

    partial = call(
        project_kernel, [(rows, columns)], *quad_heads, weight_quad, name="project", flops=10**9,
    )
    partial, _ = lax.optimization_barrier((partial, grad_cols))
    out_parts = lax.all_to_all(
        partial.reshape(seq_size, block, columns), "seq", 0, 0, tiled=True
    )
    gathered = [grad_cols] + [xor_swap(grad_cols, "grp", k) for k in range(1, grp_size)]
    out_grad = call(
        columns_kernel, [(head, width)], place, *gathered, name="grad_columns", places=["smem"]
    )
    attended = call(attended_kernel, [(block, width)], out_parts, name="attended")
    return (attended[None], out_grad)


def solution(mesh):
    placed = (
        P("dp", "seq", "grp", None), P(), P(), P("dp", "seq", "grp"), P(), P(),
        P(None, None, "seq"), P(), P(), P("seq", None), P("dp", ("grp", "seq"), None),
    )
    return jax.shard_map(
        shards,
        mesh=mesh,
        in_specs=placed,
        out_specs=(P("dp", ("grp", "seq"), None), P("seq", None)),
        check_vma=False,
    )
```

```python
import functools
import math

import jax
import jax.numpy as jnp
from jax import lax
from jax.experimental import pallas as pl
from jax.experimental.pallas import tpu as pltpu
from jax.sharding import PartitionSpec as P

F32 = jnp.float32
BF16 = jnp.bfloat16
LANES = 128
HALF = 64
NT = (((1,), (1,)), ((), ()))
TN = (((0,), (0,)), ((), ()))


def shifted_frames(block, axis, distance):
    devices = range(lax.axis_size(axis))
    route = [(i - distance, i) for i in devices if i - distance in devices]
    return lax.ppermute(block, axis, route)


def xor_swap(block, axis, mask):
    route = [(i, i ^ mask) for i in range(lax.axis_size(axis))]
    return lax.ppermute(block, axis, route)


def lane_index(rows):
    return lax.broadcasted_iota(jnp.int32, (rows, LANES), 1)


def split_pairs(sums):
    lane = lane_index(sums.shape[0])
    high = sums.astype(BF16).astype(F32)
    keep = jnp.logical_or(lane < HALF, lane == LANES - 2)
    return jnp.where(keep, high, sums - high).astype(BF16)


def join_pairs(pairs):
    lane = lane_index(pairs.shape[0])
    total = pairs + jnp.where(lane < HALF - 2, pltpu.roll(pairs, HALF, 1), 0.0)
    counts = pairs[:, LANES - 2 : LANES - 1] + pairs[:, LANES - 1 :]
    return total, counts


def latent_rows(windows, conv_ref, latent_ref):
    channels = conv_ref.shape[1]
    taps = conv_ref[...].reshape(3 * channels, channels)
    weights = jnp.concatenate([latent_ref[...], latent_ref[...]], axis=0)
    latent = None
    for part, views in enumerate(windows):
        cols = slice(part * channels, (part + 1) * channels)
        preact = jnp.dot(jnp.concatenate(views, axis=1), taps, preferred_element_type=F32)
        hidden = (views[0].astype(F32) + preact / (1.0 + jnp.exp(-preact))).astype(BF16)
        term = lax.dot_general(hidden, weights[:, cols], NT, preferred_element_type=F32)
        latent = term if latent is None else latent + term
    return jnp.where(lane_index(latent.shape[0]) < LANES - 2, latent, 1.0).astype(BF16)


def late_kernel(
    video_hbm, conv_hbm, latent_hbm, out_ref, first_ref, conv_ref, latent_ref, video_ref, sems,
):
    copies = [
        pltpu.make_async_copy(src, dst, sems.at[i])
        for i, (src, dst) in enumerate([
            (video_hbm, video_ref), (conv_hbm, conv_ref), (latent_hbm, latent_ref),
            (video_hbm.at[: first_ref.shape[0]], first_ref),
        ])
    ]
    for copy in copies:
        copy.start()
    for copy in copies:
        copy.wait()
    frame_count, tokens, width = video_ref.shape
    channels = conv_ref.shape[1]
    windows = []
    for start in range(0, width, channels):
        cols = slice(start, start + channels)
        windows.append([
            video_ref[2 - k : frame_count - k, :, cols].reshape(-1, channels) for k in range(3)
        ])
    out_ref[...] = latent_rows(windows, conv_ref, latent_ref)


def sums_kernel(
    video_ref, earlier_ref, conv_ref, latent_ref, late_ref, labels_ref, out_ref, *, grp, seq,
):
    channels = conv_ref.shape[1]
    width = video_ref.shape[2]
    windows = []
    for start in range(0, width, channels):
        cols = slice(start, start + channels)
        padded = jnp.concatenate([earlier_ref[:, :, cols], video_ref[:, :, cols]], axis=0)
        windows.append([padded[2 - k : 4 - k].reshape(-1, channels) for k in range(3)])
    first = latent_rows(windows, conv_ref, latent_ref)
    rows = jnp.concatenate([first, late_ref[...]], axis=0)
    labels = labels_ref[...]
    total = out_ref.shape[0]
    block = total // (grp * seq)
    step = 256
    for start in range(0, total, step):
        place = lax.broadcasted_iota(jnp.int32, (step, labels.shape[1]), 0) + start
        inner = place & (block - 1)
        column = (place >> (block.bit_length() - 1)) & (grp - 1)
        slab = place >> ((block * grp).bit_length() - 1)
        member = (labels == (column * seq + slab) * block + inner).astype(F32).astype(BF16)
        out_ref[start : start + step, :] = split_pairs(
            jnp.dot(member, rows, preferred_element_type=F32)
        )


def add_up(parts_ref):
    total = parts_ref[0].astype(F32)
    for i in range(1, parts_ref.shape[0]):
        total = total + parts_ref[i].astype(F32)
    return total


def resplit_kernel(parts_ref, out_ref):
    total, counts = join_pairs(add_up(parts_ref))
    lane = lane_index(total.shape[0])
    doubled = jnp.where(lane < HALF, total, pltpu.roll(total, HALF, 1))
    pairs = split_pairs(jnp.where(lane < LANES - 2, doubled, counts))
    for i in range(out_ref.shape[0]):
        out_ref[i] = pairs


def merge_kernel(parts_ref, out_ref):
    total, counts = join_pairs(add_up(parts_ref))
    lane = lane_index(total.shape[0])
    merged = jnp.where(lane < HALF, total / counts, 0.0)
    high = counts.astype(BF16).astype(F32)
    marks = jnp.where(lane == LANES - 2, high, counts - high)
    rows = jnp.where(lane < LANES - 2, merged, marks).astype(BF16)
    for i in range(out_ref.shape[0]):
        out_ref[i] = rows


def spread_kernel(parts_ref, out_ref):
    total = add_up(parts_ref).astype(BF16)
    for i in range(out_ref.shape[0]):
        out_ref[i] = total


def grad_kernel(place_ref, head_ref, first_ref, second_ref, out_ref, rows_ref, *, masks, part):
    low = (2 << len(masks)) // 2 - 1
    seq = place_ref[1]
    half = first_ref.shape[0]
    put = 0
    for slot in range(1 << len(masks)):
        mask = sum(m for bit, m in enumerate(masks) if slot >> bit & 1)
        for upper in range(rows_ref.shape[0] // (part << len(masks))):
            source = upper * (low + 1) + ((seq ^ mask) & low)
            start = pl.multiple_of(source * part, part)
            rows_ref[put : put + part, :] = head_ref[pl.ds(start, part), :]
            put += part
    out_ref[...] = (
        lax.dot_general(rows_ref[:half, :], first_ref[...], TN, preferred_element_type=F32)
        + lax.dot_general(rows_ref[half:, :], second_ref[...], TN, preferred_element_type=F32)
    ).astype(BF16)


def project_kernel(near_ref, far_ref, weight_ref, out_ref):
    heads = jnp.concatenate([near_ref[0], near_ref[1], far_ref[0], far_ref[1]], axis=1)
    out_ref[...] = jnp.dot(heads, weight_ref[...], preferred_element_type=F32).astype(BF16)


def attended_kernel(parts_ref, out_ref):
    columns = parts_ref.shape[2]
    for t in range(4):
        total = parts_ref[t].astype(F32)
        for i in range(t + 4, parts_ref.shape[0], 4):
            total = total + parts_ref[i].astype(F32)
        start = (2 * (t & 1) + (t >> 1)) * columns
        out_ref[:, start : start + columns] = total.astype(BF16)


def columns_kernel(place_ref, own_ref, other_ref, out_ref, *, pairs):
    rows, columns = own_ref.shape[1:]
    core = place_ref[2]
    for i in range(own_ref.shape[0]):
        cols = slice(i // pairs * columns, (i // pairs + 1) * columns)
        for ref, lane in ((own_ref, core), (other_ref, 1 - core)):
            start = pl.multiple_of((i % pairs * 2 + lane) * rows, rows)
            out_ref[pl.ds(start, rows), cols] = ref[i]


def head_norm(projected, gain):
    square_mean = jnp.mean(projected * projected, axis=-1, keepdims=True)
    return (projected * lax.rsqrt(square_mean + 1e-06) * gain).astype(BF16)


def attend_kernel(
    place_ref, merged_ref, embed_ref, norm_ref, qkv_ref, qgain_ref, kgain_ref, out_ref, own_ref,
    kv_ref, q_ref, k_ref, v_ref, *, grp_size, block,
):
    latents, width = embed_ref.shape
    head = q_ref.shape[1]
    total = out_ref.shape[0]
    step = 256
    kv_ref[:, :head] = qkv_ref[1]
    kv_ref[:, head:] = qkv_ref[2]
    pick = (lane_index(16) >= LANES - 2).astype(F32).astype(BF16)
    count_row = lax.dot_general(pick, merged_ref[...], NT, preferred_element_type=F32)[0:1, :]
    bias = jnp.log(count_row)
    ones = jnp.ones((16, width), BF16)
    embed_mean = lax.dot_general(ones, embed_ref[...], NT, preferred_element_type=F32)
    embed_mean = embed_mean[0:1, :] * (1.0 / width)
    embed = jnp.concatenate([embed_ref[...], jnp.ones((LANES - latents, width), BF16)], axis=0)
    lane = lane_index(step)
    for start in range(0, total, step):
        here = slice(start, start + step)
        rows = merged_ref[here, :].astype(F32)
        mean = -jnp.sum(rows[:, :latents] * embed_mean, axis=-1, keepdims=True)
        high = mean.astype(BF16).astype(F32)
        middle = (mean - high).astype(BF16).astype(F32)
        low = mean - high - middle
        tail = jnp.where(lane == latents, high, 0.0)
        tail = jnp.where(lane == latents + 1, middle, tail)
        tail = jnp.where(lane == latents + 2, low, tail)
        factors = jnp.where(lane < latents, rows, tail).astype(BF16)
        center = jnp.dot(factors, embed, preferred_element_type=F32)
        spread = jnp.mean(center * center, axis=-1, keepdims=True)
        normed = (center * lax.rsqrt(spread + 1e-06) * norm_ref[...]).astype(BF16)
        q_part = jnp.dot(normed, qkv_ref[0], preferred_element_type=F32)
        kv_part = jnp.dot(normed, kv_ref[...], preferred_element_type=F32)
        q_ref[here, :] = head_norm(q_part, qgain_ref[...])
        k_ref[here, :] = head_norm(kv_part[:, :head], kgain_ref[...])
        v_ref[here, :] = kv_part[:, head:].astype(BF16)
    scale = 1.0 / math.sqrt(head)
    for start in range(0, total, step):
        here = slice(start, start + step)
        scores = lax.dot_general(
            q_ref[here, :], k_ref[...], NT, preferred_element_type=F32
        ) * scale + bias
        top = jnp.max(scores, axis=-1, keepdims=True)
        weights = jnp.exp(scores - top)
        denominator = jnp.sum(weights, axis=-1, keepdims=True)
        mixed = jnp.dot(weights.astype(BF16), v_ref[...], preferred_element_type=F32)
        out_ref[here, :] = (mixed / denominator).astype(BF16)
    grp = place_ref[0]
    for i in range(total // (block * grp_size)):
        start = pl.multiple_of((i * grp_size + grp) * block, block)
        own_ref[i * block : (i + 1) * block, :] = out_ref[pl.ds(start, block), :]


def call(body, shapes, *args, name, scratch=(), places=(), flops=10**8, moved=10**6):
    spaces = {"smem": pltpu.SMEM, "hbm": pltpu.HBM}
    outs = tuple(jax.ShapeDtypeStruct(shape, BF16) for shape in shapes)
    whole = pl.BlockSpec(memory_space=pltpu.VMEM)
    in_specs = [whole] * len(args)
    for i, place in enumerate(places):
        in_specs[i] = pl.BlockSpec(memory_space=spaces[place])
    result = pl.pallas_call(
        body,
        out_shape=outs,
        in_specs=in_specs,
        out_specs=(whole,) * len(outs),
        scratch_shapes=list(scratch),
        cost_estimate=pl.CostEstimate(flops=flops, bytes_accessed=moved, transcendentals=0),
        compiler_params=pltpu.CompilerParams(vmem_limit_bytes=48 * 2**20),
        name=name,
    )(*args)
    return result[0] if len(outs) == 1 else result


def shards(
    video, conv_weight, latent_weight, assign, embed_weight, norm_gain, qkv_weight, q_gain, k_gain,
    out_weight, cotangent,
):
    grp_size, seq_size, dp_size = (lax.axis_size(a) for a in ("grp", "seq", "dp"))
    owners = grp_size * seq_size
    block, width = cotangent.shape[1:]
    head = q_gain.shape[0]
    groups = block * owners
    columns = width // grp_size
    shared = block * grp_size
    rows = block * seq_size
    grp = lax.axis_index("grp")
    seq = lax.axis_index("seq")
    place = jnp.stack([grp, seq, lax.axis_index("dp") & 1]).astype(jnp.int32)

    frames = video[0]
    frame_count, tokens = frames.shape[:2]
    earlier = shifted_frames(frames[frame_count - 2 :], "seq", 1)
    latent_t = latent_weight.T
    labels = assign[0].reshape(1, -1)
    late, first, taps, latent_rhs = call(
        late_kernel,
        [((frame_count - 2) * tokens, LANES), (2,) + frames.shape[1:], conv_weight.shape,
         latent_t.shape],
        frames, conv_weight, latent_t, name="late_frames", flops=10**9, places=["hbm"] * 3,
        scratch=[pltpu.VMEM(frames.shape, BF16), pltpu.SemaphoreType.DMA((4,))],
    )
    sums = call(
        functools.partial(sums_kernel, grp=grp_size, seq=seq_size), [(groups, LANES)],
        first, earlier, taps, latent_rhs, late, labels, name="group_sums", flops=10**9,
    )

    by_column = jnp.concatenate(
        [cotangent[0, :, g * columns : (g + 1) * columns] for g in range(grp_size)] * 2, axis=0
    ).reshape(2 * grp_size, block, columns)
    by_column, _ = lax.optimization_barrier((by_column, earlier))
    halves = seq_size // 2
    apart = [
        [g * seq_size + h * halves + r for h in range(2) for g in range(grp_size)]
        for r in range(halves)
    ]
    near = lax.all_to_all(
        by_column, ("grp", "seq"), 0, 0, axis_index_groups=apart, tiled=True
    ).reshape(2 * shared, columns)
    near_other = xor_swap(near, "seq", 4)

    side = seq & 1
    depth = (seq >> 1) & 1

    def halves_of(matrix, choice):
        size = matrix.shape[1] // 2
        return [
            lax.dynamic_slice_in_dim(matrix, c * size, size, 1) for c in (choice, 1 - choice)
        ]

    weight, _ = lax.optimization_barrier((out_weight, sums))
    kept, given = halves_of(weight, side)
    weight_other = xor_swap(given, "seq", 1)

    parts = lax.all_to_all(sums.reshape(seq_size, shared, LANES), "seq", 0, 0, tiled=True)
    slab_sums = call(resplit_kernel, [(grp_size, shared, LANES)], parts, name="slab_sums")
    near_other, weight_other, _ = lax.optimization_barrier((near_other, weight_other, slab_sums))
    near = jnp.concatenate([near, near_other], axis=0)
    near_other = xor_swap(near, "seq", 1)
    slab_parts = lax.all_to_all(slab_sums, "grp", 0, 0, tiled=True)
    merged = call(merge_kernel, [(seq_size, shared, LANES)], slab_parts, name="merged")
    near_other, _ = lax.optimization_barrier((near_other, merged))
    near = jnp.concatenate([near, near_other], axis=0)
    far = xor_swap(near, "seq", 2)
    merged = lax.all_to_all(merged, "seq", 0, 0, tiled=True).reshape(groups, LANES)

    head_out, own_rows = call(
        functools.partial(attend_kernel, grp_size=grp_size, block=block),
        [(groups, head), (rows, head)], place, merged, embed_weight, norm_gain[None],
        qkv_weight, q_gain[None], k_gain[None], name="attend", flops=8 * 10**9, places=["smem"],
        scratch=[pltpu.VMEM((width, 2 * head), BF16)] + [pltpu.VMEM((groups, head), BF16)] * 3,
    )

    other_rows = xor_swap(own_rows, "seq", 1)
    local_grad = call(
        functools.partial(grad_kernel, masks=(4, 1, 2), part=shared), [(head, columns)], place,
        head_out, near, far, name="local_grad", places=["smem"],
        scratch=[pltpu.VMEM((groups, head), BF16)], flops=10**9,
    )
    grad_parts = lax.all_to_all(
        local_grad.reshape(dp_size, head // dp_size, columns), "dp", 0, 0, tiled=True
    )
    other_rows, weight_other, _ = lax.optimization_barrier((other_rows, weight_other, local_grad))
    pair_heads = jnp.stack([own_rows, other_rows])
    quad_heads = (pair_heads, xor_swap(pair_heads, "seq", 2))
    kept, given = halves_of(jnp.concatenate([kept, weight_other], axis=0), depth)
    weight_quad = jnp.concatenate([kept, xor_swap(given, "seq", 2)], axis=0)

    pairs = dp_size // 2
    grad_block = call(
        spread_kernel, [(grp_size * pairs, head // dp_size, columns)], grad_parts,
        name="grad_block",
    )
    same_core = [
        [g * dp_size + 2 * p + c for g in range(grp_size) for p in range(pairs)] for c in range(2)
    ]
    grad_cols = lax.all_to_all(
        grad_block, ("grp", "dp"), 0, 0, axis_index_groups=same_core, tiled=True
    )
    partial = call(
        project_kernel, [(rows, columns)], *quad_heads, weight_quad, name="project", flops=10**9,
    )
    partial, _ = lax.optimization_barrier((partial, grad_cols))
    out_parts = lax.all_to_all(
        partial.reshape(seq_size, block, columns), "seq", 0, 0, tiled=True
    )
    out_grad = call(
        functools.partial(columns_kernel, pairs=pairs), [(head, width)], place, grad_cols,
        xor_swap(grad_cols, "dp", 1), name="grad_columns", places=["smem"],
    )
    attended = call(attended_kernel, [(block, width)], out_parts, name="attended")
    return (attended[None], out_grad)


def solution(mesh):
    placed = (
        P("dp", "seq", "grp", None), P(), P(), P("dp", "seq", "grp"), P(), P(),
        P(None, None, "seq"), P(), P(), P("seq", None), P("dp", ("grp", "seq"), None),
    )
    return jax.shard_map(
        shards,
        mesh=mesh,
        in_specs=placed,
        out_specs=(P("dp", ("grp", "seq"), None), P("seq", None)),
        check_vma=False,
    )
```

```python
import functools
import math

import jax
import jax.numpy as jnp
from jax import lax
from jax.experimental import pallas as pl
from jax.experimental.pallas import tpu as pltpu
from jax.sharding import PartitionSpec as P

F32 = jnp.float32
BF16 = jnp.bfloat16
LANES = 128
HALF = 64
NT = (((1,), (1,)), ((), ()))
TN = (((0,), (0,)), ((), ()))


def shifted_frames(block, axis, distance):
    devices = range(lax.axis_size(axis))
    route = [(i - distance, i) for i in devices if i - distance in devices]
    return lax.ppermute(block, axis, route)


def xor_swap(block, axis, mask):
    route = [(i, i ^ mask) for i in range(lax.axis_size(axis))]
    return lax.ppermute(block, axis, route)


def lane_index(rows):
    return lax.broadcasted_iota(jnp.int32, (rows, LANES), 1)


def split_pairs(sums):
    lane = lane_index(sums.shape[0])
    high = sums.astype(BF16).astype(F32)
    keep = jnp.logical_or(lane < HALF, lane == LANES - 2)
    return jnp.where(keep, high, sums - high).astype(BF16)


def join_pairs(pairs):
    lane = lane_index(pairs.shape[0])
    total = pairs + jnp.where(lane < HALF - 2, pltpu.roll(pairs, HALF, 1), 0.0)
    counts = pairs[:, LANES - 2 : LANES - 1] + pairs[:, LANES - 1 :]
    return total, counts


def latent_rows(windows, conv_ref, latent_ref):
    channels = conv_ref.shape[1]
    taps = conv_ref[...].reshape(3 * channels, channels)
    weights = jnp.concatenate([latent_ref[...], latent_ref[...]], axis=0)
    latent = None
    for part, views in enumerate(windows):
        cols = slice(part * channels, (part + 1) * channels)
        preact = jnp.dot(jnp.concatenate(views, axis=1), taps, preferred_element_type=F32)
        hidden = (views[0].astype(F32) + preact / (1.0 + jnp.exp(-preact))).astype(BF16)
        term = lax.dot_general(hidden, weights[:, cols], NT, preferred_element_type=F32)
        latent = term if latent is None else latent + term
    return jnp.where(lane_index(latent.shape[0]) < LANES - 2, latent, 1.0).astype(BF16)


def late_kernel(
    video_hbm, conv_hbm, latent_hbm, out_ref, first_ref, conv_ref, latent_ref, video_ref, sems,
):
    copies = [
        pltpu.make_async_copy(src, dst, sems.at[i])
        for i, (src, dst) in enumerate([
            (video_hbm, video_ref), (conv_hbm, conv_ref), (latent_hbm, latent_ref),
            (video_hbm.at[: first_ref.shape[0]], first_ref),
        ])
    ]
    for copy in copies:
        copy.start()
    for copy in copies:
        copy.wait()
    frame_count, tokens, width = video_ref.shape
    channels = conv_ref.shape[1]
    windows = []
    for start in range(0, width, channels):
        cols = slice(start, start + channels)
        windows.append([
            video_ref[2 - k : frame_count - k, :, cols].reshape(-1, channels) for k in range(3)
        ])
    out_ref[...] = latent_rows(windows, conv_ref, latent_ref)


def sums_kernel(
    video_ref, earlier_ref, conv_ref, latent_ref, late_ref, labels_ref, out_ref, *, grp, seq,
):
    channels = conv_ref.shape[1]
    width = video_ref.shape[2]
    windows = []
    for start in range(0, width, channels):
        cols = slice(start, start + channels)
        padded = jnp.concatenate([earlier_ref[:, :, cols], video_ref[:, :, cols]], axis=0)
        windows.append([padded[2 - k : 4 - k].reshape(-1, channels) for k in range(3)])
    first = latent_rows(windows, conv_ref, latent_ref)
    rows = jnp.concatenate([first, late_ref[...]], axis=0)
    labels = labels_ref[...]
    total = out_ref.shape[0]
    block = total // (grp * seq)
    step = 256
    for start in range(0, total, step):
        place = lax.broadcasted_iota(jnp.int32, (step, labels.shape[1]), 0) + start
        inner = place & (block - 1)
        column = (place >> (block.bit_length() - 1)) & (grp - 1)
        slab = place >> ((block * grp).bit_length() - 1)
        member = (labels == (column * seq + slab) * block + inner).astype(F32).astype(BF16)
        out_ref[start : start + step, :] = split_pairs(
            jnp.dot(member, rows, preferred_element_type=F32)
        )


def add_up(parts_ref):
    total = parts_ref[0].astype(F32)
    for i in range(1, parts_ref.shape[0]):
        total = total + parts_ref[i].astype(F32)
    return total


def resplit_kernel(parts_ref, out_ref):
    total, counts = join_pairs(add_up(parts_ref))
    lane = lane_index(total.shape[0])
    doubled = jnp.where(lane < HALF, total, pltpu.roll(total, HALF, 1))
    pairs = split_pairs(jnp.where(lane < LANES - 2, doubled, counts))
    for i in range(out_ref.shape[0]):
        out_ref[i] = pairs


def merge_kernel(parts_ref, out_ref):
    total, counts = join_pairs(add_up(parts_ref))
    lane = lane_index(total.shape[0])
    merged = jnp.where(lane < HALF, total / counts, 0.0)
    high = counts.astype(BF16).astype(F32)
    marks = jnp.where(lane == LANES - 2, high, counts - high)
    rows = jnp.where(lane < LANES - 2, merged, marks).astype(BF16)
    for i in range(out_ref.shape[0]):
        out_ref[i] = rows


def spread_kernel(parts_ref, out_ref):
    total = add_up(parts_ref).astype(BF16)
    for i in range(out_ref.shape[0]):
        out_ref[i] = total


def split_kernel(rows_ref, out_ref):
    columns = out_ref.shape[2]
    for i in range(out_ref.shape[0]):
        out_ref[i] = rows_ref[:, i * columns : (i + 1) * columns]


def grad_kernel(
    place_ref, head_ref, given_ref, first_ref, second_ref, out_ref, rows_ref, *, masks, part,
):
    seq = place_ref[1]
    head = head_ref.shape[1]
    half = first_ref.shape[0]
    for slot in range(1 << len(masks)):
        mask = sum(m for bit, m in enumerate(masks) if slot >> bit & 1)
        source = seq ^ mask
        start = pl.multiple_of(source * part, part)
        given = pl.multiple_of((source >> 1) * part, part)
        here = slice(slot * part, (slot + 1) * part)
        rows_ref[here, :head] = head_ref[pl.ds(start, part), :]
        rows_ref[here, head:] = given_ref[pl.ds(given, part), :]
    total = (
        lax.dot_general(rows_ref[:half, :], first_ref[...], TN, preferred_element_type=F32)
        + lax.dot_general(rows_ref[half:, :], second_ref[...], TN, preferred_element_type=F32)
    ).astype(BF16)
    side = seq & 1
    out_ref[side] = total[:head, :]
    out_ref[1 - side] = total[head:, :]


def pair_kernel(place_ref, own_ref, given_ref, out_ref, *, part):
    grp = place_ref[0]
    side = place_ref[1] & 1
    rows = own_ref.shape[0]
    slabs = (given_ref.shape[0] - rows // 2) // part
    block = rows // (2 * slabs)
    out_ref[0] = own_ref[...]
    for i in range(slabs):
        near = pl.multiple_of((2 * i + side) * block, block)
        far = pl.multiple_of((2 * i + 1 - side) * block, block)
        start = pl.multiple_of(i * part + grp * block, block)
        out_ref[1, pl.ds(near, block), :] = given_ref[pl.ds(start, block), :]
        first = slabs * part + i * block
        out_ref[1, pl.ds(far, block), :] = given_ref[first : first + block, :]


def weights_kernel(place_ref, weight_ref, partner_ref, kept_ref, given_ref):
    columns = kept_ref.shape[1]
    size = weight_ref.shape[0]
    side = place_ref[1] & 1
    depth = (place_ref[1] >> 1) & 1
    for i, (ref, first) in enumerate([(weight_ref, 2 * side), (partner_ref, 0)]):
        keep = pl.multiple_of((first + depth) * columns, columns)
        give = pl.multiple_of((first + 1 - depth) * columns, columns)
        kept_ref[i * size : (i + 1) * size, :] = ref[:, pl.ds(keep, columns)]
        given_ref[i * size : (i + 1) * size, :] = ref[:, pl.ds(give, columns)]


def project_kernel(place_ref, near_ref, far_ref, near_weight_ref, far_weight_ref, *refs):
    out_refs, sum_ref = refs[:4], refs[4]
    near = jnp.concatenate([near_ref[0], near_ref[1]], axis=1)
    far = jnp.concatenate([far_ref[0], far_ref[1]], axis=1)
    sum_ref[...] = (
        jnp.dot(near, near_weight_ref[...], preferred_element_type=F32)
        + jnp.dot(far, far_weight_ref[...], preferred_element_type=F32)
    ).astype(BF16)
    part = sum_ref.shape[0] // 4
    for k, ref in enumerate(out_refs):
        start = pl.multiple_of(((place_ref[1] >> 2) ^ k) * part, part)
        ref[...] = sum_ref[pl.ds(start, part), :]


def total_kernel(*refs):
    total = refs[0][...].astype(F32)
    for ref in refs[1:-1]:
        total = total + ref[...].astype(F32)
    refs[-1][...] = total.astype(BF16)


def attended_kernel(parts_ref, out_ref):
    columns = parts_ref.shape[2]
    for t in range(parts_ref.shape[0]):
        start = (2 * (t & 1) + (t >> 1)) * columns
        out_ref[:, start : start + columns] = parts_ref[t]


def columns_kernel(place_ref, own_ref, other_ref, out_ref, *, pairs):
    rows, columns = own_ref.shape[1:]
    core = place_ref[2]
    for i in range(own_ref.shape[0]):
        cols = slice(i // pairs * columns, (i // pairs + 1) * columns)
        for ref, lane in ((own_ref, core), (other_ref, 1 - core)):
            start = pl.multiple_of((i % pairs * 2 + lane) * rows, rows)
            out_ref[pl.ds(start, rows), cols] = ref[i]


def head_norm(projected, gain):
    square_mean = jnp.mean(projected * projected, axis=-1, keepdims=True)
    return (projected * lax.rsqrt(square_mean + 1e-06) * gain).astype(BF16)


def attend_kernel(
    place_ref, merged_ref, embed_ref, norm_ref, qkv_ref, qgain_ref, kgain_ref, out_ref, own_ref,
    give_ref,    kv_ref, q_ref, k_ref, v_ref, *, grp_size, block,
):
    latents, width = embed_ref.shape
    head = q_ref.shape[1]
    total = out_ref.shape[0]
    step = 256
    kv_ref[:, :head] = qkv_ref[1]
    kv_ref[:, head:] = qkv_ref[2]
    pick = (lane_index(16) >= LANES - 2).astype(F32).astype(BF16)
    count_row = lax.dot_general(pick, merged_ref[...], NT, preferred_element_type=F32)[0:1, :]
    bias = jnp.log(count_row)
    ones = jnp.ones((16, width), BF16)
    embed_mean = lax.dot_general(ones, embed_ref[...], NT, preferred_element_type=F32)
    embed_mean = embed_mean[0:1, :] * (1.0 / width)
    embed = jnp.concatenate([embed_ref[...], jnp.ones((LANES - latents, width), BF16)], axis=0)
    lane = lane_index(step)
    for start in range(0, total, step):
        here = slice(start, start + step)
        rows = merged_ref[here, :].astype(F32)
        mean = -jnp.sum(rows[:, :latents] * embed_mean, axis=-1, keepdims=True)
        high = mean.astype(BF16).astype(F32)
        middle = (mean - high).astype(BF16).astype(F32)
        low = mean - high - middle
        tail = jnp.where(lane == latents, high, 0.0)
        tail = jnp.where(lane == latents + 1, middle, tail)
        tail = jnp.where(lane == latents + 2, low, tail)
        factors = jnp.where(lane < latents, rows, tail).astype(BF16)
        center = jnp.dot(factors, embed, preferred_element_type=F32)
        spread = jnp.mean(center * center, axis=-1, keepdims=True)
        normed = (center * lax.rsqrt(spread + 1e-06) * norm_ref[...]).astype(BF16)
        q_part = jnp.dot(normed, qkv_ref[0], preferred_element_type=F32)
        kv_part = jnp.dot(normed, kv_ref[...], preferred_element_type=F32)
        q_ref[here, :] = head_norm(q_part, qgain_ref[...])
        k_ref[here, :] = head_norm(kv_part[:, :head], kgain_ref[...])
        v_ref[here, :] = kv_part[:, head:].astype(BF16)
    scale = 1.0 / math.sqrt(head)
    for start in range(0, total, step):
        here = slice(start, start + step)
        scores = lax.dot_general(
            q_ref[here, :], k_ref[...], NT, preferred_element_type=F32
        ) * scale + bias
        top = jnp.max(scores, axis=-1, keepdims=True)
        weights = jnp.exp(scores - top)
        denominator = jnp.sum(weights, axis=-1, keepdims=True)
        mixed = jnp.dot(weights.astype(BF16), v_ref[...], preferred_element_type=F32)
        out_ref[here, :] = (mixed / denominator).astype(BF16)
    grp = place_ref[0]
    side = place_ref[1] & 1
    part = block * grp_size
    slabs = total // (2 * part)
    for i in range(2 * slabs):
        start = pl.multiple_of(i * part + grp * block, block)
        own_ref[i * block : (i + 1) * block, :] = out_ref[pl.ds(start, block), :]
    for i in range(slabs):
        start = pl.multiple_of((2 * i + 1 - side) * part, part)
        give_ref[i * part : (i + 1) * part, :] = out_ref[pl.ds(start, part), :]
        start = pl.multiple_of((2 * i + side) * part + grp * block, block)
        first = slabs * part + i * block
        give_ref[first : first + block, :] = out_ref[pl.ds(start, block), :]


def call(body, shapes, *args, name, scratch=(), places=(), flops=10**8, moved=10**6):
    spaces = {"smem": pltpu.SMEM, "hbm": pltpu.HBM}
    outs = tuple(jax.ShapeDtypeStruct(shape, BF16) for shape in shapes)
    whole = pl.BlockSpec(memory_space=pltpu.VMEM)
    in_specs = [whole] * len(args)
    for i, place in enumerate(places):
        in_specs[i] = pl.BlockSpec(memory_space=spaces[place])
    result = pl.pallas_call(
        body,
        out_shape=outs,
        in_specs=in_specs,
        out_specs=(whole,) * len(outs),
        scratch_shapes=list(scratch),
        cost_estimate=pl.CostEstimate(flops=flops, bytes_accessed=moved, transcendentals=0),
        compiler_params=pltpu.CompilerParams(vmem_limit_bytes=48 * 2**20),
        name=name,
    )(*args)
    return result[0] if len(outs) == 1 else result


def shards(
    video, conv_weight, latent_weight, assign, embed_weight, norm_gain, qkv_weight, q_gain, k_gain,
    out_weight, cotangent,
):
    grp_size, seq_size, dp_size = (lax.axis_size(a) for a in ("grp", "seq", "dp"))
    owners = grp_size * seq_size
    block, width = cotangent.shape[1:]
    head = q_gain.shape[0]
    groups = block * owners
    columns = width // grp_size
    shared = block * grp_size
    rows = block * seq_size
    grp = lax.axis_index("grp")
    seq = lax.axis_index("seq")
    place = jnp.stack([grp, seq, lax.axis_index("dp") & 1]).astype(jnp.int32)

    frames = video[0]
    frame_count, tokens = frames.shape[:2]
    earlier = shifted_frames(frames[frame_count - 2 :], "seq", 1)
    latent_t = latent_weight.T
    labels = assign[0].reshape(1, -1)
    late, first, taps, latent_rhs = call(
        late_kernel,
        [((frame_count - 2) * tokens, LANES), (2,) + frames.shape[1:], conv_weight.shape,
         latent_t.shape],
        frames, conv_weight, latent_t, name="late_frames", flops=10**9, places=["hbm"] * 3,
        scratch=[pltpu.VMEM(frames.shape, BF16), pltpu.SemaphoreType.DMA((4,))],
    )
    sums = call(
        functools.partial(sums_kernel, grp=grp_size, seq=seq_size), [(groups, LANES)],
        first, earlier, taps, latent_rhs, late, labels, name="group_sums", flops=10**9,
    )

    by_column = call(
        split_kernel, [(grp_size, block, columns)], cotangent[0], name="split_columns"
    )
    near = lax.all_to_all(by_column, "grp", 0, 0, tiled=True).reshape(shared, columns)
    near, _ = lax.optimization_barrier((near, sums))
    near_other = xor_swap(near, "seq", 8)

    parts = lax.all_to_all(sums.reshape(seq_size, shared, LANES), "seq", 0, 0, tiled=True)
    slab_sums = call(resplit_kernel, [(grp_size, shared, LANES)], parts, name="slab_sums")
    near_other, _ = lax.optimization_barrier((near_other, slab_sums))
    near = jnp.concatenate([near, near_other], axis=0)
    near_other = xor_swap(near, "seq", 4)
    slab_parts = lax.all_to_all(slab_sums, "grp", 0, 0, tiled=True)
    merged = call(merge_kernel, [(seq_size, shared, LANES)], slab_parts, name="merged")
    near_other, _ = lax.optimization_barrier((near_other, merged))
    near = jnp.concatenate([near, near_other], axis=0)
    far = xor_swap(near, "seq", 2)
    weight, _ = lax.optimization_barrier((out_weight, merged))
    given = lax.dynamic_slice_in_dim(weight, (1 - (seq & 1)) * (width // 2), width // 2, 1)
    weight_other = xor_swap(given, "seq", 1)
    merged = lax.all_to_all(merged, "seq", 0, 0, tiled=True).reshape(groups, LANES)

    head_out, own_rows, given_rows = call(
        functools.partial(attend_kernel, grp_size=grp_size, block=block),
        [(groups, head), (rows, head), (groups // 2 + rows // 2, head)], place, merged,
        embed_weight, norm_gain[None], qkv_weight, q_gain[None], k_gain[None], name="attend",
        flops=8 * 10**9, places=["smem"],
        scratch=[pltpu.VMEM((width, 2 * head), BF16)] + [pltpu.VMEM((groups, head), BF16)] * 3,
    )

    side_rows = xor_swap(given_rows, "seq", 1)
    weight_other, _ = lax.optimization_barrier((weight_other, own_rows))
    near_weight, given = call(
        weights_kernel, [(2 * head, columns)] * 2, place, out_weight, weight_other,
        name="weights", places=["smem"],
    )
    far_weight = xor_swap(given, "seq", 2)
    local_grad = call(
        functools.partial(grad_kernel, masks=(8, 4, 2), part=shared), [(2, head, columns)],
        place, head_out, side_rows, near, far, name="local_grad", places=["smem"],
        scratch=[pltpu.VMEM((groups // 2, 2 * head), BF16)], flops=10**9,
    )
    both_sides = [
        [(2 * z + y) * dp_size + d for y in range(2) for d in range(dp_size)]
        for z in range(seq_size // 2)
    ]
    grad_parts = lax.all_to_all(
        local_grad.reshape(2 * dp_size, head // dp_size, columns), ("seq", "dp"), 0, 0,
        axis_index_groups=both_sides, tiled=True,
    )
    pair_heads = call(
        functools.partial(pair_kernel, part=shared), [(2, rows, head)], place, own_rows,
        side_rows, name="pair_heads", places=["smem"],
    )
    far_heads = xor_swap(pair_heads, "seq", 2)

    pairs = dp_size // 2
    grad_block = call(
        spread_kernel, [(grp_size * pairs, head // dp_size, columns)], grad_parts,
        name="grad_block",
    )
    same_core = [
        [g * dp_size + 2 * p + c for g in range(grp_size) for p in range(pairs)] for c in range(2)
    ]
    grad_cols = lax.all_to_all(
        grad_block, ("grp", "dp"), 0, 0, axis_index_groups=same_core, tiled=True
    )
    partials = call(
        project_kernel, [(rows // 4, columns)] * 4, place, pair_heads, far_heads, near_weight,
        far_weight, name="project", flops=10**9, places=["smem"],
        scratch=[pltpu.VMEM((rows, columns), BF16)],
    )
    partials = [partials[0]] + [xor_swap(partials[k], "seq", 4 * k) for k in range(1, 4)]
    projected = call(total_kernel, [(rows // 4, columns)], *partials, name="projected")
    projected, _ = lax.optimization_barrier((projected, grad_cols))
    quads = [list(range(k, k + 4)) for k in range(0, seq_size, 4)]
    out_parts = lax.all_to_all(
        projected.reshape(4, block, columns), "seq", 0, 0, axis_index_groups=quads, tiled=True
    )
    out_grad = call(
        functools.partial(columns_kernel, pairs=pairs), [(head, width)], place, grad_cols,
        xor_swap(grad_cols, "dp", 1), name="grad_columns", places=["smem"],
    )
    attended = call(attended_kernel, [(block, width)], out_parts, name="attended")
    return (attended[None], out_grad)


def solution(mesh):
    placed = (
        P("dp", "seq", "grp", None), P(), P(), P("dp", "seq", "grp"), P(), P(),
        P(None, None, "seq"), P(), P(), P("seq", None), P("dp", ("grp", "seq"), None),
    )
    return jax.shard_map(
        shards,
        mesh=mesh,
        in_specs=placed,
        out_specs=(P("dp", ("grp", "seq"), None), P("seq", None)),
        check_vma=False,
    )
```

```python
import functools
import math

import jax
import jax.numpy as jnp
from jax import lax
from jax.experimental import pallas as pl
from jax.experimental.pallas import tpu as pltpu
from jax.sharding import PartitionSpec as P

F32 = jnp.float32
BF16 = jnp.bfloat16
LANES = 128
HALF = 64
NT = (((1,), (1,)), ((), ()))
TN = (((0,), (0,)), ((), ()))


def shifted_frames(block, axis, distance):
    devices = range(lax.axis_size(axis))
    route = [(i - distance, i) for i in devices if i - distance in devices]
    return lax.ppermute(block, axis, route)


def xor_swap(block, axis, mask):
    route = [(i, i ^ mask) for i in range(lax.axis_size(axis))]
    return lax.ppermute(block, axis, route)


def lane_index(rows):
    return lax.broadcasted_iota(jnp.int32, (rows, LANES), 1)


def split_pairs(sums):
    lane = lane_index(sums.shape[0])
    high = sums.astype(BF16).astype(F32)
    keep = jnp.logical_or(lane < HALF, lane == LANES - 2)
    return jnp.where(keep, high, sums - high).astype(BF16)


def join_pairs(pairs):
    lane = lane_index(pairs.shape[0])
    total = pairs + jnp.where(lane < HALF - 2, pltpu.roll(pairs, HALF, 1), 0.0)
    counts = pairs[:, LANES - 2 : LANES - 1] + pairs[:, LANES - 1 :]
    return total, counts


def latent_rows(windows, conv_ref, latent_ref):
    channels = conv_ref.shape[1]
    taps = conv_ref[...].reshape(3 * channels, channels)
    weights = jnp.concatenate([latent_ref[...], latent_ref[...]], axis=0)
    latent = None
    for part, views in enumerate(windows):
        cols = slice(part * channels, (part + 1) * channels)
        preact = jnp.dot(jnp.concatenate(views, axis=1), taps, preferred_element_type=F32)
        hidden = (views[0].astype(F32) + preact / (1.0 + jnp.exp(-preact))).astype(BF16)
        term = lax.dot_general(hidden, weights[:, cols], NT, preferred_element_type=F32)
        latent = term if latent is None else latent + term
    return jnp.where(lane_index(latent.shape[0]) < LANES - 2, latent, 1.0).astype(BF16)


def late_kernel(
    video_hbm, conv_hbm, latent_hbm, out_ref, first_ref, conv_ref, latent_ref, video_ref, sems,
):
    copies = [
        pltpu.make_async_copy(src, dst, sems.at[i])
        for i, (src, dst) in enumerate([
            (video_hbm, video_ref), (conv_hbm, conv_ref), (latent_hbm, latent_ref),
            (video_hbm.at[: first_ref.shape[0]], first_ref),
        ])
    ]
    for copy in copies:
        copy.start()
    for copy in copies:
        copy.wait()
    frame_count, tokens, width = video_ref.shape
    channels = conv_ref.shape[1]
    windows = []
    for start in range(0, width, channels):
        cols = slice(start, start + channels)
        windows.append([
            video_ref[2 - k : frame_count - k, :, cols].reshape(-1, channels) for k in range(3)
        ])
    out_ref[...] = latent_rows(windows, conv_ref, latent_ref)


def sums_kernel(
    video_ref, earlier_ref, conv_ref, latent_ref, late_ref, labels_ref, out_ref, *, grp, seq,
):
    channels = conv_ref.shape[1]
    width = video_ref.shape[2]
    windows = []
    for start in range(0, width, channels):
        cols = slice(start, start + channels)
        padded = jnp.concatenate([earlier_ref[:, :, cols], video_ref[:, :, cols]], axis=0)
        windows.append([padded[2 - k : 4 - k].reshape(-1, channels) for k in range(3)])
    first = latent_rows(windows, conv_ref, latent_ref)
    rows = jnp.concatenate([first, late_ref[...]], axis=0)
    labels = jnp.concatenate(
        [labels_ref[i : i + 1, :] for i in range(labels_ref.shape[0])], axis=1
    )
    total = out_ref.shape[0]
    block = total // (grp * seq)
    step = 256
    for start in range(0, total, step):
        place = lax.broadcasted_iota(jnp.int32, (step, labels.shape[1]), 0) + start
        inner = place & (block - 1)
        column = (place >> (block.bit_length() - 1)) & (grp - 1)
        slab = place >> ((block * grp).bit_length() - 1)
        member = (labels == (column * seq + slab) * block + inner).astype(F32).astype(BF16)
        out_ref[start : start + step, :] = split_pairs(
            jnp.dot(member, rows, preferred_element_type=F32)
        )


def add_up(parts_ref):
    total = parts_ref[0].astype(F32)
    for i in range(1, parts_ref.shape[0]):
        total = total + parts_ref[i].astype(F32)
    return total


def resplit_kernel(parts_ref, out_ref):
    total, counts = join_pairs(add_up(parts_ref))
    lane = lane_index(total.shape[0])
    doubled = jnp.where(lane < HALF, total, pltpu.roll(total, HALF, 1))
    pairs = split_pairs(jnp.where(lane < LANES - 2, doubled, counts))
    for i in range(out_ref.shape[0]):
        out_ref[i] = pairs


def merge_kernel(parts_ref, out_ref):
    total, counts = join_pairs(add_up(parts_ref))
    lane = lane_index(total.shape[0])
    merged = jnp.where(lane < HALF, total / counts, 0.0)
    high = counts.astype(BF16).astype(F32)
    marks = jnp.where(lane == LANES - 2, high, counts - high)
    rows = jnp.where(lane < LANES - 2, merged, marks).astype(BF16)
    for i in range(out_ref.shape[0]):
        out_ref[i] = rows


def spread_kernel(parts_ref, out_ref):
    total = add_up(parts_ref).astype(BF16)
    for i in range(out_ref.shape[0]):
        out_ref[i] = total


def split_kernel(rows_ref, out_ref):
    columns = out_ref.shape[2]
    for i in range(out_ref.shape[0]):
        out_ref[i] = rows_ref[:, i * columns : (i + 1) * columns]


def grad_kernel(
    place_ref, head_ref, given_ref, first_ref, second_ref, out_ref, rows_ref, *, masks, part,
):
    seq = place_ref[1]
    head = head_ref.shape[1]
    half = first_ref.shape[0]
    for slot in range(1 << len(masks)):
        mask = sum(m for bit, m in enumerate(masks) if slot >> bit & 1)
        source = seq ^ mask
        start = pl.multiple_of(source * part, part)
        given = pl.multiple_of((source >> 1) * part, part)
        here = slice(slot * part, (slot + 1) * part)
        rows_ref[here, :head] = head_ref[pl.ds(start, part), :]
        rows_ref[here, head:] = given_ref[pl.ds(given, part), :]
    total = (
        lax.dot_general(rows_ref[:half, :], first_ref[...], TN, preferred_element_type=F32)
        + lax.dot_general(rows_ref[half:, :], second_ref[...], TN, preferred_element_type=F32)
    ).astype(BF16)
    side = seq & 1
    out_ref[side] = total[:head, :]
    out_ref[1 - side] = total[head:, :]


def pair_kernel(place_ref, own_ref, given_ref, out_ref, *, part):
    grp = place_ref[0]
    side = place_ref[1] & 1
    rows = own_ref.shape[0]
    slabs = (given_ref.shape[0] - rows // 2) // part
    block = rows // (2 * slabs)
    out_ref[0] = own_ref[...]
    for i in range(slabs):
        near = pl.multiple_of((2 * i + side) * block, block)
        far = pl.multiple_of((2 * i + 1 - side) * block, block)
        start = pl.multiple_of(i * part + grp * block, block)
        out_ref[1, pl.ds(near, block), :] = given_ref[pl.ds(start, block), :]
        first = slabs * part + i * block
        out_ref[1, pl.ds(far, block), :] = given_ref[first : first + block, :]


def weights_kernel(place_ref, weight_ref, partner_ref, kept_ref, given_ref):
    columns = kept_ref.shape[1]
    size = weight_ref.shape[0]
    side = place_ref[1] & 1
    depth = (place_ref[1] >> 1) & 1
    for i, (ref, first) in enumerate([(weight_ref, 2 * side), (partner_ref, 0)]):
        keep = pl.multiple_of((first + depth) * columns, columns)
        give = pl.multiple_of((first + 1 - depth) * columns, columns)
        kept_ref[i * size : (i + 1) * size, :] = ref[:, pl.ds(keep, columns)]
        given_ref[i * size : (i + 1) * size, :] = ref[:, pl.ds(give, columns)]


def project_kernel(place_ref, near_ref, far_ref, near_weight_ref, far_weight_ref, *refs):
    out_refs, sum_ref = refs[:4], refs[4]
    near = jnp.concatenate([near_ref[0], near_ref[1]], axis=1)
    far = jnp.concatenate([far_ref[0], far_ref[1]], axis=1)
    sum_ref[...] = (
        jnp.dot(near, near_weight_ref[...], preferred_element_type=F32)
        + jnp.dot(far, far_weight_ref[...], preferred_element_type=F32)
    ).astype(BF16)
    part = sum_ref.shape[0] // 4
    for k, ref in enumerate(out_refs):
        start = pl.multiple_of(((place_ref[1] >> 2) ^ k) * part, part)
        ref[...] = sum_ref[pl.ds(start, part), :]


def total_kernel(*refs):
    total = refs[0][...].astype(F32)
    for ref in refs[1:-1]:
        total = total + ref[...].astype(F32)
    refs[-1][...] = total.astype(BF16)


def attended_kernel(parts_ref, out_ref):
    columns = parts_ref.shape[2]
    for t in range(parts_ref.shape[0]):
        start = (2 * (t & 1) + (t >> 1)) * columns
        out_ref[:, start : start + columns] = parts_ref[t]


def columns_kernel(place_ref, own_ref, other_ref, out_ref, *, pairs):
    rows, columns = own_ref.shape[1:]
    core = place_ref[2]
    for i in range(own_ref.shape[0]):
        cols = slice(i // pairs * columns, (i // pairs + 1) * columns)
        for ref, lane in ((own_ref, core), (other_ref, 1 - core)):
            start = pl.multiple_of((i % pairs * 2 + lane) * rows, rows)
            out_ref[pl.ds(start, rows), cols] = ref[i]


def head_norm(projected, gain):
    square_mean = jnp.mean(projected * projected, axis=-1, keepdims=True)
    return (projected * lax.rsqrt(square_mean + 1e-06) * gain).astype(BF16)


def attend_kernel(
    place_ref, merged_ref, embed_ref, norm_ref, qkv_ref, qgain_ref, kgain_ref, out_ref, own_ref,
    give_ref,    kv_ref, q_ref, k_ref, v_ref, *, grp_size, block,
):
    latents, width = embed_ref.shape
    head = q_ref.shape[1]
    total = out_ref.shape[0]
    step = 256
    kv_ref[:, :head] = qkv_ref[1]
    kv_ref[:, head:] = qkv_ref[2]
    pick = (lane_index(16) >= LANES - 2).astype(F32).astype(BF16)
    count_row = lax.dot_general(pick, merged_ref[...], NT, preferred_element_type=F32)[0:1, :]
    bias = jnp.log(count_row)
    ones = jnp.ones((16, width), BF16)
    embed_mean = lax.dot_general(ones, embed_ref[...], NT, preferred_element_type=F32)
    embed_mean = embed_mean[0:1, :] * (1.0 / width)
    embed = jnp.concatenate([embed_ref[...], jnp.ones((LANES - latents, width), BF16)], axis=0)
    lane = lane_index(step)
    for start in range(0, total, step):
        here = slice(start, start + step)
        rows = merged_ref[here, :].astype(F32)
        mean = -jnp.sum(rows[:, :latents] * embed_mean, axis=-1, keepdims=True)
        high = mean.astype(BF16).astype(F32)
        middle = (mean - high).astype(BF16).astype(F32)
        low = mean - high - middle
        tail = jnp.where(lane == latents, high, 0.0)
        tail = jnp.where(lane == latents + 1, middle, tail)
        tail = jnp.where(lane == latents + 2, low, tail)
        factors = jnp.where(lane < latents, rows, tail).astype(BF16)
        center = jnp.dot(factors, embed, preferred_element_type=F32)
        spread = jnp.mean(center * center, axis=-1, keepdims=True)
        normed = (center * lax.rsqrt(spread + 1e-06) * norm_ref[...]).astype(BF16)
        q_part = jnp.dot(normed, qkv_ref[0], preferred_element_type=F32)
        kv_part = jnp.dot(normed, kv_ref[...], preferred_element_type=F32)
        q_ref[here, :] = head_norm(q_part, qgain_ref[...])
        k_ref[here, :] = head_norm(kv_part[:, :head], kgain_ref[...])
        v_ref[here, :] = kv_part[:, head:].astype(BF16)
    scale = 1.0 / math.sqrt(head)
    for start in range(0, total, step):
        here = slice(start, start + step)
        scores = lax.dot_general(
            q_ref[here, :], k_ref[...], NT, preferred_element_type=F32
        ) * scale + bias
        top = jnp.max(scores, axis=-1, keepdims=True)
        weights = jnp.exp(scores - top)
        denominator = jnp.sum(weights, axis=-1, keepdims=True)
        mixed = jnp.dot(weights.astype(BF16), v_ref[...], preferred_element_type=F32)
        out_ref[here, :] = (mixed / denominator).astype(BF16)
    grp = place_ref[0]
    side = place_ref[1] & 1
    part = block * grp_size
    slabs = total // (2 * part)
    for i in range(2 * slabs):
        start = pl.multiple_of(i * part + grp * block, block)
        own_ref[i * block : (i + 1) * block, :] = out_ref[pl.ds(start, block), :]
    for i in range(slabs):
        start = pl.multiple_of((2 * i + 1 - side) * part, part)
        give_ref[i * part : (i + 1) * part, :] = out_ref[pl.ds(start, part), :]
        start = pl.multiple_of((2 * i + side) * part + grp * block, block)
        first = slabs * part + i * block
        give_ref[first : first + block, :] = out_ref[pl.ds(start, block), :]


def call(body, shapes, *args, name, scratch=(), places=(), flops=10**8, moved=10**6):
    spaces = {"smem": pltpu.SMEM, "hbm": pltpu.HBM}
    outs = tuple(jax.ShapeDtypeStruct(shape, BF16) for shape in shapes)
    whole = pl.BlockSpec(memory_space=pltpu.VMEM)
    in_specs = [whole] * len(args)
    for i, place in enumerate(places):
        in_specs[i] = pl.BlockSpec(memory_space=spaces[place])
    result = pl.pallas_call(
        body,
        out_shape=outs,
        in_specs=in_specs,
        out_specs=(whole,) * len(outs),
        scratch_shapes=list(scratch),
        cost_estimate=pl.CostEstimate(flops=flops, bytes_accessed=moved, transcendentals=0),
        compiler_params=pltpu.CompilerParams(vmem_limit_bytes=48 * 2**20),
        name=name,
    )(*args)
    return result[0] if len(outs) == 1 else result


def shards(
    video, conv_weight, latent_weight, assign, embed_weight, norm_gain, qkv_weight, q_gain, k_gain,
    out_weight, cotangent,
):
    grp_size, seq_size, dp_size = (lax.axis_size(a) for a in ("grp", "seq", "dp"))
    owners = grp_size * seq_size
    block, width = cotangent.shape[1:]
    head = q_gain.shape[0]
    groups = block * owners
    columns = width // grp_size
    shared = block * grp_size
    rows = block * seq_size
    grp = lax.axis_index("grp")
    seq = lax.axis_index("seq")
    place = jnp.stack([grp, seq, lax.axis_index("dp") & 1]).astype(jnp.int32)

    frames = video[0]
    frame_count, tokens = frames.shape[:2]
    earlier = shifted_frames(frames[frame_count - 2 :], "seq", 1)
    latent_t = latent_weight.T
    late, first, taps, latent_rhs = call(
        late_kernel,
        [((frame_count - 2) * tokens, LANES), (2,) + frames.shape[1:], conv_weight.shape,
         latent_t.shape],
        frames, conv_weight, latent_t, name="late_frames", flops=10**9, places=["hbm"] * 3,
        scratch=[pltpu.VMEM(frames.shape, BF16), pltpu.SemaphoreType.DMA((4,))],
    )
    by_column = call(
        split_kernel, [(grp_size, block, columns)], cotangent[0], name="split_columns"
    )
    near = lax.all_to_all(by_column, "grp", 0, 0, tiled=True).reshape(shared, columns)
    late, near = lax.optimization_barrier((late, near))
    sums = call(
        functools.partial(sums_kernel, grp=grp_size, seq=seq_size), [(groups, LANES)],
        first, earlier, taps, latent_rhs, late, assign[0], name="group_sums", flops=10**9,
    )
    near_other = xor_swap(near, "seq", 8)

    parts = lax.all_to_all(sums.reshape(seq_size, shared, LANES), "seq", 0, 0, tiled=True)
    slab_sums = call(resplit_kernel, [(grp_size, shared, LANES)], parts, name="slab_sums")
    near = jnp.concatenate([near, near_other], axis=0)
    near, slab_sums = lax.optimization_barrier((near, slab_sums))
    near_other = xor_swap(near, "seq", 4)
    slab_parts = lax.all_to_all(slab_sums, "grp", 0, 0, tiled=True)
    merged = call(merge_kernel, [(seq_size, shared, LANES)], slab_parts, name="merged")
    near_other, merged = lax.optimization_barrier((near_other, merged))
    near = jnp.concatenate([near, near_other], axis=0)
    far = xor_swap(near, "seq", 2)
    weight, _ = lax.optimization_barrier((out_weight, merged))
    given = lax.dynamic_slice_in_dim(weight, (1 - (seq & 1)) * (width // 2), width // 2, 1)
    weight_other = xor_swap(given, "seq", 1)
    merged = lax.all_to_all(merged, "seq", 0, 0, tiled=True).reshape(groups, LANES)

    head_out, own_rows, given_rows = call(
        functools.partial(attend_kernel, grp_size=grp_size, block=block),
        [(groups, head), (rows, head), (groups // 2 + rows // 2, head)], place, merged,
        embed_weight, norm_gain[None], qkv_weight, q_gain[None], k_gain[None], name="attend",
        flops=8 * 10**9, places=["smem"],
        scratch=[pltpu.VMEM((width, 2 * head), BF16)] + [pltpu.VMEM((groups, head), BF16)] * 3,
    )

    given_rows, weight_other = lax.optimization_barrier((given_rows, weight_other))
    side_rows = xor_swap(given_rows, "seq", 1)
    near_weight, given = call(
        weights_kernel, [(2 * head, columns)] * 2, place, out_weight, weight_other,
        name="weights", places=["smem"],
    )
    far_weight = xor_swap(given, "seq", 2)
    local_grad = call(
        functools.partial(grad_kernel, masks=(8, 4, 2), part=shared), [(2, head, columns)],
        place, head_out, side_rows, near, far, name="local_grad", places=["smem"],
        scratch=[pltpu.VMEM((groups // 2, 2 * head), BF16)], flops=10**9,
    )
    both_sides = [
        [(2 * z + y) * dp_size + d for y in range(2) for d in range(dp_size)]
        for z in range(seq_size // 2)
    ]
    grad_parts = lax.all_to_all(
        local_grad.reshape(2 * dp_size, head // dp_size, columns), ("seq", "dp"), 0, 0,
        axis_index_groups=both_sides, tiled=True,
    )
    pair_heads = call(
        functools.partial(pair_kernel, part=shared), [(2, rows, head)], place, own_rows,
        side_rows, name="pair_heads", places=["smem"],
    )
    far_heads = xor_swap(pair_heads, "seq", 2)

    partials = call(
        project_kernel, [(rows // 4, columns)] * 4, place, pair_heads, far_heads, near_weight,
        far_weight, name="project", flops=10**9, places=["smem"],
        scratch=[pltpu.VMEM((rows, columns), BF16)],
    )
    pairs = dp_size // 2
    grad_block = call(
        spread_kernel, [(grp_size * pairs, head // dp_size, columns)], grad_parts,
        name="grad_block",
    )
    grad_block, *partials = lax.optimization_barrier((grad_block, *partials))
    same_core = [
        [g * dp_size + 2 * p + c for g in range(grp_size) for p in range(pairs)] for c in range(2)
    ]
    grad_cols = lax.all_to_all(
        grad_block, ("grp", "dp"), 0, 0, axis_index_groups=same_core, tiled=True
    )
    partials = [partials[0]] + [xor_swap(partials[k], "seq", 4 * k) for k in range(1, 4)]
    projected = call(total_kernel, [(rows // 4, columns)], *partials, name="projected")
    projected, _ = lax.optimization_barrier((projected, grad_cols))
    quads = [list(range(k, k + 4)) for k in range(0, seq_size, 4)]
    out_parts = lax.all_to_all(
        projected.reshape(4, block, columns), "seq", 0, 0, axis_index_groups=quads, tiled=True
    )
    out_grad = call(
        functools.partial(columns_kernel, pairs=pairs), [(head, width)], place, grad_cols,
        xor_swap(grad_cols, "dp", 1), name="grad_columns", places=["smem"],
    )
    attended = call(attended_kernel, [(block, width)], out_parts, name="attended")
    return (attended[None], out_grad)


def solution(mesh):
    placed = (
        P("dp", "seq", "grp", None), P(), P(), P("dp", "seq", "grp"), P(), P(),
        P(None, None, "seq"), P(), P(), P("seq", None), P("dp", ("grp", "seq"), None),
    )
    return jax.shard_map(
        shards,
        mesh=mesh,
        in_specs=placed,
        out_specs=(P("dp", ("grp", "seq"), None), P("seq", None)),
        check_vma=False,
    )
```

```python
import functools
import math

import jax
import jax.numpy as jnp
from jax import lax
from jax.experimental import pallas as pl
from jax.experimental.pallas import tpu as pltpu
from jax.sharding import PartitionSpec as P

F32 = jnp.float32
BF16 = jnp.bfloat16
LANES = 128
HALF = 64
NT = (((1,), (1,)), ((), ()))
TN = (((0,), (0,)), ((), ()))


def shifted_frames(block, axis, distance):
    devices = range(lax.axis_size(axis))
    route = [(i - distance, i) for i in devices if i - distance in devices]
    return lax.ppermute(block, axis, route)


def ring_step(block, distance):
    size = lax.axis_size("seq")
    return lax.ppermute(block, "seq", [(i, (i + 2 * distance) % size) for i in range(size)])


def xor_swap(block, axis, mask):
    route = [(i, i ^ mask) for i in range(lax.axis_size(axis))]
    return lax.ppermute(block, axis, route)


def lane_index(rows):
    return lax.broadcasted_iota(jnp.int32, (rows, LANES), 1)


def split_pairs(sums):
    lane = lane_index(sums.shape[0])
    high = sums.astype(BF16).astype(F32)
    keep = jnp.logical_or(lane < HALF, lane == LANES - 2)
    return jnp.where(keep, high, sums - high).astype(BF16)


def join_pairs(pairs):
    lane = lane_index(pairs.shape[0])
    total = pairs + jnp.where(lane < HALF - 2, pltpu.roll(pairs, HALF, 1), 0.0)
    counts = pairs[:, LANES - 2 : LANES - 1] + pairs[:, LANES - 1 :]
    return total, counts


def latent_rows(windows, conv_ref, latent_ref):
    channels = conv_ref.shape[1]
    taps = conv_ref[...].reshape(3 * channels, channels)
    weights = jnp.concatenate([latent_ref[...], latent_ref[...]], axis=0)
    latent = None
    for part, views in enumerate(windows):
        cols = slice(part * channels, (part + 1) * channels)
        preact = jnp.dot(jnp.concatenate(views, axis=1), taps, preferred_element_type=F32)
        hidden = (views[0].astype(F32) + preact / (1.0 + jnp.exp(-preact))).astype(BF16)
        term = lax.dot_general(hidden, weights[:, cols], NT, preferred_element_type=F32)
        latent = term if latent is None else latent + term
    return jnp.where(lane_index(latent.shape[0]) < LANES - 2, latent, 1.0).astype(BF16)


def late_kernel(
    video_hbm, conv_hbm, latent_hbm, out_ref, first_ref, conv_ref, latent_ref, video_ref, sems,
):
    copies = [
        pltpu.make_async_copy(src, dst, sems.at[i])
        for i, (src, dst) in enumerate([
            (video_hbm, video_ref), (conv_hbm, conv_ref), (latent_hbm, latent_ref),
            (video_hbm.at[: first_ref.shape[0]], first_ref),
        ])
    ]
    for copy in copies:
        copy.start()
    for copy in copies:
        copy.wait()
    frame_count, tokens, width = video_ref.shape
    channels = conv_ref.shape[1]
    windows = []
    for start in range(0, width, channels):
        cols = slice(start, start + channels)
        windows.append([
            video_ref[2 - k : frame_count - k, :, cols].reshape(-1, channels) for k in range(3)
        ])
    out_ref[...] = latent_rows(windows, conv_ref, latent_ref)


def sums_kernel(
    video_ref, earlier_ref, conv_ref, latent_ref, late_ref, labels_ref, out_ref, *, grp, seq,
):
    channels = conv_ref.shape[1]
    width = video_ref.shape[2]
    windows = []
    for start in range(0, width, channels):
        cols = slice(start, start + channels)
        padded = jnp.concatenate([earlier_ref[:, :, cols], video_ref[:, :, cols]], axis=0)
        windows.append([padded[2 - k : 4 - k].reshape(-1, channels) for k in range(3)])
    first = latent_rows(windows, conv_ref, latent_ref)
    rows = jnp.concatenate([first, late_ref[...]], axis=0)
    labels = jnp.concatenate(
        [labels_ref[i : i + 1, :] for i in range(labels_ref.shape[0])], axis=1
    )
    total = out_ref.shape[0]
    block = total // (grp * seq)
    step = 256
    for start in range(0, total, step):
        place = lax.broadcasted_iota(jnp.int32, (step, labels.shape[1]), 0) + start
        inner = place & (block - 1)
        column = (place >> (block.bit_length() - 1)) & (grp - 1)
        slab = place >> ((block * grp).bit_length() - 1)
        member = (labels == (column * seq + slab) * block + inner).astype(F32).astype(BF16)
        out_ref[start : start + step, :] = split_pairs(
            jnp.dot(member, rows, preferred_element_type=F32)
        )


def add_up(parts_ref):
    total = parts_ref[0].astype(F32)
    for i in range(1, parts_ref.shape[0]):
        total = total + parts_ref[i].astype(F32)
    return total


def resplit_kernel(parts_ref, out_ref):
    total, counts = join_pairs(add_up(parts_ref))
    lane = lane_index(total.shape[0])
    doubled = jnp.where(lane < HALF, total, pltpu.roll(total, HALF, 1))
    pairs = split_pairs(jnp.where(lane < LANES - 2, doubled, counts))
    for i in range(out_ref.shape[0]):
        out_ref[i] = pairs


def merge_kernel(parts_ref, out_ref):
    total, counts = join_pairs(add_up(parts_ref))
    lane = lane_index(total.shape[0])
    merged = jnp.where(lane < HALF, total / counts, 0.0)
    high = counts.astype(BF16).astype(F32)
    marks = jnp.where(lane == LANES - 2, high, counts - high)
    rows = jnp.where(lane < LANES - 2, merged, marks).astype(BF16)
    for i in range(out_ref.shape[0]):
        out_ref[i] = rows


def total_kernel(parts_ref, out_ref):
    out_ref[...] = add_up(parts_ref).astype(BF16)


def split_kernel(rows_ref, out_ref):
    columns = out_ref.shape[2]
    parts = rows_ref.shape[1] // columns
    for i in range(out_ref.shape[0]):
        start = i % parts * columns
        out_ref[i] = rows_ref[:, start : start + columns]


def grad_kernel(place_ref, head_ref, *refs, offsets):
    slab = place_ref[1] >> 1
    part = refs[0].shape[0]
    slabs = head_ref.shape[0] // part
    total = None
    for offset, ref in zip(offsets, refs):
        start = pl.multiple_of(((slab + offset) & (slabs - 1)) * part, part)
        term = lax.dot_general(
            head_ref[pl.ds(start, part), :], ref[...], TN, preferred_element_type=F32
        )
        total = term if total is None else total + term
    refs[-1][...] = total.astype(BF16)


def project_kernel(own_ref, weight_ref, out_ref):
    step = 768
    for start in range(0, weight_ref.shape[1], step):
        cols = slice(start, start + step)
        out_ref[:, cols] = jnp.dot(
            own_ref[...], weight_ref[:, cols], preferred_element_type=F32
        ).astype(BF16)


def columns_kernel(place_ref, *refs):
    out_ref = refs[-1]
    grp, high, core = place_ref[0], place_ref[2] >> 1, place_ref[2] & 1
    columns = refs[0].shape[1]
    rows = refs[0].shape[0] // 8
    for j, ref in enumerate(refs[:-1]):
        left = pl.multiple_of((grp ^ j) * columns, columns)
        for k in range(8):
            lane = core ^ (k & 1)
            top = pl.multiple_of(((high ^ (k >> 1)) * 2 + lane) * rows, rows)
            out_ref[pl.ds(top, rows), pl.ds(left, columns)] = ref[k * rows : (k + 1) * rows, :]


def head_norm(projected, gain):
    square_mean = jnp.mean(projected * projected, axis=-1, keepdims=True)
    return (projected * lax.rsqrt(square_mean + 1e-06) * gain).astype(BF16)


def attend_kernel(
    place_ref, merged_ref, embed_ref, norm_ref, qkv_ref, qgain_ref, kgain_ref, out_ref, own_ref,
       kv_ref, q_ref, k_ref, v_ref, *, grp_size, block,
):
    latents, width = embed_ref.shape
    head = q_ref.shape[1]
    total = out_ref.shape[0]
    step = 256
    kv_ref[:, :head] = qkv_ref[1]
    kv_ref[:, head:] = qkv_ref[2]
    pick = (lane_index(16) >= LANES - 2).astype(F32).astype(BF16)
    count_row = lax.dot_general(pick, merged_ref[...], NT, preferred_element_type=F32)[0:1, :]
    bias = jnp.log(count_row)
    ones = jnp.ones((16, width), BF16)
    embed_mean = lax.dot_general(ones, embed_ref[...], NT, preferred_element_type=F32)
    embed_mean = embed_mean[0:1, :] * (1.0 / width)
    embed = jnp.concatenate([embed_ref[...], jnp.ones((LANES - latents, width), BF16)], axis=0)
    lane = lane_index(step)
    for start in range(0, total, step):
        here = slice(start, start + step)
        rows = merged_ref[here, :].astype(F32)
        mean = -jnp.sum(rows[:, :latents] * embed_mean, axis=-1, keepdims=True)
        high = mean.astype(BF16).astype(F32)
        middle = (mean - high).astype(BF16).astype(F32)
        low = mean - high - middle
        tail = jnp.where(lane == latents, high, 0.0)
        tail = jnp.where(lane == latents + 1, middle, tail)
        tail = jnp.where(lane == latents + 2, low, tail)
        factors = jnp.where(lane < latents, rows, tail).astype(BF16)
        center = jnp.dot(factors, embed, preferred_element_type=F32)
        spread = jnp.mean(center * center, axis=-1, keepdims=True)
        normed = (center * lax.rsqrt(spread + 1e-06) * norm_ref[...]).astype(BF16)
        q_part = jnp.dot(normed, qkv_ref[0], preferred_element_type=F32)
        kv_part = jnp.dot(normed, kv_ref[...], preferred_element_type=F32)
        q_ref[here, :] = head_norm(q_part, qgain_ref[...])
        k_ref[here, :] = head_norm(kv_part[:, :head], kgain_ref[...])
        v_ref[here, :] = kv_part[:, head:].astype(BF16)
    scale = 1.0 / math.sqrt(head)
    for start in range(0, total, step):
        here = slice(start, start + step)
        scores = lax.dot_general(
            q_ref[here, :], k_ref[...], NT, preferred_element_type=F32
        ) * scale + bias
        top = jnp.max(scores, axis=-1, keepdims=True)
        weights = jnp.exp(scores - top)
        denominator = jnp.sum(weights, axis=-1, keepdims=True)
        mixed = jnp.dot(weights.astype(BF16), v_ref[...], preferred_element_type=F32)
        out_ref[here, :] = (mixed / denominator).astype(BF16)
    for i in range(total // (block * grp_size)):
        start = pl.multiple_of((i * grp_size + place_ref[0]) * block, block)
        own_ref[i * block : (i + 1) * block, :] = out_ref[pl.ds(start, block), :]


def call(body, shapes, *args, name, scratch=(), places=(), flops=10**8, moved=10**6):
    spaces = {"smem": pltpu.SMEM, "hbm": pltpu.HBM}
    outs = tuple(jax.ShapeDtypeStruct(shape, BF16) for shape in shapes)
    whole = pl.BlockSpec(memory_space=pltpu.VMEM)
    in_specs = [whole] * len(args)
    for i, place in enumerate(places):
        in_specs[i] = pl.BlockSpec(memory_space=spaces[place])
    result = pl.pallas_call(
        body,
        out_shape=outs,
        in_specs=in_specs,
        out_specs=(whole,) * len(outs),
        scratch_shapes=list(scratch),
        cost_estimate=pl.CostEstimate(flops=flops, bytes_accessed=moved, transcendentals=0),
        compiler_params=pltpu.CompilerParams(vmem_limit_bytes=48 * 2**20),
        name=name,
    )(*args)
    return result[0] if len(outs) == 1 else result


def shards(
    video, conv_weight, latent_weight, assign, embed_weight, norm_gain, qkv_weight, q_gain, k_gain,
    out_weight, cotangent,
):
    grp_size, seq_size, dp_size = (lax.axis_size(a) for a in ("grp", "seq", "dp"))
    owners = grp_size * seq_size
    block, width = cotangent.shape[1:]
    head = q_gain.shape[0]
    groups = block * owners
    columns = width // grp_size
    shared = block * grp_size
    rows = block * seq_size
    grp = lax.axis_index("grp")
    seq = lax.axis_index("seq")
    place = jnp.stack([grp, seq, lax.axis_index("dp")]).astype(jnp.int32)

    frames = video[0]
    frame_count, tokens = frames.shape[:2]
    earlier = shifted_frames(frames[frame_count - 2 :], "seq", 1)
    latent_t = latent_weight.T
    late, first, taps, latent_rhs = call(
        late_kernel,
        [((frame_count - 2) * tokens, LANES), (2,) + frames.shape[1:], conv_weight.shape,
         latent_t.shape],
        frames, conv_weight, latent_t, name="late_frames", flops=10**9, places=["hbm"] * 3,
        scratch=[pltpu.VMEM(frames.shape, BF16), pltpu.SemaphoreType.DMA((4,))],
    )
    by_column = call(
        split_kernel, [(2 * grp_size, block, columns)], cotangent[0], name="split_columns"
    )
    corners = [
        [g * seq_size + 2 * z + y for y in range(2) for g in range(grp_size)]
        for z in range(seq_size // 2)
    ]
    near = lax.all_to_all(
        by_column, ("grp", "seq"), 0, 0, axis_index_groups=corners, tiled=True
    ).reshape(2 * shared, columns)
    late, near = lax.optimization_barrier((late, near))
    sums = call(
        functools.partial(sums_kernel, grp=grp_size, seq=seq_size), [(groups, LANES)],
        first, earlier, taps, latent_rhs, late, assign[0], name="group_sums", flops=10**9,
    )
    near, sums = lax.optimization_barrier((near, sums))
    up, down = ring_step(near, 1), ring_step(near, -1)
    parts = lax.all_to_all(sums.reshape(seq_size, shared, LANES), "seq", 0, 0, tiled=True)
    grad_rows = [near, up, down]
    slab_sums = call(resplit_kernel, [(grp_size, shared, LANES)], parts, name="slab_sums")
    up, down, slab_sums = lax.optimization_barrier((up, down, slab_sums))
    slab_parts = lax.all_to_all(slab_sums, "grp", 0, 0, tiled=True)
    up, down = ring_step(up, 1), ring_step(down, -1)
    grad_rows += [up, down]
    merged = call(merge_kernel, [(seq_size, shared, LANES)], slab_parts, name="merged")
    up, down, merged = lax.optimization_barrier((up, down, merged))
    merged = lax.all_to_all(merged, "seq", 0, 0, tiled=True)
    up, down = ring_step(up, 1), ring_step(down, -1)
    grad_rows += [up, down]
    up, down, merged = lax.optimization_barrier((up, down, merged))
    grad_rows += [ring_step(up, 1)]
    offsets = (0, -1, 1, -2, 2, -3, 3, -4)

    head_out, own_rows = call(
        functools.partial(attend_kernel, grp_size=grp_size, block=block),
        [(groups, head), (rows, head)], place, merged.reshape(groups, LANES), embed_weight,
        norm_gain[None], qkv_weight, q_gain[None], k_gain[None], name="attend",
        flops=8 * 10**9, places=["smem"],
        scratch=[pltpu.VMEM((width, 2 * head), BF16)] + [pltpu.VMEM((groups, head), BF16)] * 3,
    )
    local_grad = call(
        functools.partial(grad_kernel, offsets=offsets), [(head, columns)], place, head_out,
        *grad_rows, name="local_grad", places=["smem"], flops=10**9,
    )
    grad_parts = lax.all_to_all(
        local_grad.reshape(dp_size, head // dp_size, columns), "dp", 0, 0, tiled=True
    )
    partial = call(
        project_kernel, [(rows, width)], own_rows, out_weight, name="project", flops=10**9,
    )
    grad_block = call(
        total_kernel, [(head // dp_size, columns)], grad_parts, name="grad_block"
    )
    partial, grad_block = lax.optimization_barrier((partial, grad_block))
    out_parts = lax.all_to_all(
        partial.reshape(seq_size, block, width), "seq", 0, 0, tiled=True
    )
    both = jnp.concatenate([grad_block, xor_swap(grad_block, "dp", 1)], axis=0)
    grad_cols = jnp.concatenate(
        [both] + [xor_swap(both, "dp", 2 * k) for k in range(1, dp_size // 2)], axis=0
    )
    out_grad = call(
        columns_kernel, [(head, width)], place, grad_cols,
        *[xor_swap(grad_cols, "grp", k) for k in range(1, grp_size)], name="grad_columns",
        places=["smem"],
    )
    attended = call(total_kernel, [(block, width)], out_parts, name="attended")
    return (attended[None], out_grad)


def solution(mesh):
    placed = (
        P("dp", "seq", "grp", None), P(), P(), P("dp", "seq", "grp"), P(), P(),
        P(None, None, "seq"), P(), P(), P("seq", None), P("dp", ("grp", "seq"), None),
    )
    return jax.shard_map(
        shards,
        mesh=mesh,
        in_specs=placed,
        out_specs=(P("dp", ("grp", "seq"), None), P("seq", None)),
        check_vma=False,
    )
```

```python
import functools
import math

import jax
import jax.numpy as jnp
from jax import lax
from jax.experimental import pallas as pl
from jax.experimental.pallas import tpu as pltpu
from jax.sharding import PartitionSpec as P

F32 = jnp.float32
BF16 = jnp.bfloat16
LANES = 128
HALF = 64
NT = (((1,), (1,)), ((), ()))
TN = (((0,), (0,)), ((), ()))


def shifted_frames(block, axis, distance):
    devices = range(lax.axis_size(axis))
    route = [(i - distance, i) for i in devices if i - distance in devices]
    return lax.ppermute(block, axis, route)


def xor_swap(block, axis, mask):
    route = [(i, i ^ mask) for i in range(lax.axis_size(axis))]
    return lax.ppermute(block, axis, route)


def lane_index(rows):
    return lax.broadcasted_iota(jnp.int32, (rows, LANES), 1)


def split_pairs(sums):
    lane = lane_index(sums.shape[0])
    high = sums.astype(BF16).astype(F32)
    keep = jnp.logical_or(lane < HALF, lane == LANES - 2)
    return jnp.where(keep, high, sums - high).astype(BF16)


def join_pairs(pairs):
    lane = lane_index(pairs.shape[0])
    total = pairs + jnp.where(lane < HALF - 2, pltpu.roll(pairs, HALF, 1), 0.0)
    counts = pairs[:, LANES - 2 : LANES - 1] + pairs[:, LANES - 1 :]
    return total, counts


def latent_rows(windows, conv_ref, latent_ref):
    channels = conv_ref.shape[1]
    taps = conv_ref[...].reshape(3 * channels, channels)
    weights = jnp.concatenate([latent_ref[...], latent_ref[...]], axis=0)
    latent = None
    for part, views in enumerate(windows):
        cols = slice(part * channels, (part + 1) * channels)
        preact = jnp.dot(jnp.concatenate(views, axis=1), taps, preferred_element_type=F32)
        hidden = (views[0].astype(F32) + preact / (1.0 + jnp.exp(-preact))).astype(BF16)
        term = lax.dot_general(hidden, weights[:, cols], NT, preferred_element_type=F32)
        latent = term if latent is None else latent + term
    return jnp.where(lane_index(latent.shape[0]) < LANES - 2, latent, 1.0).astype(BF16)


def late_kernel(
    video_hbm, conv_hbm, latent_hbm, out_ref, first_ref, conv_ref, latent_ref, video_ref, sems,
):
    copies = [
        pltpu.make_async_copy(src, dst, sems.at[i])
        for i, (src, dst) in enumerate([
            (video_hbm, video_ref), (conv_hbm, conv_ref), (latent_hbm, latent_ref),
            (video_hbm.at[: first_ref.shape[0]], first_ref),
        ])
    ]
    for copy in copies:
        copy.start()
    for copy in copies:
        copy.wait()
    frame_count, tokens, width = video_ref.shape
    channels = conv_ref.shape[1]
    windows = []
    for start in range(0, width, channels):
        cols = slice(start, start + channels)
        windows.append([
            video_ref[2 - k : frame_count - k, :, cols].reshape(-1, channels) for k in range(3)
        ])
    out_ref[...] = latent_rows(windows, conv_ref, latent_ref)


def sums_kernel(
    video_ref, earlier_ref, conv_ref, latent_ref, late_ref, labels_ref, out_ref, *, grp, seq,
):
    channels = conv_ref.shape[1]
    width = video_ref.shape[2]
    windows = []
    for start in range(0, width, channels):
        cols = slice(start, start + channels)
        padded = jnp.concatenate([earlier_ref[:, :, cols], video_ref[:, :, cols]], axis=0)
        windows.append([padded[2 - k : 4 - k].reshape(-1, channels) for k in range(3)])
    first = latent_rows(windows, conv_ref, latent_ref)
    rows = jnp.concatenate([first, late_ref[...]], axis=0)
    labels = jnp.concatenate(
        [labels_ref[i : i + 1, :] for i in range(labels_ref.shape[0])], axis=1
    )
    total = out_ref.shape[0]
    block = total // (grp * seq)
    step = 256
    for start in range(0, total, step):
        place = lax.broadcasted_iota(jnp.int32, (step, labels.shape[1]), 0) + start
        inner = place & (block - 1)
        column = (place >> (block.bit_length() - 1)) & (grp - 1)
        slab = place >> ((block * grp).bit_length() - 1)
        member = (labels == (column * seq + slab) * block + inner).astype(F32).astype(BF16)
        out_ref[start : start + step, :] = split_pairs(
            jnp.dot(member, rows, preferred_element_type=F32)
        )


def add_up(parts_ref):
    total = parts_ref[0].astype(F32)
    for i in range(1, parts_ref.shape[0]):
        total = total + parts_ref[i].astype(F32)
    return total


def resplit_kernel(parts_ref, cot_ref, out_ref):
    total, counts = join_pairs(add_up(parts_ref))
    lane = lane_index(total.shape[0])
    doubled = jnp.where(lane < HALF, total, pltpu.roll(total, HALF, 1))
    pairs = split_pairs(jnp.where(lane < LANES - 2, doubled, counts))
    for i in range(out_ref.shape[0]):
        out_ref[i, : pairs.shape[0], :] = pairs
    block, width = cot_ref.shape
    pieces = width // LANES // out_ref.shape[0]
    for i in range(width // LANES):
        start = pairs.shape[0] + i % pieces * block
        here = cot_ref[:, i * LANES : (i + 1) * LANES]
        out_ref[i // pieces, start : start + block, :] = here


def merge_kernel(parts_ref, out_ref):
    total, counts = join_pairs(add_up(parts_ref)[: out_ref.shape[1], :])
    lane = lane_index(total.shape[0])
    merged = jnp.where(lane < HALF, total / counts, 0.0)
    high = counts.astype(BF16).astype(F32)
    marks = jnp.where(lane == LANES - 2, high, counts - high)
    rows = jnp.where(lane < LANES - 2, merged, marks).astype(BF16)
    for i in range(out_ref.shape[0]):
        out_ref[i] = rows


def spread_kernel(parts_ref, out_ref):
    total = add_up(parts_ref).astype(BF16)
    for i in range(out_ref.shape[0]):
        out_ref[i] = total


def near_kernel(parts_ref, out_ref):
    rows, columns = out_ref.shape[1:]
    block = rows // parts_ref.shape[0]
    first = parts_ref.shape[1] - columns // LANES * block
    for g in range(parts_ref.shape[0]):
        for b in range(columns // LANES):
            start = first + b * block
            piece = parts_ref[g, start : start + block, :]
            for i in range(out_ref.shape[0]):
                cols = slice(b * LANES, (b + 1) * LANES)
                out_ref[i, g * block : (g + 1) * block, cols] = piece


def grad_kernel(place_ref, head_ref, given_ref, cot_ref, out_ref, rows_ref):
    side = place_ref[1] & 1
    head = head_ref.shape[1]
    slabs, part = cot_ref.shape[:2]
    for slab in range(slabs):
        start = pl.multiple_of((2 * slab + side) * part, part)
        here = slice(slab * part, (slab + 1) * part)
        rows_ref[here, :head] = head_ref[pl.ds(start, part), :]
        rows_ref[here, head:] = given_ref[here, :]
    cot = cot_ref[...].reshape(slabs * part, cot_ref.shape[2])
    total = lax.dot_general(rows_ref[...], cot, TN, preferred_element_type=F32).astype(BF16)
    out_ref[side] = total[:head, :]
    out_ref[1 - side] = total[head:, :]


def pair_kernel(place_ref, own_ref, given_ref, out_ref, *, part):
    grp = place_ref[0]
    side = place_ref[1] & 1
    rows = own_ref.shape[0]
    slabs = (given_ref.shape[0] - rows // 2) // part
    block = rows // (2 * slabs)
    out_ref[0] = own_ref[...]
    for i in range(slabs):
        near = pl.multiple_of((2 * i + side) * block, block)
        far = pl.multiple_of((2 * i + 1 - side) * block, block)
        start = pl.multiple_of(i * part + grp * block, block)
        out_ref[1, pl.ds(near, block), :] = given_ref[pl.ds(start, block), :]
        first = slabs * part + i * block
        out_ref[1, pl.ds(far, block), :] = given_ref[first : first + block, :]


def weights_kernel(place_ref, weight_ref, partner_ref, kept_ref, given_ref):
    columns = kept_ref.shape[1]
    size = weight_ref.shape[0]
    side = place_ref[1] & 1
    depth = (place_ref[1] >> 1) & 1
    for i, (ref, first) in enumerate([(weight_ref, 2 * side), (partner_ref, 0)]):
        keep = pl.multiple_of((first + depth) * columns, columns)
        give = pl.multiple_of((first + 1 - depth) * columns, columns)
        kept_ref[i * size : (i + 1) * size, :] = ref[:, pl.ds(keep, columns)]
        given_ref[i * size : (i + 1) * size, :] = ref[:, pl.ds(give, columns)]


def project_kernel(near_ref, far_ref, near_weight_ref, far_weight_ref, out_ref):
    near = jnp.concatenate([near_ref[0], near_ref[1]], axis=1)
    far = jnp.concatenate([far_ref[0], far_ref[1]], axis=1)
    out_ref[...] = (
        jnp.dot(near, near_weight_ref[...], preferred_element_type=F32)
        + jnp.dot(far, far_weight_ref[...], preferred_element_type=F32)
    ).astype(BF16)


def attended_kernel(parts_ref, out_ref):
    columns = parts_ref.shape[2]
    for t in range(4):
        total = parts_ref[t].astype(F32)
        for i in range(t + 4, parts_ref.shape[0], 4):
            total = total + parts_ref[i].astype(F32)
        start = (2 * (t & 1) + (t >> 1)) * columns
        out_ref[:, start : start + columns] = total.astype(BF16)


def columns_kernel(place_ref, *refs):
    out_ref = refs[-1]
    columns = refs[0].shape[1]
    for k, ref in enumerate(refs[:-1]):
        start = pl.multiple_of((place_ref[0] ^ k) * columns, columns)
        out_ref[:, pl.ds(start, columns)] = ref[...]


def head_norm(projected, gain):
    square_mean = jnp.mean(projected * projected, axis=-1, keepdims=True)
    return (projected * lax.rsqrt(square_mean + 1e-06) * gain).astype(BF16)


def attend_kernel(
    place_ref, merged_ref, embed_ref, norm_ref, qkv_ref, qgain_ref, kgain_ref, out_ref, own_ref,
    give_ref,    kv_ref, q_ref, k_ref, v_ref, *, grp_size, block,
):
    latents, width = embed_ref.shape
    head = q_ref.shape[1]
    total = out_ref.shape[0]
    step = 256
    kv_ref[:, :head] = qkv_ref[1]
    kv_ref[:, head:] = qkv_ref[2]
    pick = (lane_index(16) >= LANES - 2).astype(F32).astype(BF16)
    count_row = lax.dot_general(pick, merged_ref[...], NT, preferred_element_type=F32)[0:1, :]
    bias = jnp.log(count_row)
    ones = jnp.ones((16, width), BF16)
    embed_mean = lax.dot_general(ones, embed_ref[...], NT, preferred_element_type=F32)
    embed_mean = embed_mean[0:1, :] * (1.0 / width)
    embed = jnp.concatenate([embed_ref[...], jnp.ones((LANES - latents, width), BF16)], axis=0)
    lane = lane_index(step)
    for start in range(0, total, step):
        here = slice(start, start + step)
        rows = merged_ref[here, :].astype(F32)
        mean = -jnp.sum(rows[:, :latents] * embed_mean, axis=-1, keepdims=True)
        high = mean.astype(BF16).astype(F32)
        middle = (mean - high).astype(BF16).astype(F32)
        low = mean - high - middle
        tail = jnp.where(lane == latents, high, 0.0)
        tail = jnp.where(lane == latents + 1, middle, tail)
        tail = jnp.where(lane == latents + 2, low, tail)
        factors = jnp.where(lane < latents, rows, tail).astype(BF16)
        center = jnp.dot(factors, embed, preferred_element_type=F32)
        spread = jnp.mean(center * center, axis=-1, keepdims=True)
        normed = (center * lax.rsqrt(spread + 1e-06) * norm_ref[...]).astype(BF16)
        q_part = jnp.dot(normed, qkv_ref[0], preferred_element_type=F32)
        kv_part = jnp.dot(normed, kv_ref[...], preferred_element_type=F32)
        q_ref[here, :] = head_norm(q_part, qgain_ref[...])
        k_ref[here, :] = head_norm(kv_part[:, :head], kgain_ref[...])
        v_ref[here, :] = kv_part[:, head:].astype(BF16)
    scale = 1.0 / math.sqrt(head)
    for start in range(0, total, step):
        here = slice(start, start + step)
        scores = lax.dot_general(
            q_ref[here, :], k_ref[...], NT, preferred_element_type=F32
        ) * scale + bias
        top = jnp.max(scores, axis=-1, keepdims=True)
        weights = jnp.exp(scores - top)
        denominator = jnp.sum(weights, axis=-1, keepdims=True)
        mixed = jnp.dot(weights.astype(BF16), v_ref[...], preferred_element_type=F32)
        out_ref[here, :] = (mixed / denominator).astype(BF16)
    grp = place_ref[0]
    side = place_ref[1] & 1
    part = block * grp_size
    slabs = total // (2 * part)
    for i in range(2 * slabs):
        start = pl.multiple_of(i * part + grp * block, block)
        own_ref[i * block : (i + 1) * block, :] = out_ref[pl.ds(start, block), :]
    for i in range(slabs):
        start = pl.multiple_of((2 * i + 1 - side) * part, part)
        give_ref[i * part : (i + 1) * part, :] = out_ref[pl.ds(start, part), :]
        start = pl.multiple_of((2 * i + side) * part + grp * block, block)
        first = slabs * part + i * block
        give_ref[first : first + block, :] = out_ref[pl.ds(start, block), :]


def call(body, shapes, *args, name, scratch=(), places=(), flops=10**8, moved=10**6):
    spaces = {"smem": pltpu.SMEM, "hbm": pltpu.HBM}
    outs = tuple(jax.ShapeDtypeStruct(shape, BF16) for shape in shapes)
    whole = pl.BlockSpec(memory_space=pltpu.VMEM)
    in_specs = [whole] * len(args)
    for i, place in enumerate(places):
        in_specs[i] = pl.BlockSpec(memory_space=spaces[place])
    result = pl.pallas_call(
        body,
        out_shape=outs,
        in_specs=in_specs,
        out_specs=(whole,) * len(outs),
        scratch_shapes=list(scratch),
        cost_estimate=pl.CostEstimate(flops=flops, bytes_accessed=moved, transcendentals=0),
        compiler_params=pltpu.CompilerParams(vmem_limit_bytes=48 * 2**20),
        name=name,
    )(*args)
    return result[0] if len(outs) == 1 else result


def shards(
    video, conv_weight, latent_weight, assign, embed_weight, norm_gain, qkv_weight, q_gain, k_gain,
    out_weight, cotangent,
):
    grp_size, seq_size, dp_size = (lax.axis_size(a) for a in ("grp", "seq", "dp"))
    owners = grp_size * seq_size
    block, width = cotangent.shape[1:]
    head = q_gain.shape[0]
    groups = block * owners
    columns = width // grp_size
    shared = block * grp_size
    rows = block * seq_size
    grp = lax.axis_index("grp")
    seq = lax.axis_index("seq")
    place = jnp.stack([grp, seq, lax.axis_index("dp") & 1]).astype(jnp.int32)

    frames = video[0]
    frame_count, tokens = frames.shape[:2]
    earlier = shifted_frames(frames[frame_count - 2 :], "seq", 1)
    latent_t = latent_weight.T
    late, first, taps, latent_rhs = call(
        late_kernel,
        [((frame_count - 2) * tokens, LANES), (2,) + frames.shape[1:], conv_weight.shape,
         latent_t.shape],
        frames, conv_weight, latent_t, name="late_frames", flops=10**9, places=["hbm"] * 3,
        scratch=[pltpu.VMEM(frames.shape, BF16), pltpu.SemaphoreType.DMA((4,))],
    )
    sums = call(
        functools.partial(sums_kernel, grp=grp_size, seq=seq_size), [(groups, LANES)],
        first, earlier, taps, latent_rhs, late, assign[0], name="group_sums", flops=10**9,
    )

    parts = lax.all_to_all(sums.reshape(seq_size, shared, LANES), "seq", 0, 0, tiled=True)
    carried = shared + columns // LANES * block
    slab_sums = call(
        resplit_kernel, [(grp_size, carried, LANES)], parts, cotangent[0], name="slab_sums"
    )
    slab_parts = lax.all_to_all(slab_sums, "grp", 0, 0, tiled=True)
    merged = call(merge_kernel, [(seq_size, shared, LANES)], slab_parts, name="merged")
    merged = lax.all_to_all(merged, "seq", 0, 0, tiled=True).reshape(groups, LANES)
    slabs = seq_size // 2
    near = call(near_kernel, [(slabs, shared, columns)], slab_parts, name="near_rows")
    near, merged = lax.optimization_barrier((near, merged))
    same_side = [list(range(k, seq_size, 2)) for k in range(2)]
    grad_rows = lax.all_to_all(near, "seq", 0, 0, axis_index_groups=same_side, tiled=True)

    head_out, own_rows, given_rows = call(
        functools.partial(attend_kernel, grp_size=grp_size, block=block),
        [(groups, head), (rows, head), (groups // 2 + rows // 2, head)], place, merged,
        embed_weight, norm_gain[None], qkv_weight, q_gain[None], k_gain[None], name="attend",
        flops=8 * 10**9, places=["smem"],
        scratch=[pltpu.VMEM((width, 2 * head), BF16)] + [pltpu.VMEM((groups, head), BF16)] * 3,
    )

    side_rows = xor_swap(given_rows, "seq", 1)
    side_rows, weight = lax.optimization_barrier((side_rows, out_weight))
    given = lax.dynamic_slice_in_dim(weight, (1 - (seq & 1)) * (width // 2), width // 2, 1)
    weight_other = xor_swap(given, "seq", 1)
    local_grad = call(
        grad_kernel, [(2, head, columns)], place, head_out, side_rows, grad_rows,
        name="local_grad", places=["smem"],
        scratch=[pltpu.VMEM((groups // 2, 2 * head), BF16)], flops=10**9,
    )
    both_sides = [
        [(2 * z + y) * dp_size + d for y in range(2) for d in range(dp_size)]
        for z in range(slabs)
    ]
    grad_parts = lax.all_to_all(
        local_grad.reshape(2 * dp_size, head // dp_size, columns), ("seq", "dp"), 0, 0,
        axis_index_groups=both_sides, tiled=True,
    )
    pair_heads = call(
        functools.partial(pair_kernel, part=shared), [(2, rows, head)], place, own_rows,
        side_rows, name="pair_heads", places=["smem"],
    )
    far_heads = xor_swap(pair_heads, "seq", 2)
    near_weight, given = call(
        weights_kernel, [(2 * head, columns)] * 2, place, weight, weight_other, name="weights",
        places=["smem"],
    )
    far_weight = xor_swap(given, "seq", 2)
    grad_block = call(
        spread_kernel, [(dp_size, head // dp_size, columns)], grad_parts, name="grad_block"
    )
    grad_cols = lax.all_to_all(grad_block, "dp", 0, 0, tiled=True).reshape(head, columns)
    partial = call(
        project_kernel, [(rows, columns)], pair_heads, far_heads, near_weight, far_weight,
        name="project", flops=10**9,
    )
    partial, grad_cols = lax.optimization_barrier((partial, grad_cols))
    out_parts = lax.all_to_all(
        partial.reshape(seq_size, block, columns), "seq", 0, 0, tiled=True
    )
    gathered = [grad_cols] + [xor_swap(grad_cols, "grp", k) for k in range(1, grp_size)]
    out_grad = call(
        columns_kernel, [(head, width)], place, *gathered, name="grad_columns", places=["smem"]
    )
    attended = call(attended_kernel, [(block, width)], out_parts, name="attended")
    return (attended[None], out_grad)


def solution(mesh):
    placed = (
        P("dp", "seq", "grp", None), P(), P(), P("dp", "seq", "grp"), P(), P(),
        P(None, None, "seq"), P(), P(), P("seq", None), P("dp", ("grp", "seq"), None),
    )
    return jax.shard_map(
        shards,
        mesh=mesh,
        in_specs=placed,
        out_specs=(P("dp", ("grp", "seq"), None), P("seq", None)),
        check_vma=False,
    )
```

```python
import functools
import math

import jax
import jax.numpy as jnp
from jax import lax
from jax.experimental import pallas as pl
from jax.experimental.pallas import tpu as pltpu
from jax.sharding import PartitionSpec as P

F32 = jnp.float32
BF16 = jnp.bfloat16
LANES = 128
HALF = 64
NT = (((1,), (1,)), ((), ()))
TN = (((0,), (0,)), ((), ()))


def shifted_frames(block, axis, distance):
    devices = range(lax.axis_size(axis))
    route = [(i - distance, i) for i in devices if i - distance in devices]
    return lax.ppermute(block, axis, route)


def xor_swap(block, axis, mask):
    route = [(i, i ^ mask) for i in range(lax.axis_size(axis))]
    return lax.ppermute(block, axis, route)


def lane_index(rows):
    return lax.broadcasted_iota(jnp.int32, (rows, LANES), 1)


def split_pairs(sums):
    lane = lane_index(sums.shape[0])
    high = sums.astype(BF16).astype(F32)
    keep = jnp.logical_or(lane < HALF, lane == LANES - 2)
    return jnp.where(keep, high, sums - high).astype(BF16)


def join_pairs(pairs):
    lane = lane_index(pairs.shape[0])
    total = pairs + jnp.where(lane < HALF - 2, pltpu.roll(pairs, HALF, 1), 0.0)
    counts = pairs[:, LANES - 2 : LANES - 1] + pairs[:, LANES - 1 :]
    return total, counts


def latent_rows(windows, conv_ref, latent_ref):
    channels = conv_ref.shape[1]
    taps = conv_ref[...].reshape(3 * channels, channels)
    weights = jnp.concatenate([latent_ref[...], latent_ref[...]], axis=0)
    latent = None
    for part, views in enumerate(windows):
        cols = slice(part * channels, (part + 1) * channels)
        preact = jnp.dot(jnp.concatenate(views, axis=1), taps, preferred_element_type=F32)
        hidden = (views[0].astype(F32) + preact / (1.0 + jnp.exp(-preact))).astype(BF16)
        term = lax.dot_general(hidden, weights[:, cols], NT, preferred_element_type=F32)
        latent = term if latent is None else latent + term
    return jnp.where(lane_index(latent.shape[0]) < LANES - 2, latent, 1.0).astype(BF16)


def late_kernel(
    video_hbm, conv_hbm, latent_hbm, out_ref, first_ref, conv_ref, latent_ref, video_ref, sems,
):
    copies = [
        pltpu.make_async_copy(src, dst, sems.at[i])
        for i, (src, dst) in enumerate([
            (video_hbm, video_ref), (conv_hbm, conv_ref), (latent_hbm, latent_ref),
            (video_hbm.at[: first_ref.shape[0]], first_ref),
        ])
    ]
    for copy in copies:
        copy.start()
    for copy in copies:
        copy.wait()
    frame_count, tokens, width = video_ref.shape
    channels = conv_ref.shape[1]
    windows = []
    for start in range(0, width, channels):
        cols = slice(start, start + channels)
        windows.append([
            video_ref[2 - k : frame_count - k, :, cols].reshape(-1, channels) for k in range(3)
        ])
    out_ref[...] = latent_rows(windows, conv_ref, latent_ref)


def sums_kernel(
    video_ref, earlier_ref, conv_ref, latent_ref, late_ref, labels_ref, out_ref, *, grp, seq,
):
    channels = conv_ref.shape[1]
    width = video_ref.shape[2]
    windows = []
    for start in range(0, width, channels):
        cols = slice(start, start + channels)
        padded = jnp.concatenate([earlier_ref[:, :, cols], video_ref[:, :, cols]], axis=0)
        windows.append([padded[2 - k : 4 - k].reshape(-1, channels) for k in range(3)])
    first = latent_rows(windows, conv_ref, latent_ref)
    rows = jnp.concatenate([first, late_ref[...]], axis=0)
    labels = jnp.concatenate(
        [labels_ref[i : i + 1, :] for i in range(labels_ref.shape[0])], axis=1
    )
    total = out_ref.shape[0]
    block = total // (grp * seq)
    step = 256
    for start in range(0, total, step):
        place = lax.broadcasted_iota(jnp.int32, (step, labels.shape[1]), 0) + start
        inner = place & (block - 1)
        column = (place >> (block.bit_length() - 1)) & (grp - 1)
        slab = place >> ((block * grp).bit_length() - 1)
        member = (labels == (column * seq + slab) * block + inner).astype(F32).astype(BF16)
        out_ref[start : start + step, :] = split_pairs(
            jnp.dot(member, rows, preferred_element_type=F32)
        )


def add_up(parts_ref):
    total = parts_ref[0].astype(F32)
    for i in range(1, parts_ref.shape[0]):
        total = total + parts_ref[i].astype(F32)
    return total


def resplit_kernel(parts_ref, cot_ref, out_ref):
    total, counts = join_pairs(add_up(parts_ref))
    lane = lane_index(total.shape[0])
    doubled = jnp.where(lane < HALF, total, pltpu.roll(total, HALF, 1))
    pairs = split_pairs(jnp.where(lane < LANES - 2, doubled, counts))
    for i in range(out_ref.shape[0]):
        out_ref[i, : pairs.shape[0], :] = pairs
    block, width = cot_ref.shape
    pieces = width // LANES // out_ref.shape[0]
    for i in range(width // LANES):
        start = pairs.shape[0] + i % pieces * block
        here = cot_ref[:, i * LANES : (i + 1) * LANES]
        out_ref[i // pieces, start : start + block, :] = here


def merge_kernel(parts_ref, out_ref):
    total, counts = join_pairs(add_up(parts_ref)[: out_ref.shape[1], :])
    lane = lane_index(total.shape[0])
    merged = jnp.where(lane < HALF, total / counts, 0.0)
    high = counts.astype(BF16).astype(F32)
    marks = jnp.where(lane == LANES - 2, high, counts - high)
    rows = jnp.where(lane < LANES - 2, merged, marks).astype(BF16)
    for i in range(out_ref.shape[0]):
        out_ref[i] = rows


def spread_kernel(parts_ref, out_ref):
    total = add_up(parts_ref).astype(BF16)
    for i in range(out_ref.shape[0]):
        out_ref[i] = total


def near_kernel(parts_ref, out_ref):
    rows, columns = out_ref.shape[1:]
    block = rows // parts_ref.shape[0]
    first = parts_ref.shape[1] - columns // LANES * block
    for g in range(parts_ref.shape[0]):
        for b in range(columns // LANES):
            start = first + b * block
            piece = parts_ref[g, start : start + block, :]
            for i in range(out_ref.shape[0]):
                cols = slice(b * LANES, (b + 1) * LANES)
                out_ref[i, g * block : (g + 1) * block, cols] = piece


def grad_kernel(place_ref, head_ref, given_ref, cot_ref, out_ref, rows_ref):
    side = place_ref[1] & 1
    head = head_ref.shape[1]
    slabs, part = cot_ref.shape[:2]
    for slab in range(slabs):
        start = pl.multiple_of((2 * slab + side) * part, part)
        here = slice(slab * part, (slab + 1) * part)
        rows_ref[here, :head] = head_ref[pl.ds(start, part), :]
        rows_ref[here, head:] = given_ref[here, :]
    cot = cot_ref[...].reshape(slabs * part, cot_ref.shape[2])
    total = lax.dot_general(rows_ref[...], cot, TN, preferred_element_type=F32).astype(BF16)
    out_ref[side] = total[:head, :]
    out_ref[1 - side] = total[head:, :]


def project_kernel(
    place_ref, own_ref, given_ref, weight_ref, partner_ref, out_ref, heads_ref, *, part,
):
    grp = place_ref[0]
    side = place_ref[1] & 1
    rows, head = own_ref.shape
    slabs = (given_ref.shape[0] - rows // 2) // part
    block = rows // (2 * slabs)
    heads_ref[:, :head] = own_ref[...]
    for i in range(slabs):
        near = pl.multiple_of((2 * i + side) * block, block)
        far = pl.multiple_of((2 * i + 1 - side) * block, block)
        start = pl.multiple_of(i * part + grp * block, block)
        heads_ref[pl.ds(near, block), head:] = given_ref[pl.ds(start, block), :]
        first = slabs * part + i * block
        heads_ref[pl.ds(far, block), head:] = given_ref[first : first + block, :]
    step = 768
    for start in range(0, out_ref.shape[1], step):
        here = slice(start, start + step)
        kept = pl.multiple_of(side * out_ref.shape[1] + start, step)
        weights = jnp.concatenate([weight_ref[:, pl.ds(kept, step)], partner_ref[:, here]], axis=0)
        out_ref[:, here] = jnp.dot(
            heads_ref[...], weights, preferred_element_type=F32
        ).astype(BF16)


def attended_kernel(parts_ref, out_ref):
    columns = parts_ref.shape[2]
    for side in range(2):
        total = parts_ref[side].astype(F32)
        for i in range(side + 2, parts_ref.shape[0], 2):
            total = total + parts_ref[i].astype(F32)
        out_ref[:, side * columns : (side + 1) * columns] = total.astype(BF16)


def columns_kernel(place_ref, *refs):
    out_ref = refs[-1]
    columns = refs[0].shape[1]
    for k, ref in enumerate(refs[:-1]):
        start = pl.multiple_of((place_ref[0] ^ k) * columns, columns)
        out_ref[:, pl.ds(start, columns)] = ref[...]


def head_norm(projected, gain):
    square_mean = jnp.mean(projected * projected, axis=-1, keepdims=True)
    return (projected * lax.rsqrt(square_mean + 1e-06) * gain).astype(BF16)


def attend_kernel(
    place_ref, merged_ref, embed_ref, norm_ref, qkv_ref, qgain_ref, kgain_ref, out_ref, own_ref,
    give_ref,    kv_ref, q_ref, k_ref, v_ref, *, grp_size, block,
):
    latents, width = embed_ref.shape
    head = q_ref.shape[1]
    total = out_ref.shape[0]
    step = 256
    kv_ref[:, :head] = qkv_ref[1]
    kv_ref[:, head:] = qkv_ref[2]
    pick = (lane_index(16) >= LANES - 2).astype(F32).astype(BF16)
    count_row = lax.dot_general(pick, merged_ref[...], NT, preferred_element_type=F32)[0:1, :]
    bias = jnp.log(count_row)
    ones = jnp.ones((16, width), BF16)
    embed_mean = lax.dot_general(ones, embed_ref[...], NT, preferred_element_type=F32)
    embed_mean = embed_mean[0:1, :] * (1.0 / width)
    embed = jnp.concatenate([embed_ref[...], jnp.ones((LANES - latents, width), BF16)], axis=0)
    lane = lane_index(step)
    for start in range(0, total, step):
        here = slice(start, start + step)
        rows = merged_ref[here, :].astype(F32)
        mean = -jnp.sum(rows[:, :latents] * embed_mean, axis=-1, keepdims=True)
        high = mean.astype(BF16).astype(F32)
        middle = (mean - high).astype(BF16).astype(F32)
        low = mean - high - middle
        tail = jnp.where(lane == latents, high, 0.0)
        tail = jnp.where(lane == latents + 1, middle, tail)
        tail = jnp.where(lane == latents + 2, low, tail)
        factors = jnp.where(lane < latents, rows, tail).astype(BF16)
        center = jnp.dot(factors, embed, preferred_element_type=F32)
        spread = jnp.mean(center * center, axis=-1, keepdims=True)
        normed = (center * lax.rsqrt(spread + 1e-06) * norm_ref[...]).astype(BF16)
        q_part = jnp.dot(normed, qkv_ref[0], preferred_element_type=F32)
        kv_part = jnp.dot(normed, kv_ref[...], preferred_element_type=F32)
        q_ref[here, :] = head_norm(q_part, qgain_ref[...])
        k_ref[here, :] = head_norm(kv_part[:, :head], kgain_ref[...])
        v_ref[here, :] = kv_part[:, head:].astype(BF16)
    scale = 1.0 / math.sqrt(head)
    for start in range(0, total, step):
        here = slice(start, start + step)
        scores = lax.dot_general(
            q_ref[here, :], k_ref[...], NT, preferred_element_type=F32
        ) * scale + bias
        top = jnp.max(scores, axis=-1, keepdims=True)
        weights = jnp.exp(scores - top)
        denominator = jnp.sum(weights, axis=-1, keepdims=True)
        mixed = jnp.dot(weights.astype(BF16), v_ref[...], preferred_element_type=F32)
        out_ref[here, :] = (mixed / denominator).astype(BF16)
    grp = place_ref[0]
    side = place_ref[1] & 1
    part = block * grp_size
    slabs = total // (2 * part)
    for i in range(2 * slabs):
        start = pl.multiple_of(i * part + grp * block, block)
        own_ref[i * block : (i + 1) * block, :] = out_ref[pl.ds(start, block), :]
    for i in range(slabs):
        start = pl.multiple_of((2 * i + 1 - side) * part, part)
        give_ref[i * part : (i + 1) * part, :] = out_ref[pl.ds(start, part), :]
        start = pl.multiple_of((2 * i + side) * part + grp * block, block)
        first = slabs * part + i * block
        give_ref[first : first + block, :] = out_ref[pl.ds(start, block), :]


def call(body, shapes, *args, name, scratch=(), places=(), flops=10**8, moved=10**6):
    spaces = {"smem": pltpu.SMEM, "hbm": pltpu.HBM}
    outs = tuple(jax.ShapeDtypeStruct(shape, BF16) for shape in shapes)
    whole = pl.BlockSpec(memory_space=pltpu.VMEM)
    in_specs = [whole] * len(args)
    for i, place in enumerate(places):
        in_specs[i] = pl.BlockSpec(memory_space=spaces[place])
    result = pl.pallas_call(
        body,
        out_shape=outs,
        in_specs=in_specs,
        out_specs=(whole,) * len(outs),
        scratch_shapes=list(scratch),
        cost_estimate=pl.CostEstimate(flops=flops, bytes_accessed=moved, transcendentals=0),
        compiler_params=pltpu.CompilerParams(vmem_limit_bytes=48 * 2**20),
        name=name,
    )(*args)
    return result[0] if len(outs) == 1 else result


def shards(
    video, conv_weight, latent_weight, assign, embed_weight, norm_gain, qkv_weight, q_gain, k_gain,
    out_weight, cotangent,
):
    grp_size, seq_size, dp_size = (lax.axis_size(a) for a in ("grp", "seq", "dp"))
    owners = grp_size * seq_size
    block, width = cotangent.shape[1:]
    head = q_gain.shape[0]
    groups = block * owners
    columns = width // grp_size
    shared = block * grp_size
    rows = block * seq_size
    grp = lax.axis_index("grp")
    seq = lax.axis_index("seq")
    place = jnp.stack([grp, seq, lax.axis_index("dp") & 1]).astype(jnp.int32)

    frames = video[0]
    frame_count, tokens = frames.shape[:2]
    earlier = shifted_frames(frames[frame_count - 2 :], "seq", 1)
    latent_t = latent_weight.T
    late, first, taps, latent_rhs = call(
        late_kernel,
        [((frame_count - 2) * tokens, LANES), (2,) + frames.shape[1:], conv_weight.shape,
         latent_t.shape],
        frames, conv_weight, latent_t, name="late_frames", flops=10**9, places=["hbm"] * 3,
        scratch=[pltpu.VMEM(frames.shape, BF16), pltpu.SemaphoreType.DMA((4,))],
    )
    sums = call(
        functools.partial(sums_kernel, grp=grp_size, seq=seq_size), [(groups, LANES)],
        first, earlier, taps, latent_rhs, late, assign[0], name="group_sums", flops=10**9,
    )

    parts = lax.all_to_all(sums.reshape(seq_size, shared, LANES), "seq", 0, 0, tiled=True)
    carried = shared + columns // LANES * block
    slab_sums = call(
        resplit_kernel, [(grp_size, carried, LANES)], parts, cotangent[0], name="slab_sums"
    )
    slab_parts = lax.all_to_all(slab_sums, "grp", 0, 0, tiled=True)
    merged = call(merge_kernel, [(seq_size, shared, LANES)], slab_parts, name="merged")
    merged, weight = lax.optimization_barrier((merged, out_weight))
    given = lax.dynamic_slice_in_dim(weight, (1 - (seq & 1)) * (width // 2), width // 2, 1)
    weight_other = xor_swap(given, "seq", 1)
    merged = lax.all_to_all(merged, "seq", 0, 0, tiled=True).reshape(groups, LANES)
    slabs = seq_size // 2
    near = call(near_kernel, [(slabs, shared, columns)], slab_parts, name="near_rows")
    near, merged = lax.optimization_barrier((near, merged))
    same_side = [list(range(k, seq_size, 2)) for k in range(2)]
    grad_rows = lax.all_to_all(near, "seq", 0, 0, axis_index_groups=same_side, tiled=True)

    head_out, own_rows, given_rows = call(
        functools.partial(attend_kernel, grp_size=grp_size, block=block),
        [(groups, head), (rows, head), (groups // 2 + rows // 2, head)], place, merged,
        embed_weight, norm_gain[None], qkv_weight, q_gain[None], k_gain[None], name="attend",
        flops=8 * 10**9, places=["smem"],
        scratch=[pltpu.VMEM((width, 2 * head), BF16)] + [pltpu.VMEM((groups, head), BF16)] * 3,
    )

    given_rows, weight_other = lax.optimization_barrier((given_rows, weight_other))
    side_rows = xor_swap(given_rows, "seq", 1)
    local_grad = call(
        grad_kernel, [(2, head, columns)], place, head_out, side_rows, grad_rows,
        name="local_grad", places=["smem"],
        scratch=[pltpu.VMEM((groups // 2, 2 * head), BF16)], flops=10**9,
    )
    both_sides = [
        [(2 * z + y) * dp_size + d for y in range(2) for d in range(dp_size)]
        for z in range(slabs)
    ]
    grad_parts = lax.all_to_all(
        local_grad.reshape(2 * dp_size, head // dp_size, columns), ("seq", "dp"), 0, 0,
        axis_index_groups=both_sides, tiled=True,
    )
    partial = call(
        functools.partial(project_kernel, part=shared), [(rows, width // 2)], place, own_rows,
        side_rows, out_weight, weight_other, name="project", flops=10**9, places=["smem"],
        scratch=[pltpu.VMEM((rows, 2 * head), BF16)],
    )
    grad_block = call(
        spread_kernel, [(dp_size, head // dp_size, columns)], grad_parts, name="grad_block"
    )
    grad_block, partial = lax.optimization_barrier((grad_block, partial))
    grad_cols = lax.all_to_all(grad_block, "dp", 0, 0, tiled=True).reshape(head, columns)
    partial, grad_cols = lax.optimization_barrier((partial, grad_cols))
    out_parts = lax.all_to_all(
        partial.reshape(seq_size, block, width // 2), "seq", 0, 0, tiled=True
    )
    gathered = [grad_cols] + [xor_swap(grad_cols, "grp", k) for k in range(1, grp_size)]
    out_grad = call(
        columns_kernel, [(head, width)], place, *gathered, name="grad_columns", places=["smem"]
    )
    attended = call(attended_kernel, [(block, width)], out_parts, name="attended")
    return (attended[None], out_grad)


def solution(mesh):
    placed = (
        P("dp", "seq", "grp", None), P(), P(), P("dp", "seq", "grp"), P(), P(),
        P(None, None, "seq"), P(), P(), P("seq", None), P("dp", ("grp", "seq"), None),
    )
    return jax.shard_map(
        shards,
        mesh=mesh,
        in_specs=placed,
        out_specs=(P("dp", ("grp", "seq"), None), P("seq", None)),
        check_vma=False,
    )
```

```python
import functools
import math

import jax
import jax.numpy as jnp
from jax import lax
from jax.experimental import pallas as pl
from jax.experimental.pallas import tpu as pltpu
from jax.sharding import PartitionSpec as P

F32 = jnp.float32
BF16 = jnp.bfloat16
LANES = 128
HALF = 64
NT = (((1,), (1,)), ((), ()))
TN = (((0,), (0,)), ((), ()))


def shifted_frames(block, axis, distance):
    devices = range(lax.axis_size(axis))
    route = [(i - distance, i) for i in devices if i - distance in devices]
    return lax.ppermute(block, axis, route)


def xor_swap(block, axis, mask):
    route = [(i, i ^ mask) for i in range(lax.axis_size(axis))]
    return lax.ppermute(block, axis, route)


def lane_index(rows):
    return lax.broadcasted_iota(jnp.int32, (rows, LANES), 1)


def split_pairs(sums):
    lane = lane_index(sums.shape[0])
    high = sums.astype(BF16).astype(F32)
    keep = jnp.logical_or(lane < HALF, lane == LANES - 2)
    return jnp.where(keep, high, sums - high).astype(BF16)


def join_pairs(pairs):
    lane = lane_index(pairs.shape[0])
    total = pairs + jnp.where(lane < HALF - 2, pltpu.roll(pairs, HALF, 1), 0.0)
    counts = pairs[:, LANES - 2 : LANES - 1] + pairs[:, LANES - 1 :]
    return total, counts


def latent_rows(windows, conv_ref, latent_ref):
    channels = conv_ref.shape[1]
    taps = conv_ref[...].reshape(3 * channels, channels)
    weights = jnp.concatenate([latent_ref[...], latent_ref[...]], axis=0)
    latent = None
    for part, views in enumerate(windows):
        cols = slice(part * channels, (part + 1) * channels)
        preact = jnp.dot(jnp.concatenate(views, axis=1), taps, preferred_element_type=F32)
        hidden = (views[0].astype(F32) + preact / (1.0 + jnp.exp(-preact))).astype(BF16)
        term = lax.dot_general(hidden, weights[:, cols], NT, preferred_element_type=F32)
        latent = term if latent is None else latent + term
    return jnp.where(lane_index(latent.shape[0]) < LANES - 2, latent, 1.0).astype(BF16)


def late_kernel(
    video_hbm, conv_hbm, latent_hbm, out_ref, first_ref, conv_ref, latent_ref, video_ref, sems,
):
    copies = [
        pltpu.make_async_copy(src, dst, sems.at[i])
        for i, (src, dst) in enumerate([
            (video_hbm, video_ref), (conv_hbm, conv_ref), (latent_hbm, latent_ref),
            (video_hbm.at[: first_ref.shape[0]], first_ref),
        ])
    ]
    for copy in copies:
        copy.start()
    for copy in copies:
        copy.wait()
    frame_count, tokens, width = video_ref.shape
    channels = conv_ref.shape[1]
    windows = []
    for start in range(0, width, channels):
        cols = slice(start, start + channels)
        windows.append([
            video_ref[2 - k : frame_count - k, :, cols].reshape(-1, channels) for k in range(3)
        ])
    out_ref[...] = latent_rows(windows, conv_ref, latent_ref)


def sums_kernel(
    video_ref, earlier_ref, conv_ref, latent_ref, late_ref, labels_ref, out_ref, *, grp, seq,
):
    channels = conv_ref.shape[1]
    width = video_ref.shape[2]
    windows = []
    for start in range(0, width, channels):
        cols = slice(start, start + channels)
        padded = jnp.concatenate([earlier_ref[:, :, cols], video_ref[:, :, cols]], axis=0)
        windows.append([padded[2 - k : 4 - k].reshape(-1, channels) for k in range(3)])
    first = latent_rows(windows, conv_ref, latent_ref)
    rows = jnp.concatenate([first, late_ref[...]], axis=0)
    labels = jnp.concatenate(
        [labels_ref[i : i + 1, :] for i in range(labels_ref.shape[0])], axis=1
    )
    total = out_ref.shape[0]
    block = total // (grp * seq)
    step = 256
    for start in range(0, total, step):
        place = lax.broadcasted_iota(jnp.int32, (step, labels.shape[1]), 0) + start
        inner = place & (block - 1)
        column = (place >> (block.bit_length() - 1)) & (grp - 1)
        slab = place >> ((block * grp).bit_length() - 1)
        member = (labels == (column * seq + slab) * block + inner).astype(F32).astype(BF16)
        out_ref[start : start + step, :] = split_pairs(
            jnp.dot(member, rows, preferred_element_type=F32)
        )


def add_up(parts_ref):
    total = parts_ref[0].astype(F32)
    for i in range(1, parts_ref.shape[0]):
        total = total + parts_ref[i].astype(F32)
    return total


def resplit_kernel(parts_ref, cot_ref, out_ref):
    total, counts = join_pairs(add_up(parts_ref))
    lane = lane_index(total.shape[0])
    doubled = jnp.where(lane < HALF, total, pltpu.roll(total, HALF, 1))
    pairs = split_pairs(jnp.where(lane < LANES - 2, doubled, counts))
    for i in range(out_ref.shape[0]):
        out_ref[i, : pairs.shape[0], :] = pairs
    block, width = cot_ref.shape
    pieces = width // LANES // out_ref.shape[0]
    for i in range(width // LANES):
        start = pairs.shape[0] + i % pieces * block
        here = cot_ref[:, i * LANES : (i + 1) * LANES]
        out_ref[i // pieces, start : start + block, :] = here


def merge_kernel(parts_ref, out_ref):
    total, counts = join_pairs(add_up(parts_ref)[: out_ref.shape[1], :])
    lane = lane_index(total.shape[0])
    merged = jnp.where(lane < HALF, total / counts, 0.0)
    high = counts.astype(BF16).astype(F32)
    marks = jnp.where(lane == LANES - 2, high, counts - high)
    rows = jnp.where(lane < LANES - 2, merged, marks).astype(BF16)
    for i in range(out_ref.shape[0]):
        out_ref[i] = rows


def spread_kernel(parts_ref, out_ref):
    total = add_up(parts_ref).astype(BF16)
    for i in range(out_ref.shape[0]):
        out_ref[i] = total


def near_kernel(parts_ref, out_ref):
    rows, columns = out_ref.shape[1:]
    block = rows // parts_ref.shape[0]
    first = parts_ref.shape[1] - columns // LANES * block
    for g in range(parts_ref.shape[0]):
        for b in range(columns // LANES):
            start = first + b * block
            piece = parts_ref[g, start : start + block, :]
            for i in range(out_ref.shape[0]):
                cols = slice(b * LANES, (b + 1) * LANES)
                out_ref[i, g * block : (g + 1) * block, cols] = piece


def grad_kernel(place_ref, head_ref, given_ref, cot_ref, out_ref, rows_ref):
    side = place_ref[1] & 1
    head = head_ref.shape[1]
    slabs, part = cot_ref.shape[:2]
    for slab in range(slabs):
        start = pl.multiple_of((2 * slab + side) * part, part)
        here = slice(slab * part, (slab + 1) * part)
        rows_ref[here, :head] = head_ref[pl.ds(start, part), :]
        rows_ref[here, head:] = given_ref[here, :]
    cot = cot_ref[...].reshape(slabs * part, cot_ref.shape[2])
    total = lax.dot_general(rows_ref[...], cot, TN, preferred_element_type=F32).astype(BF16)
    out_ref[side] = total[:head, :]
    out_ref[1 - side] = total[head:, :]


def project_kernel(
    place_ref, own_ref, given_ref, weight_ref, partner_ref, out_ref, heads_ref, *, part,
):
    grp = place_ref[0]
    side = place_ref[1] & 1
    rows, head = own_ref.shape
    slabs = (given_ref.shape[0] - rows // 2) // part
    block = rows // (2 * slabs)
    heads_ref[:, :head] = own_ref[...]
    for i in range(slabs):
        near = pl.multiple_of((2 * i + side) * block, block)
        far = pl.multiple_of((2 * i + 1 - side) * block, block)
        start = pl.multiple_of(i * part + grp * block, block)
        heads_ref[pl.ds(near, block), head:] = given_ref[pl.ds(start, block), :]
        first = slabs * part + i * block
        heads_ref[pl.ds(far, block), head:] = given_ref[first : first + block, :]
    step = 768
    for start in range(0, out_ref.shape[1], step):
        here = slice(start, start + step)
        kept = pl.multiple_of(side * out_ref.shape[1] + start, step)
        weights = jnp.concatenate([weight_ref[:, pl.ds(kept, step)], partner_ref[:, here]], axis=0)
        out_ref[:, here] = jnp.dot(
            heads_ref[...], weights, preferred_element_type=F32
        ).astype(BF16)


def attended_kernel(parts_ref, out_ref):
    columns = parts_ref.shape[2]
    for side in range(2):
        total = parts_ref[side].astype(F32)
        for i in range(side + 2, parts_ref.shape[0], 2):
            total = total + parts_ref[i].astype(F32)
        out_ref[:, side * columns : (side + 1) * columns] = total.astype(BF16)


def columns_kernel(place_ref, *refs):
    out_ref = refs[-1]
    columns = refs[0].shape[1]
    for k, ref in enumerate(refs[:-1]):
        start = pl.multiple_of((place_ref[0] ^ k) * columns, columns)
        out_ref[:, pl.ds(start, columns)] = ref[...]


def qkv_kernel(qkv_ref, q_ref, kv_ref, sems):
    head = q_ref.shape[1]
    copies = [
        pltpu.make_async_copy(qkv_ref.at[i], ref, sems.at[i])
        for i, ref in enumerate((q_ref, kv_ref.at[:, :head], kv_ref.at[:, head:]))
    ]
    for copy in copies:
        copy.start()
    for copy in copies:
        copy.wait()


def head_norm(projected, gain):
    square_mean = jnp.mean(projected * projected, axis=-1, keepdims=True)
    return (projected * lax.rsqrt(square_mean + 1e-06) * gain).astype(BF16)


def attend_kernel(
    place_ref, merged_ref, embed_ref, norm_ref, qw_ref, kv_ref, qgain_ref, kgain_ref, out_ref, own_ref,
    give_ref, normed_ref, q_ref, k_ref, v_ref, *, grp_size, block,
):
    latents, width = embed_ref.shape
    head = q_ref.shape[1]
    total = out_ref.shape[0]
    step = 256
    pick = (lane_index(16) >= LANES - 2).astype(F32).astype(BF16)
    count_row = lax.dot_general(pick, merged_ref[...], NT, preferred_element_type=F32)[0:1, :]
    bias = jnp.log(count_row)
    ones = jnp.ones((16, width), BF16)
    embed_mean = lax.dot_general(ones, embed_ref[...], NT, preferred_element_type=F32)
    embed_mean = embed_mean[0:1, :] * (1.0 / width)
    embed = jnp.concatenate([embed_ref[...], jnp.ones((LANES - latents, width), BF16)], axis=0)
    lane = lane_index(step)
    for start in range(0, total, step):
        here = slice(start, start + step)
        rows = merged_ref[here, :].astype(F32)
        mean = -jnp.sum(rows[:, :latents] * embed_mean, axis=-1, keepdims=True)
        high = mean.astype(BF16).astype(F32)
        middle = (mean - high).astype(BF16).astype(F32)
        low = mean - high - middle
        tail = jnp.where(lane == latents, high, 0.0)
        tail = jnp.where(lane == latents + 1, middle, tail)
        tail = jnp.where(lane == latents + 2, low, tail)
        factors = jnp.where(lane < latents, rows, tail).astype(BF16)
        center = jnp.dot(factors, embed, preferred_element_type=F32)
        spread = jnp.mean(center * center, axis=-1, keepdims=True)
        scaled = center * lax.rsqrt(spread + 1e-06) * norm_ref[...]
        normed_ref[here, :] = scaled.astype(BF16)
    q_part = jnp.dot(normed_ref[...], qw_ref[...], preferred_element_type=F32)
    q_ref[...] = head_norm(q_part, qgain_ref[...])
    kv_part = jnp.dot(normed_ref[...], kv_ref[...], preferred_element_type=F32)
    k_ref[...] = head_norm(kv_part[:, :head], kgain_ref[...])
    v_ref[...] = kv_part[:, head:].astype(BF16)
    step = 512
    scale = 1.0 / math.sqrt(head)
    for start in range(0, total, step):
        here = slice(start, start + step)
        scores = lax.dot_general(
            q_ref[here, :], k_ref[...], NT, preferred_element_type=F32
        ) * scale + bias
        top = jnp.max(scores, axis=-1, keepdims=True)
        weights = jnp.exp(scores - top)
        denominator = jnp.sum(weights, axis=-1, keepdims=True)
        mixed = jnp.dot(weights.astype(BF16), v_ref[...], preferred_element_type=F32)
        out_ref[here, :] = (mixed / denominator).astype(BF16)
    grp = place_ref[0]
    side = place_ref[1] & 1
    part = block * grp_size
    slabs = total // (2 * part)
    for i in range(2 * slabs):
        start = pl.multiple_of(i * part + grp * block, block)
        own_ref[i * block : (i + 1) * block, :] = out_ref[pl.ds(start, block), :]
    for i in range(slabs):
        start = pl.multiple_of((2 * i + 1 - side) * part, part)
        give_ref[i * part : (i + 1) * part, :] = out_ref[pl.ds(start, part), :]
        start = pl.multiple_of((2 * i + side) * part + grp * block, block)
        first = slabs * part + i * block
        give_ref[first : first + block, :] = out_ref[pl.ds(start, block), :]


def call(body, shapes, *args, name, scratch=(), places=(), flops=10**8, moved=10**6):
    spaces = {"smem": pltpu.SMEM, "hbm": pltpu.HBM}
    outs = tuple(jax.ShapeDtypeStruct(shape, BF16) for shape in shapes)
    whole = pl.BlockSpec(memory_space=pltpu.VMEM)
    in_specs = [whole] * len(args)
    for i, place in enumerate(places):
        in_specs[i] = pl.BlockSpec(memory_space=spaces[place])
    result = pl.pallas_call(
        body,
        out_shape=outs,
        in_specs=in_specs,
        out_specs=(whole,) * len(outs),
        scratch_shapes=list(scratch),
        cost_estimate=pl.CostEstimate(flops=flops, bytes_accessed=moved, transcendentals=0),
        compiler_params=pltpu.CompilerParams(vmem_limit_bytes=48 * 2**20),
        name=name,
    )(*args)
    return result[0] if len(outs) == 1 else result


def shards(
    video, conv_weight, latent_weight, assign, embed_weight, norm_gain, qkv_weight, q_gain, k_gain,
    out_weight, cotangent,
):
    grp_size, seq_size, dp_size = (lax.axis_size(a) for a in ("grp", "seq", "dp"))
    owners = grp_size * seq_size
    block, width = cotangent.shape[1:]
    head = q_gain.shape[0]
    groups = block * owners
    columns = width // grp_size
    shared = block * grp_size
    rows = block * seq_size
    grp = lax.axis_index("grp")
    seq = lax.axis_index("seq")
    place = jnp.stack([grp, seq, lax.axis_index("dp") & 1]).astype(jnp.int32)

    frames = video[0]
    frame_count, tokens = frames.shape[:2]
    earlier = shifted_frames(frames[frame_count - 2 :], "seq", 1)
    latent_t = latent_weight.T
    late, first, taps, latent_rhs = call(
        late_kernel,
        [((frame_count - 2) * tokens, LANES), (2,) + frames.shape[1:], conv_weight.shape,
         latent_t.shape],
        frames, conv_weight, latent_t, name="late_frames", flops=10**9, places=["hbm"] * 3,
        scratch=[pltpu.VMEM(frames.shape, BF16), pltpu.SemaphoreType.DMA((4,))],
    )
    sums = call(
        functools.partial(sums_kernel, grp=grp_size, seq=seq_size), [(groups, LANES)],
        first, earlier, taps, latent_rhs, late, assign[0], name="group_sums", flops=10**9,
    )

    sums, weight, qkv = lax.optimization_barrier((sums, out_weight, qkv_weight))
    given = lax.dynamic_slice_in_dim(weight, (1 - (seq & 1)) * (width // 2), width // 2, 1)
    weight_other = xor_swap(given, "seq", 1)
    q_weight, kv_weight = call(
        qkv_kernel, [(width, head), (width, 2 * head)], qkv, name="qkv_layout", places=["hbm"],
        moved=10**7,
        scratch=[pltpu.SemaphoreType.DMA((3,))],
    )
    parts = lax.all_to_all(sums.reshape(seq_size, shared, LANES), "seq", 0, 0, tiled=True)
    carried = shared + columns // LANES * block
    slab_sums = call(
        resplit_kernel, [(grp_size, carried, LANES)], parts, cotangent[0], name="slab_sums"
    )
    slab_sums, weight_other, q_weight, kv_weight = lax.optimization_barrier(
        (slab_sums, weight_other, q_weight, kv_weight)
    )
    slab_parts = lax.all_to_all(slab_sums, "grp", 0, 0, tiled=True)
    merged = call(merge_kernel, [(seq_size, shared, LANES)], slab_parts, name="merged")
    merged = lax.all_to_all(merged, "seq", 0, 0, tiled=True).reshape(groups, LANES)
    slabs = seq_size // 2
    near = call(near_kernel, [(slabs, shared, columns)], slab_parts, name="near_rows")
    near, merged = lax.optimization_barrier((near, merged))
    same_side = [list(range(k, seq_size, 2)) for k in range(2)]
    grad_rows = lax.all_to_all(near, "seq", 0, 0, axis_index_groups=same_side, tiled=True)

    head_out, own_rows, given_rows = call(
        functools.partial(attend_kernel, grp_size=grp_size, block=block),
        [(groups, head), (rows, head), (groups // 2 + rows // 2, head)], place, merged,
        embed_weight, norm_gain[None], q_weight, kv_weight, q_gain[None], k_gain[None], name="attend",
        flops=8 * 10**9, places=["smem"],
        scratch=[pltpu.VMEM((groups, width), BF16)] + [pltpu.VMEM((groups, head), BF16)] * 3,
    )

    side_rows = xor_swap(given_rows, "seq", 1)
    local_grad = call(
        grad_kernel, [(2, head, columns)], place, head_out, side_rows, grad_rows,
        name="local_grad", places=["smem"],
        scratch=[pltpu.VMEM((groups // 2, 2 * head), BF16)], flops=10**9,
    )
    both_sides = [
        [(2 * z + y) * dp_size + d for y in range(2) for d in range(dp_size)]
        for z in range(slabs)
    ]
    grad_parts = lax.all_to_all(
        local_grad.reshape(2 * dp_size, head // dp_size, columns), ("seq", "dp"), 0, 0,
        axis_index_groups=both_sides, tiled=True,
    )
    partial = call(
        functools.partial(project_kernel, part=shared), [(rows, width // 2)], place, own_rows,
        side_rows, out_weight, weight_other, name="project", flops=10**9, places=["smem"],
        scratch=[pltpu.VMEM((rows, 2 * head), BF16)],
    )
    grad_block = call(
        spread_kernel, [(dp_size, head // dp_size, columns)], grad_parts, name="grad_block"
    )
    grad_block, partial = lax.optimization_barrier((grad_block, partial))
    grad_cols = lax.all_to_all(grad_block, "dp", 0, 0, tiled=True).reshape(head, columns)
    partial, grad_cols = lax.optimization_barrier((partial, grad_cols))
    out_parts = lax.all_to_all(
        partial.reshape(seq_size, block, width // 2), "seq", 0, 0, tiled=True
    )
    gathered = [grad_cols] + [xor_swap(grad_cols, "grp", k) for k in range(1, grp_size)]
    out_grad = call(
        columns_kernel, [(head, width)], place, *gathered, name="grad_columns", places=["smem"]
    )
    attended = call(attended_kernel, [(block, width)], out_parts, name="attended")
    return (attended[None], out_grad)


def solution(mesh):
    placed = (
        P("dp", "seq", "grp", None), P(), P(), P("dp", "seq", "grp"), P(), P(),
        P(None, None, "seq"), P(), P(), P("seq", None), P("dp", ("grp", "seq"), None),
    )
    return jax.shard_map(
        shards,
        mesh=mesh,
        in_specs=placed,
        out_specs=(P("dp", ("grp", "seq"), None), P("seq", None)),
        check_vma=False,
    )
```

```python
import functools
import math

import jax
import jax.numpy as jnp
from jax import lax
from jax.experimental import pallas as pl
from jax.experimental.pallas import tpu as pltpu
from jax.sharding import PartitionSpec as P

F32 = jnp.float32
BF16 = jnp.bfloat16
LANES = 128
HALF = 64
NT = (((1,), (1,)), ((), ()))
TN = (((0,), (0,)), ((), ()))


def shifted_frames(block, axis, distance):
    devices = range(lax.axis_size(axis))
    route = [(i - distance, i) for i in devices if i - distance in devices]
    return lax.ppermute(block, axis, route)


def xor_swap(block, axis, mask):
    route = [(i, i ^ mask) for i in range(lax.axis_size(axis))]
    return lax.ppermute(block, axis, route)


def lane_index(rows):
    return lax.broadcasted_iota(jnp.int32, (rows, LANES), 1)


def split_pairs(sums):
    lane = lane_index(sums.shape[0])
    high = sums.astype(BF16).astype(F32)
    keep = jnp.logical_or(lane < HALF, lane == LANES - 2)
    return jnp.where(keep, high, sums - high).astype(BF16)


def join_pairs(pairs):
    lane = lane_index(pairs.shape[0])
    total = pairs + jnp.where(lane < HALF - 2, pltpu.roll(pairs, HALF, 1), 0.0)
    counts = pairs[:, LANES - 2 : LANES - 1] + pairs[:, LANES - 1 :]
    return total, counts


def latent_rows(windows, conv_ref, latent_ref):
    channels = conv_ref.shape[1]
    taps = conv_ref[...].reshape(3 * channels, channels)
    weights = jnp.concatenate([latent_ref[...], latent_ref[...]], axis=0)
    latent = None
    for part, views in enumerate(windows):
        cols = slice(part * channels, (part + 1) * channels)
        preact = jnp.dot(jnp.concatenate(views, axis=1), taps, preferred_element_type=F32)
        hidden = (views[0].astype(F32) + preact / (1.0 + jnp.exp(-preact))).astype(BF16)
        term = lax.dot_general(hidden, weights[:, cols], NT, preferred_element_type=F32)
        latent = term if latent is None else latent + term
    return jnp.where(lane_index(latent.shape[0]) < LANES - 2, latent, 1.0).astype(BF16)


def late_kernel(
    video_hbm, conv_hbm, latent_hbm, out_ref, first_ref, conv_ref, latent_ref, video_ref, sems,
):
    copies = [
        pltpu.make_async_copy(src, dst, sems.at[i])
        for i, (src, dst) in enumerate([
            (video_hbm, video_ref), (conv_hbm, conv_ref), (latent_hbm, latent_ref),
            (video_hbm.at[: first_ref.shape[0]], first_ref),
        ])
    ]
    for copy in copies:
        copy.start()
    for copy in copies:
        copy.wait()
    frame_count, tokens, width = video_ref.shape
    channels = conv_ref.shape[1]
    windows = []
    for start in range(0, width, channels):
        cols = slice(start, start + channels)
        windows.append([
            video_ref[2 - k : frame_count - k, :, cols].reshape(-1, channels) for k in range(3)
        ])
    out_ref[...] = latent_rows(windows, conv_ref, latent_ref)


def sums_kernel(
    video_ref, earlier_ref, conv_ref, latent_ref, late_ref, labels_ref, out_ref, *, grp, seq,
):
    channels = conv_ref.shape[1]
    width = video_ref.shape[2]
    windows = []
    for start in range(0, width, channels):
        cols = slice(start, start + channels)
        padded = jnp.concatenate([earlier_ref[:, :, cols], video_ref[:, :, cols]], axis=0)
        windows.append([padded[2 - k : 4 - k].reshape(-1, channels) for k in range(3)])
    first = latent_rows(windows, conv_ref, latent_ref)
    rows = jnp.concatenate([first, late_ref[...]], axis=0)
    labels = jnp.concatenate(
        [labels_ref[i : i + 1, :] for i in range(labels_ref.shape[0])], axis=1
    )
    total = out_ref.shape[0]
    block = total // (grp * seq)
    step = 256
    for start in range(0, total, step):
        place = lax.broadcasted_iota(jnp.int32, (step, labels.shape[1]), 0) + start
        inner = place & (block - 1)
        column = (place >> (block.bit_length() - 1)) & (grp - 1)
        slab = place >> ((block * grp).bit_length() - 1)
        member = (labels == (column * seq + slab) * block + inner).astype(F32).astype(BF16)
        out_ref[start : start + step, :] = split_pairs(
            jnp.dot(member, rows, preferred_element_type=F32)
        )


def add_up(parts_ref):
    total = parts_ref[0].astype(F32)
    for i in range(1, parts_ref.shape[0]):
        total = total + parts_ref[i].astype(F32)
    return total


def resplit_kernel(parts_ref, cot_ref, out_ref):
    total, counts = join_pairs(add_up(parts_ref))
    lane = lane_index(total.shape[0])
    doubled = jnp.where(lane < HALF, total, pltpu.roll(total, HALF, 1))
    pairs = split_pairs(jnp.where(lane < LANES - 2, doubled, counts))
    for i in range(out_ref.shape[0]):
        out_ref[i, : pairs.shape[0], :] = pairs
    block, width = cot_ref.shape
    pieces = width // LANES // out_ref.shape[0]
    for i in range(width // LANES):
        start = pairs.shape[0] + i % pieces * block
        here = cot_ref[:, i * LANES : (i + 1) * LANES]
        out_ref[i // pieces, start : start + block, :] = here


def merge_kernel(parts_ref, out_ref):
    total, counts = join_pairs(add_up(parts_ref)[: out_ref.shape[1], :])
    lane = lane_index(total.shape[0])
    merged = jnp.where(lane < HALF, total / counts, 0.0)
    high = counts.astype(BF16).astype(F32)
    marks = jnp.where(lane == LANES - 2, high, counts - high)
    rows = jnp.where(lane < LANES - 2, merged, marks).astype(BF16)
    for i in range(out_ref.shape[0]):
        out_ref[i] = rows


def spread_kernel(parts_ref, out_ref):
    total = add_up(parts_ref).astype(BF16)
    for i in range(out_ref.shape[0]):
        out_ref[i] = total


def near_kernel(parts_ref, out_ref):
    rows, columns = out_ref.shape[1:]
    block = rows // parts_ref.shape[0]
    first = parts_ref.shape[1] - columns // LANES * block
    for g in range(parts_ref.shape[0]):
        for b in range(columns // LANES):
            start = first + b * block
            piece = parts_ref[g, start : start + block, :]
            for i in range(out_ref.shape[0]):
                cols = slice(b * LANES, (b + 1) * LANES)
                out_ref[i, g * block : (g + 1) * block, cols] = piece


def grad_kernel(place_ref, head_ref, given_ref, cot_ref, out_ref, rows_ref):
    side = place_ref[1] & 1
    head = head_ref.shape[1]
    slabs, part = cot_ref.shape[:2]
    for slab in range(slabs):
        start = pl.multiple_of((2 * slab + side) * part, part)
        here = slice(slab * part, (slab + 1) * part)
        rows_ref[here, :head] = head_ref[pl.ds(start, part), :]
        rows_ref[here, head:] = given_ref[here, :]
    cot = cot_ref[...].reshape(slabs * part, cot_ref.shape[2])
    total = lax.dot_general(rows_ref[...], cot, TN, preferred_element_type=F32).astype(BF16)
    out_ref[side] = total[:head, :]
    out_ref[1 - side] = total[head:, :]


def project_kernel(
    place_ref, own_ref, given_ref, weight_ref, partner_ref, out_ref, heads_ref, *, part,
):
    grp = place_ref[0]
    side = place_ref[1] & 1
    rows, head = own_ref.shape
    slabs = (given_ref.shape[0] - rows // 2) // part
    block = rows // (2 * slabs)
    heads_ref[:, :head] = own_ref[...]
    for i in range(slabs):
        near = pl.multiple_of((2 * i + side) * block, block)
        far = pl.multiple_of((2 * i + 1 - side) * block, block)
        start = pl.multiple_of(i * part + grp * block, block)
        heads_ref[pl.ds(near, block), head:] = given_ref[pl.ds(start, block), :]
        first = slabs * part + i * block
        heads_ref[pl.ds(far, block), head:] = given_ref[first : first + block, :]
    step = 768
    for start in range(0, out_ref.shape[1], step):
        here = slice(start, start + step)
        kept = pl.multiple_of(side * out_ref.shape[1] + start, step)
        weights = jnp.concatenate([weight_ref[:, pl.ds(kept, step)], partner_ref[:, here]], axis=0)
        out_ref[:, here] = jnp.dot(
            heads_ref[...], weights, preferred_element_type=F32
        ).astype(BF16)


def attended_kernel(parts_ref, out_ref):
    columns = parts_ref.shape[2]
    for side in range(2):
        total = parts_ref[side].astype(F32)
        for i in range(side + 2, parts_ref.shape[0], 2):
            total = total + parts_ref[i].astype(F32)
        out_ref[:, side * columns : (side + 1) * columns] = total.astype(BF16)


def columns_kernel(place_ref, *refs):
    out_ref = refs[-1]
    columns = refs[0].shape[1]
    for k, ref in enumerate(refs[:-1]):
        start = pl.multiple_of((place_ref[0] ^ k) * columns, columns)
        out_ref[:, pl.ds(start, columns)] = ref[...]


def head_norm(projected, gain):
    square_mean = jnp.mean(projected * projected, axis=-1, keepdims=True)
    return (projected * lax.rsqrt(square_mean + 1e-06) * gain).astype(BF16)


def attend_kernel(
    place_ref, merged_ref, embed_ref, norm_ref, qkv_ref, qgain_ref, kgain_ref, out_ref, own_ref,
    give_ref, normed_ref, kv_ref, q_ref, k_ref, v_ref, *, grp_size, block,
):
    latents, width = embed_ref.shape
    head = q_ref.shape[1]
    total = out_ref.shape[0]
    step = 512
    kv_ref[:, :head] = qkv_ref[1]
    kv_ref[:, head:] = qkv_ref[2]
    pick = (lane_index(16) >= LANES - 2).astype(F32).astype(BF16)
    count_row = lax.dot_general(pick, merged_ref[...], NT, preferred_element_type=F32)[0:1, :]
    bias = jnp.log(count_row)
    ones = jnp.ones((16, width), BF16)
    embed_mean = lax.dot_general(ones, embed_ref[...], NT, preferred_element_type=F32)
    embed_mean = embed_mean[0:1, :] * (1.0 / width)
    embed = jnp.concatenate([embed_ref[...], jnp.ones((LANES - latents, width), BF16)], axis=0)
    lane = lane_index(step)
    for start in range(0, total, step):
        here = slice(start, start + step)
        rows = merged_ref[here, :].astype(F32)
        mean = -jnp.sum(rows[:, :latents] * embed_mean, axis=-1, keepdims=True)
        high = mean.astype(BF16).astype(F32)
        middle = (mean - high).astype(BF16).astype(F32)
        low = mean - high - middle
        tail = jnp.where(lane == latents, high, 0.0)
        tail = jnp.where(lane == latents + 1, middle, tail)
        tail = jnp.where(lane == latents + 2, low, tail)
        factors = jnp.where(lane < latents, rows, tail).astype(BF16)
        center = jnp.dot(factors, embed, preferred_element_type=F32)
        spread = jnp.mean(center * center, axis=-1, keepdims=True)
        scaled = center * lax.rsqrt(spread + 1e-06) * norm_ref[...]
        normed_ref[here, :] = scaled.astype(BF16)
    q_part = jnp.dot(normed_ref[...], qkv_ref[0], preferred_element_type=F32)
    q_ref[...] = head_norm(q_part, qgain_ref[...])
    kv_part = jnp.dot(normed_ref[...], kv_ref[...], preferred_element_type=F32)
    k_ref[...] = head_norm(kv_part[:, :head], kgain_ref[...])
    v_ref[...] = kv_part[:, head:].astype(BF16)
    scale = 1.0 / math.sqrt(head)
    for start in range(0, total, step):
        here = slice(start, start + step)
        scores = lax.dot_general(
            q_ref[here, :], k_ref[...], NT, preferred_element_type=F32
        ) * scale + bias
        top = jnp.max(scores, axis=-1, keepdims=True)
        weights = jnp.exp(scores - top)
        denominator = jnp.sum(weights, axis=-1, keepdims=True)
        mixed = jnp.dot(weights.astype(BF16), v_ref[...], preferred_element_type=F32)
        out_ref[here, :] = (mixed / denominator).astype(BF16)
    grp = place_ref[0]
    side = place_ref[1] & 1
    part = block * grp_size
    slabs = total // (2 * part)
    for i in range(2 * slabs):
        start = pl.multiple_of(i * part + grp * block, block)
        own_ref[i * block : (i + 1) * block, :] = out_ref[pl.ds(start, block), :]
    for i in range(slabs):
        start = pl.multiple_of((2 * i + 1 - side) * part, part)
        give_ref[i * part : (i + 1) * part, :] = out_ref[pl.ds(start, part), :]
        start = pl.multiple_of((2 * i + side) * part + grp * block, block)
        first = slabs * part + i * block
        give_ref[first : first + block, :] = out_ref[pl.ds(start, block), :]


def call(body, shapes, *args, name, scratch=(), places=(), flops=10**8, moved=10**6):
    spaces = {"smem": pltpu.SMEM, "hbm": pltpu.HBM}
    outs = tuple(jax.ShapeDtypeStruct(shape, BF16) for shape in shapes)
    whole = pl.BlockSpec(memory_space=pltpu.VMEM)
    in_specs = [whole] * len(args)
    for i, place in enumerate(places):
        in_specs[i] = pl.BlockSpec(memory_space=spaces[place])
    result = pl.pallas_call(
        body,
        out_shape=outs,
        in_specs=in_specs,
        out_specs=(whole,) * len(outs),
        scratch_shapes=list(scratch),
        cost_estimate=pl.CostEstimate(flops=flops, bytes_accessed=moved, transcendentals=0),
        compiler_params=pltpu.CompilerParams(vmem_limit_bytes=48 * 2**20),
        name=name,
    )(*args)
    return result[0] if len(outs) == 1 else result


def shards(
    video, conv_weight, latent_weight, assign, embed_weight, norm_gain, qkv_weight, q_gain, k_gain,
    out_weight, cotangent,
):
    grp_size, seq_size, dp_size = (lax.axis_size(a) for a in ("grp", "seq", "dp"))
    owners = grp_size * seq_size
    block, width = cotangent.shape[1:]
    head = q_gain.shape[0]
    groups = block * owners
    columns = width // grp_size
    shared = block * grp_size
    rows = block * seq_size
    grp = lax.axis_index("grp")
    seq = lax.axis_index("seq")
    place = jnp.stack([grp, seq, lax.axis_index("dp") & 1]).astype(jnp.int32)

    frames = video[0]
    frame_count, tokens = frames.shape[:2]
    earlier = shifted_frames(frames[frame_count - 2 :], "seq", 1)
    latent_t = latent_weight.T
    late, first, taps, latent_rhs = call(
        late_kernel,
        [((frame_count - 2) * tokens, LANES), (2,) + frames.shape[1:], conv_weight.shape,
         latent_t.shape],
        frames, conv_weight, latent_t, name="late_frames", flops=10**9, places=["hbm"] * 3,
        scratch=[pltpu.VMEM(frames.shape, BF16), pltpu.SemaphoreType.DMA((4,))],
    )
    sums = call(
        functools.partial(sums_kernel, grp=grp_size, seq=seq_size), [(groups, LANES)],
        first, earlier, taps, latent_rhs, late, assign[0], name="group_sums", flops=10**9,
    )

    parts = lax.all_to_all(sums.reshape(seq_size, shared, LANES), "seq", 0, 0, tiled=True)
    carried = shared + columns // LANES * block
    slab_sums = call(
        resplit_kernel, [(grp_size, carried, LANES)], parts, cotangent[0], name="slab_sums"
    )
    slab_parts = lax.all_to_all(slab_sums, "grp", 0, 0, tiled=True)
    merged = call(merge_kernel, [(seq_size, shared, LANES)], slab_parts, name="merged")
    merged, weight = lax.optimization_barrier((merged, out_weight))
    given = lax.dynamic_slice_in_dim(weight, (1 - (seq & 1)) * (width // 2), width // 2, 1)
    weight_other = xor_swap(given, "seq", 1)
    merged = lax.all_to_all(merged, "seq", 0, 0, tiled=True).reshape(groups, LANES)
    slabs = seq_size // 2
    near = call(near_kernel, [(slabs, shared, columns)], slab_parts, name="near_rows")
    near, merged = lax.optimization_barrier((near, merged))
    same_side = [list(range(k, seq_size, 2)) for k in range(2)]
    grad_rows = lax.all_to_all(near, "seq", 0, 0, axis_index_groups=same_side, tiled=True)

    head_out, own_rows, given_rows = call(
        functools.partial(attend_kernel, grp_size=grp_size, block=block),
        [(groups, head), (rows, head), (groups // 2 + rows // 2, head)], place, merged,
        embed_weight, norm_gain[None], qkv_weight, q_gain[None], k_gain[None], name="attend",
        flops=8 * 10**9, places=["smem"],
        scratch=[pltpu.VMEM((groups, width), BF16), pltpu.VMEM((width, 2 * head), BF16)]
        + [pltpu.VMEM((groups, head), BF16)] * 3,
    )

    given_rows, weight_other = lax.optimization_barrier((given_rows, weight_other))
    side_rows = xor_swap(given_rows, "seq", 1)
    local_grad = call(
        grad_kernel, [(2, head, columns)], place, head_out, side_rows, grad_rows,
        name="local_grad", places=["smem"],
        scratch=[pltpu.VMEM((groups // 2, 2 * head), BF16)], flops=10**9,
    )
    both_sides = [
        [(2 * z + y) * dp_size + d for y in range(2) for d in range(dp_size)]
        for z in range(slabs)
    ]
    grad_parts = lax.all_to_all(
        local_grad.reshape(2 * dp_size, head // dp_size, columns), ("seq", "dp"), 0, 0,
        axis_index_groups=both_sides, tiled=True,
    )
    partial = call(
        functools.partial(project_kernel, part=shared), [(rows, width // 2)], place, own_rows,
        side_rows, out_weight, weight_other, name="project", flops=10**9, places=["smem"],
        scratch=[pltpu.VMEM((rows, 2 * head), BF16)],
    )
    grad_block = call(
        spread_kernel, [(dp_size, head // dp_size, columns)], grad_parts, name="grad_block"
    )
    grad_block, partial = lax.optimization_barrier((grad_block, partial))
    grad_cols = lax.all_to_all(grad_block, "dp", 0, 0, tiled=True).reshape(head, columns)
    partial, grad_cols = lax.optimization_barrier((partial, grad_cols))
    out_parts = lax.all_to_all(
        partial.reshape(seq_size, block, width // 2), "seq", 0, 0, tiled=True
    )
    gathered = [grad_cols] + [xor_swap(grad_cols, "grp", k) for k in range(1, grp_size)]
    out_grad = call(
        columns_kernel, [(head, width)], place, *gathered, name="grad_columns", places=["smem"]
    )
    attended = call(attended_kernel, [(block, width)], out_parts, name="attended")
    return (attended[None], out_grad)


def solution(mesh):
    placed = (
        P("dp", "seq", "grp", None), P(), P(), P("dp", "seq", "grp"), P(), P(),
        P(None, None, "seq"), P(), P(), P("seq", None), P("dp", ("grp", "seq"), None),
    )
    return jax.shard_map(
        shards,
        mesh=mesh,
        in_specs=placed,
        out_specs=(P("dp", ("grp", "seq"), None), P("seq", None)),
        check_vma=False,
    )
```
